256 devices in a mesh: gx: 4 (over y), gy: 16 (over z, x_lo), gz: 4 (over x_hi, core).
Axes of the slice: x: 4 (x_hi: 2, x_lo: 2; x = x_hi * 2 + x_lo), y: 4, z: 8, core: 2. Of those that a mesh axis runs over, the one named last changes fastest.
Arguments:
- source_field: float32 [16, 3, 2, 16, 64, 512], P(None, None, None, 'gx', 'gy', 'gz'), may hold values from -15 to 15
- receiver_tensor: bfloat16 [12, 16, 6, 2, 16, 64, 512], P(None, None, None, None, 'gx', 'gy', 'gz'), may hold values from -6 to 6
- metric_ids: int32 [16, 64, 512], P('gx', 'gy', 'gz'), may hold values from 0 to 7
- metric_table: float32 [8, 3], replicated, may hold values from 0.5 to 2
- observed: float32 [2, 384, 16], P(None, 'gz'), may hold values from -6 to 6
- receiver_index: int32 [384], P('gz'), may hold values from 0 to 11
- bin_ids: int32 [384, 16], P('gz'), may hold values from 0 to 15
- window: int32 [384, 16], P('gz'), may hold values 0 or 1
Outputs:
- model_update: float32 [16, 64, 512], P('gx', 'gy', 'gz')
- direction_field: float32 [16, 64, 512], P('gx', 'gy', 'gz')
- data_vector: float32 [2, 384, 16], P(None, 'gz')
The draws below stay inside these ranges and needn't reach their ends.
All inputs are finite; a program needn't handle non-finite values. No bound on the sum of `window` on one device may be relied on, other than what follows from the above.
Results may differ from the reference program's by a relative error of at most 0.0003.
Values sent between devices are 32-bit elements; how exact they have to be, the bound alone decides.
No kernel may reach another device: no remote copies, remote signals or barrier semaphores. Data moves between devices by JAX's collectives and lax.ppermute only.
A program may use at most 64 MiB of HBM per device.

```python
import math
import jax
import jax.numpy as jnp
from jax import lax

NBIN = 16
NF = 16
M = 384
NSGT = 12
NMET = 8
ITERS = 2
NX = 16
NY = 64
NZ = 512


def draw_source_field(key, part):
    key = jax.random.fold_in(key, 11)
    shape = (NBIN, 3, 2, NX, NY, NZ)
    pos_x = jnp.arange(NX, dtype=jnp.float32) / NX
    pos_y = jnp.arange(NY, dtype=jnp.float32) / NY
    pos_z = jnp.arange(NZ, dtype=jnp.float32) / NZ
    position = (pos_x[:, None, None] + pos_y[None, :, None] + pos_z[None, None, :]) / 3.0
    amplitude = jnp.exp(math.log(3.0) * position)
    values = jnp.clip(jax.random.normal(key, shape, jnp.float32), -5.0, 5.0) * amplitude
    return values.astype(jnp.float32)


def set_ends(entries, key, least, top_value):
    shape = entries.shape
    place = [jax.random.randint(jax.random.fold_in(key, axis), (), 0, shape[axis]) for axis in range(len(shape))]
    entries = entries.at[tuple(place)].set(least)
    longest = shape.index(max(shape))
    place[longest] = (place[longest] + 1) % shape[longest]
    return entries.at[tuple(place)].set(top_value)


def shard_levels(rng, dims, shards, least, high):
    gain = 1.0
    for axis_at, shards_of in shards:
        steps = jax.random.uniform(jax.random.fold_in(jax.random.fold_in(rng, 6), axis_at), (shards_of,), jnp.float32, least / len(shards), high / len(shards))
        gain = gain * jnp.repeat(jnp.exp(steps), dims[axis_at] // shards_of).reshape((-1,) + (1,) * (len(dims) - 1 - axis_at))
    return gain


def scatter_about(rng, dims, scale, reach, cuts=(), held_as=jnp.bfloat16):
    values = scale * jax.random.normal(rng, dims, jnp.float32)
    if cuts:
        values = values * shard_levels(rng, dims, cuts, -0.22, 0.18)
    return jnp.clip(values, -reach, reach).astype(held_as)


def setup_inputs(seed: int = 0) -> dict:
    key_of = jax.random.split(jax.random.key(seed), 9)
    return {
        "source_field": draw_source_field(jax.random.fold_in(key_of[8], 71), 0),
        "receiver_tensor": scatter_about(key_of[1], (NSGT, NBIN, 6, 2, NX, NY, NZ), 1.0, 6.0, ((4, 4), (5, 16), (6, 4))),
        "metric_ids": set_ends(jax.random.randint(key_of[2], (NX, NY, NZ), 0, NMET), jax.random.fold_in(key_of[2], 1), 0, NMET - 1).astype(jnp.int32),
        "metric_table": jnp.clip(jnp.exp(jax.random.uniform(key_of[3], (NMET, 3), jnp.float32, math.log(0.5), math.log(2.0))), 0.5, 2.0),
        "observed": scatter_about(key_of[4], (2, M, NF), 1.0, 6.0, ((1, 4),), jnp.float32),
        "receiver_index": set_ends(jax.random.randint(key_of[5], (M,), 0, NSGT), jax.random.fold_in(key_of[5], 1), 0, NSGT - 1).astype(jnp.int32),
        "bin_ids": set_ends(jax.random.randint(key_of[6], (M, NF), 0, NBIN), jax.random.fold_in(key_of[6], 1), 0, NBIN - 1).astype(jnp.int32),
        "window": set_ends((jax.random.randint(key_of[7], (M, NF), 0, 4) < 3).astype(jnp.int32), jax.random.fold_in(key_of[7], 1), 0, 1),
    }


epsilon = 1e-06

def derivative(padded, axis_dim):
    length = padded.shape[axis_dim] - 4

    def shifted(start):
        return lax.slice_in_dim(padded, start, start + length, axis=axis_dim)
    return (8.0 * (shifted(3) - shifted(1)) - (shifted(4) - shifted(0))) / 12.0

def pad_axis(field, axis_dim):
    widths = [(0, 0)] * field.ndim
    widths[axis_dim] = (2, 2)
    return jnp.pad(field, widths)

def metric_scales(metric_ids, metric_table):
    levels = jnp.arange(metric_table.shape[0], dtype=jnp.int32)
    onehot = (metric_ids[None] == levels[:, None, None, None]).astype(jnp.float32)
    return jnp.einsum('mxyz,mp->pxyz', onehot, metric_table, precision=lax.Precision.HIGHEST)

def strain_from(along_x, along_y, along_z, scales):
    grads = [scales[0] * along_x, scales[1] * along_y, scales[2] * along_z]
    comps = [grads[0][:, 0], grads[1][:, 1], grads[2][:, 2], 0.5 * (grads[1][:, 2] + grads[2][:, 1]), 0.5 * (grads[0][:, 2] + grads[2][:, 0]), 0.5 * (grads[0][:, 1] + grads[1][:, 0])]
    return jnp.stack(comps, axis=1)

def kernel_of(receiver, strain):
    weights = jnp.array([1.0, 1.0, 1.0, 2.0, 2.0, 2.0], jnp.float32)[:, None, None, None]
    rec_re = jnp.take(receiver, 0, axis=-4).astype(jnp.float32)
    rec_im = jnp.take(receiver, 1, axis=-4).astype(jnp.float32)
    src_re = jnp.take(strain, 0, axis=-4)
    src_im = jnp.take(strain, 1, axis=-4)
    real_part = lax.optimization_barrier(jnp.sum(weights * (rec_re * src_re - rec_im * src_im), axis=-4))
    imag_part = lax.optimization_barrier(jnp.sum(weights * (rec_re * src_im + rec_im * src_re), axis=-4))
    return jnp.stack([real_part, imag_part], axis=-4)

def select_data(synth, onerec, onebin, window_mask):
    picked = jnp.einsum('ir,rbk->kib', onerec, synth, precision=lax.Precision.HIGHEST)
    return jnp.einsum('kib,ifb->kif', picked, onebin, precision=lax.Precision.HIGHEST) * window_mask

def spread_data(data, onerec, onebin, window_mask):
    summed = jnp.einsum('kif,ifb->kib', data * window_mask, onebin, precision=lax.Precision.HIGHEST)
    return jnp.einsum('kib,ir->rbk', summed, onerec, precision=lax.Precision.HIGHEST)

def norm_of(total):
    return jnp.sqrt(total + epsilon)

def reference(source_field, receiver_tensor, metric_ids, metric_table, observed, receiver_index, bin_ids, window):
    along_x = derivative(pad_axis(source_field, 3), 3)
    along_y = derivative(pad_axis(source_field, 4), 4)
    along_z = derivative(pad_axis(source_field, 5), 5)
    strain = strain_from(along_x, along_y, along_z, metric_scales(metric_ids, metric_table))
    kernel = lax.map(lambda one: kernel_of(one, strain), receiver_tensor)
    onerec = (receiver_index[:, None] == jnp.arange(NSGT, dtype=jnp.int32)[None]).astype(jnp.float32)
    onebin = (bin_ids[:, :, None] == jnp.arange(NBIN, dtype=jnp.int32)[None, None]).astype(jnp.float32)
    window_mask = window.astype(jnp.float32)

    def forward(model_vec):
        synth = jnp.einsum('rbkxyz,xyz->rbk', kernel, model_vec, precision=lax.Precision.HIGHEST)
        return select_data(synth, onerec, onebin, window_mask)

    def adjoint(data_vec):
        spread = spread_data(data_vec, onerec, onebin, window_mask)
        return jnp.einsum('rbk,rbkxyz->xyz', spread, kernel, precision=lax.Precision.HIGHEST)
    rhs = observed * window_mask
    beta_val = norm_of(jnp.sum(rhs * rhs))
    data_vec = rhs / beta_val
    beta_first = beta_val
    model_raw = adjoint(data_vec)
    alpha_val = norm_of(jnp.sum(model_raw * model_raw))
    model_vec = model_raw / alpha_val
    alpha_first = alpha_val
    search = model_vec
    solution = jnp.zeros_like(model_vec)
    phi_bar = beta_val
    rho_bar = alpha_val
    for iteration in range(ITERS):
        data_raw = forward(model_vec) - alpha_val * data_vec
        beta_val = norm_of(jnp.sum(data_raw * data_raw))
        data_vec = data_raw / beta_val
        model_raw = adjoint(data_vec) - beta_val * model_vec
        alpha_val = norm_of(jnp.sum(model_raw * model_raw))
        model_vec = model_raw / alpha_val
        rho_new = jnp.sqrt(rho_bar * rho_bar + beta_val * beta_val)
        cosine = rho_bar / rho_new
        sine_val = beta_val / rho_new
        theta_val = sine_val * alpha_val
        rho_bar = -cosine * alpha_val
        phi_val = cosine * phi_bar
        phi_bar = sine_val * phi_bar
        solution = solution + phi_val / rho_new * search
        search = model_vec - theta_val / rho_new * search
    cell_scale = math.sqrt(NX * NY * NZ)
    model_update = solution * alpha_first * cell_scale / beta_first
    direction_field = model_vec * cell_scale
    data_vector = data_vec * math.sqrt(2 * M * NF)
    return (model_update, direction_field, data_vector)
```

```python
import functools
import math

import jax
import jax.numpy as jnp
from jax import lax
from jax.experimental import pallas as pl
from jax.experimental.pallas import tpu as pltpu
from jax.sharding import Mesh, PartitionSpec as P

ITERS = 2
EPSILON = 1e-06
F32 = jnp.float32
BF16 = jnp.bfloat16

AXES = ("y", "z", "xlo", "xhi", "core")
SIZES = {"y": 4, "z": 8, "xlo": 2, "xhi": 2, "core": 2}
GX = ("y",)
GY = ("z", "xlo")
GZ = ("xhi", "core")
PLANE = ("y", "xlo", "xhi")
VMEM_LIMIT = 40 * 1024 * 1024

BINS = 16
TENSORS = 12
FIELDS = 96
PLANES = 16
LANES = 128
ROWS = 384
BLOCKS = ((0, 0), (0, 1), (0, 2), (1, 1), (1, 2), (2, 2))


def vmem():
    return pl.BlockSpec(memory_space=pltpu.VMEM)


def smem():
    return pl.BlockSpec(memory_space=pltpu.SMEM)


def lane_ids(shape):
    return lax.broadcasted_iota(jnp.int32, shape, len(shape) - 1)


def pack_kernel(src, x_lo, x_hi, y_lo, y_hi, z_lo, z_hi):
    x_lo[...] = src[:, 0:8, :]
    x_hi[...] = src[:, 8:16, :]
    lane = lane_ids((FIELDS, LANES))
    low = jnp.zeros((FIELDS, LANES), F32)
    high = jnp.zeros((FIELDS, LANES), F32)
    for plane in range(PLANES):
        value = src[:, plane, :]
        x, y = divmod(plane, 4)
        if y < 2:
            y_lo[x * 2 + y] = value
        else:
            y_hi[x * 2 + y - 2] = value
        turned = pltpu.roll(value, 8 * plane, 1) if plane else value
        place = (lane - 8 * plane) & (LANES - 1)
        low = jnp.where(place < 2, turned, low)
        high = jnp.where(place >= LANES - 2, turned, high)
    z_lo[...] = low
    z_hi[...] = high


def pack(src):
    face = jax.ShapeDtypeStruct((FIELDS, 8, LANES), F32)
    side = jax.ShapeDtypeStruct((8, FIELDS, LANES), F32)
    ends = jax.ShapeDtypeStruct((FIELDS, LANES), F32)
    return pl.pallas_call(
        pack_kernel,
        out_shape=(face, face, side, side, ends, ends),
        in_specs=[vmem()],
        out_specs=(vmem(),) * 6,
        compiler_params=pltpu.CompilerParams(vmem_limit_bytes=VMEM_LIMIT),
        name="pack",
    )(src)


def spread(values, bins, tensor):
    parts = []
    for b in range(BINS):
        here = bins == b
        for k in range(2):
            parts.append(jnp.sum(jnp.where(here, values[k], 0.0), axis=0, keepdims=True))
    table = jnp.concatenate(parts, axis=0)
    return jnp.concatenate(
        [
            jnp.sum(jnp.where(tensor == r, table, 0.0), axis=1, keepdims=True)
            for r in range(TENSORS)
        ],
        axis=0,
    )


def pick(column, bins, tensor):
    table = jnp.zeros((2 * BINS, bins.shape[1]), F32)
    for r in range(TENSORS):
        table = jnp.where(tensor == r, column[r * 32 : (r + 1) * 32, :], table)
    out = [jnp.zeros(bins.shape, F32), jnp.zeros(bins.shape, F32)]
    for b in range(BINS):
        here = bins == b
        for k in range(2):
            out[k] = jnp.where(here, table[2 * b + k : 2 * b + k + 1, :], out[k])
    return out


def data_kernel(observed, tensor_ref, bins_ref, window, stats):
    tensor, bins = tensor_ref[...], bins_ref[...]
    mask = window[...].astype(F32)
    rhs = [observed[k] * mask for k in range(2)]
    total = spread(rhs, bins, tensor)
    count = spread([mask, mask], bins, tensor)
    mean = total / jnp.maximum(count, 1.0)
    near = pick(mean, bins, tensor)
    rest = [rhs[k] - near[k] * mask for k in range(2)]
    square = jnp.sum(rest[0] * rest[0] + rest[1] * rest[1], axis=(0, 1), keepdims=True)
    lane = lane_ids((ROWS, LANES))
    wide = jnp.where(lane == 0, total, jnp.where(lane == 1, count, square))
    for j in range(3):
        stats[:, j * LANES : (j + 1) * LANES] = wide[j * LANES : (j + 1) * LANES, :].T[:8]


def data_sums(observed, tensor, bins, window):
    return pl.pallas_call(
        data_kernel,
        out_shape=jax.ShapeDtypeStruct((8, ROWS), F32),
        in_specs=[vmem()] * 4,
        out_specs=vmem(),
        compiler_params=pltpu.CompilerParams(vmem_limit_bytes=VMEM_LIMIT),
        name="data_sums",
    )(observed, tensor, bins, window)


def merge_sums(one, two):
    total, count = one[0:1] + two[0:1], one[1:2] + two[1:2]
    gap = one[0:1] / jnp.maximum(one[1:2], 1.0) - two[0:1] / jnp.maximum(two[1:2], 1.0)
    apart = jnp.sum(one[1:2] * two[1:2] / jnp.maximum(count, 1.0) * gap * gap)
    rest = one[2:3] + two[2:3] + apart
    return jnp.concatenate([total, count, rest, jnp.zeros((5, ROWS), F32)], axis=0)


def gram_kernel(
    flags, table, src, ids, xb, xa, yb, ya, zb, za, receiver, out, cells, grads, scales
):
    step = pl.program_id(0)

    @pl.when(step == 0)
    def _():
        marks = ids[...]
        for p in range(3):
            scale = jnp.zeros((PLANES, LANES), F32)
            for m in range(8):
                scale = jnp.where(marks == m, table[m, p], scale)
            scales[p] = scale * (1.0 / 12.0)
        lane = lane_ids((FIELDS, LANES))
        halo = zb[...] * flags[4] + za[...] * flags[5]

        def at(x, y):
            if x < 0:
                return xb[:, (x + 2) * 4 + y, :] * flags[0]
            if x > 3:
                return xa[:, (x - 4) * 4 + y, :] * flags[1]
            if y < 0:
                return yb[x * 2 + y + 2] * flags[2]
            if y > 3:
                return ya[x * 2 + y - 4] * flags[3]
            return src[:, x * 4 + y, :]

        for x in range(4):
            for y in range(4):
                plane = x * 4 + y
                grads[0, :, plane, :] = 8.0 * (at(x + 1, y) - at(x - 1, y)) - (
                    at(x + 2, y) - at(x - 2, y)
                )
                grads[1, :, plane, :] = 8.0 * (at(x, y + 1) - at(x, y - 1)) - (
                    at(x, y + 2) - at(x, y - 2)
                )
                mid = at(x, y)
                ends = pltpu.roll(halo, LANES - 8 * plane, 1) if plane else halo
                later = pltpu.roll(jnp.where(lane < 1, ends, mid), LANES - 1, 1)
                sooner = pltpu.roll(jnp.where(lane >= LANES - 1, ends, mid), 1, 1)
                later_two = pltpu.roll(jnp.where(lane < 2, ends, mid), LANES - 2, 1)
                sooner_two = pltpu.roll(jnp.where(lane >= LANES - 2, ends, mid), 2, 1)
                grads[2, :, plane, :] = 8.0 * (later - sooner) - (later_two - sooner_two)

    def grad(p, q, k):
        return scales[p] * grads[p, step * 6 + q * 2 + k]

    def strain(k):
        return (
            grad(0, 0, k),
            grad(1, 1, k),
            grad(2, 2, k),
            grad(1, 2, k) + grad(2, 1, k),
            grad(0, 2, k) + grad(2, 0, k),
            grad(0, 1, k) + grad(1, 0, k),
        )

    real, imag = strain(0), strain(1)
    for r in range(TENSORS):
        re = jnp.zeros((PLANES, LANES), F32)
        im = jnp.zeros((PLANES, LANES), F32)
        for j in range(6):
            rec_re = receiver[r, 0, 2 * j].astype(F32)
            rec_im = receiver[r, 0, 2 * j + 1].astype(F32)
            re = re + (rec_re * real[j] - rec_im * imag[j])
            im = im + (rec_re * imag[j] + rec_im * real[j])
        cells[r * 32 + step * 2] = re
        cells[r * 32 + step * 2 + 1] = im

    @pl.when(step == BINS - 1)
    def _():
        total = jnp.zeros((ROWS, ROWS), F32)
        for plane in range(0, PLANES, 2):
            both = jnp.concatenate([cells[:, plane, :], cells[:, plane + 1, :]], axis=1)
            high = both.astype(BF16)
            low = (both - high.astype(F32)).astype(BF16)
            left = jnp.concatenate([high, high], axis=1)
            right = jnp.concatenate([high * BF16(0.5), low], axis=1)
            total = total + lax.dot_general(
                left, right, (((1,), (1,)), ((), ())), preferred_element_type=F32
            )

        def block(i, j):
            return total[i * LANES : (i + 1) * LANES, j * LANES : (j + 1) * LANES]

        for n, (i, j) in enumerate(BLOCKS):
            out[n * LANES : (n + 1) * LANES, :] = block(i, j) + block(j, i).T


def gram(flags, table, src, ids, halos, receiver):
    whole = lambda *shape: pl.BlockSpec(shape, lambda b: (0,) * len(shape))
    face = whole(FIELDS, 8, LANES)
    side = whole(8, FIELDS, LANES)
    ends = whole(FIELDS, LANES)
    return pl.pallas_call(
        gram_kernel,
        grid=(BINS,),
        out_shape=(
            jax.ShapeDtypeStruct((768, LANES), F32),
            jax.ShapeDtypeStruct((ROWS, PLANES, LANES), F32),
        ),
        in_specs=[
            smem(),
            smem(),
            whole(FIELDS, PLANES, LANES),
            whole(PLANES, LANES),
            face,
            face,
            side,
            side,
            ends,
            ends,
            pl.BlockSpec((TENSORS, 1, 12, PLANES, LANES), lambda b: (0, b, 0, 0, 0)),
        ],
        out_specs=(whole(768, LANES), whole(ROWS, PLANES, LANES)),
        scratch_shapes=[
            pltpu.VMEM((3, FIELDS, PLANES, LANES), F32),
            pltpu.VMEM((3, PLANES, LANES), F32),
        ],
        compiler_params=pltpu.CompilerParams(vmem_limit_bytes=VMEM_LIMIT),
        name="gram",
    )(flags, table, src, ids, *halos, receiver)


def chain_kernel(
    packed, stats, cells, observed, tensor_ref, bins_ref, window, update, direction, data, full, coef
):
    for n, (i, j) in enumerate(BLOCKS):
        tile = packed[n * LANES : (n + 1) * LANES, :]
        full[i * LANES : (i + 1) * LANES, j * LANES : (j + 1) * LANES] = tile
        if i != j:
            full[j * LANES : (j + 1) * LANES, i * LANES : (i + 1) * LANES] = tile.T
    eye = lax.broadcasted_iota(jnp.int32, (LANES, LANES), 0) == lane_ids((LANES, LANES))

    def column(row):
        return jnp.concatenate(
            [
                jnp.sum(
                    jnp.where(eye, row[:, j * LANES : (j + 1) * LANES], 0.0), axis=1, keepdims=True
                )
                for j in range(3)
            ],
            axis=0,
        )

    def product(row):
        return jnp.sum(full[...] * column(row), axis=0, keepdims=True)

    def total(row):
        return jnp.sum(row, axis=1, keepdims=True)

    def norm_of(square):
        return jnp.sqrt(square + EPSILON)

    sums, count, rest = stats[0:1, :], stats[1:2, :], stats[2:3, 0:1]
    mean = sums / jnp.maximum(count, 1.0)

    def data_norm(scale, row):
        inside = scale * mean + row
        return norm_of(scale * scale * rest + total(count * inside * inside))

    one = jnp.ones((1, 1), F32)
    row = jnp.zeros((1, ROWS), F32)
    beta = data_norm(one, row)
    beta_first = beta
    scale = one / beta
    raw = scale * sums
    image = product(raw)
    alpha = norm_of(total(raw * image))
    alpha_first = alpha
    model = raw / alpha
    search = model
    answer = jnp.zeros((1, ROWS), F32)
    phi_bar, rho_bar = beta, alpha
    for _ in range(ITERS):
        scale, row = -alpha * scale, image / alpha - alpha * row
        beta = data_norm(scale, row)
        scale, row = scale / beta, row / beta
        raw = scale * sums + count * row - beta * model
        image = product(raw)
        alpha = norm_of(total(raw * image))
        model = raw / alpha
        rho = jnp.sqrt(rho_bar * rho_bar + beta * beta)
        cosine, sine = rho_bar / rho, beta / rho
        theta = sine * alpha
        rho_bar = -cosine * alpha
        phi = cosine * phi_bar
        phi_bar = sine * phi_bar
        answer = answer + phi / rho * search
        search = model - theta / rho * search
    cell_scale = math.sqrt(PLANES * LANES * math.prod(SIZES.values()))
    coef[0] = jnp.broadcast_to(
        column(answer * (alpha_first * cell_scale / beta_first)), (ROWS, LANES)
    )
    coef[1] = jnp.broadcast_to(column(model * cell_scale), (ROWS, LANES))

    mask = window[...].astype(F32)
    size = math.sqrt(math.prod(observed.shape) * SIZES["xhi"] * SIZES["core"])
    near = pick(column(row * size), bins_ref[...], tensor_ref[...])
    for k in range(2):
        data[k] = (observed[k] * (scale * size) + near[k]) * mask

    def body(n, sums_of):
        tile = cells[n]
        return (
            sums_of[0] + coef[0, pl.ds(n, 1), :] * tile,
            sums_of[1] + coef[1, pl.ds(n, 1), :] * tile,
        )

    start = (jnp.zeros((PLANES, LANES), F32), jnp.zeros((PLANES, LANES), F32))
    first, second = lax.fori_loop(0, ROWS, body, start, unroll=16)
    update[...] = first
    direction[...] = second


def chain(packed, stats, cells, observed, tensor, bins, window):
    field = jax.ShapeDtypeStruct((PLANES, LANES), F32)
    return pl.pallas_call(
        chain_kernel,
        out_shape=(field, field, jax.ShapeDtypeStruct(observed.shape, F32)),
        in_specs=[vmem()] * 7,
        out_specs=(vmem(),) * 3,
        scratch_shapes=[pltpu.VMEM((ROWS, ROWS), F32), pltpu.VMEM((2, ROWS, LANES), F32)],
        compiler_params=pltpu.CompilerParams(vmem_limit_bytes=VMEM_LIMIT),
        name="chain",
    )(packed, stats, cells, observed, tensor, bins, window)


def shift(value, axes, step):
    count = math.prod(SIZES[a] for a in axes)
    return lax.ppermute(value, axes, [(i, (i + step) % count) for i in range(count)])


def swap(value, axis):
    return lax.ppermute(value, axis, [(0, 1), (1, 0)])


def half_scatter(value, axis):
    half = value.shape[0] // 2
    upper = lax.axis_index(axis) == 1
    low, high = value[:half], value[half:]
    return jnp.where(upper, high, low) + swap(jnp.where(upper, low, high), axis)


def half_gather(value, axis):
    upper = lax.axis_index(axis) == 1
    other = swap(value, axis)
    return jnp.where(
        upper, jnp.concatenate([other, value]), jnp.concatenate([value, other])
    )


def exchange(value, axes):
    return lax.all_to_all(value, axes, 0, 0, tiled=True)


def scatter_sum(value, axes):
    count = math.prod(SIZES[a] for a in axes)
    return jnp.sum(exchange(value.reshape(count, -1, LANES), axes), axis=0)


def whole_sum(value, axes):
    count = math.prod(SIZES[a] for a in axes)
    return jnp.sum(exchange(jnp.broadcast_to(value, (count,) + value.shape), axes), axis=0)


def gather(value, axes):
    count = math.prod(SIZES[a] for a in axes)
    return exchange(jnp.broadcast_to(value, (count,) + value.shape), axes).reshape(-1, LANES)


def reduce_all(value):
    value = half_scatter(value, "core")
    value = scatter_sum(value, PLANE)
    value = whole_sum(value, ("z",))
    value = gather(value, PLANE)
    return half_gather(value, "core")


def per_device(
    source_field,
    receiver_tensor,
    metric_ids,
    metric_table,
    observed,
    receiver_index,
    bin_ids,
    window,
):
    src = source_field.reshape(FIELDS, PLANES, LANES)
    receiver = receiver_tensor.reshape(TENSORS, BINS, 12, PLANES, LANES)
    ids = metric_ids.reshape(PLANES, LANES)
    x_lo, x_hi, y_lo, y_hi, z_lo, z_hi = pack(src)
    x_at, y_at, z_at = lax.axis_index(GX), lax.axis_index(GY), lax.axis_index(GZ)
    ends = [math.prod(SIZES[a] for a in axes) - 1 for axes in (GX, GY, GZ)]
    flags = jnp.stack(
        [x_at > 0, x_at < ends[0], y_at > 0, y_at < ends[1], z_at > 0, z_at < ends[2]]
    ).astype(F32)
    yb, ya = shift(y_hi, GY, 1), shift(y_lo, GY, -1)
    xb, xa = shift(x_hi, GX, 1), shift(x_lo, GX, -1)
    zb, za = shift(z_hi, GZ, 1), shift(z_lo, GZ, -1)

    values = observed.transpose(0, 2, 1)
    tensor = receiver_index.reshape(1, -1)
    bins, marks = bin_ids.T, window.T
    stats = data_sums(values, tensor, bins, marks)
    stats = merge_sums(stats, swap(stats, "core"))
    stats = merge_sums(stats, swap(stats, "xhi"))

    packed, cells = gram(
        flags, metric_table, src, ids, (xb, xa, yb, ya, zb, za), receiver
    )
    packed = reduce_all(packed)
    update, direction, data = chain(packed, stats, cells, values, tensor, bins, marks)
    return (
        update.reshape(metric_ids.shape),
        direction.reshape(metric_ids.shape),
        data.transpose(0, 2, 1),
    )


def solution(mesh):
    fine = Mesh(mesh.devices.reshape([SIZES[a] for a in AXES]), AXES)
    return jax.shard_map(
        per_device,
        mesh=fine,
        in_specs=(
            P(None, None, None, GX, GY, GZ),
            P(None, None, None, None, GX, GY, GZ),
            P(GX, GY, GZ),
            P(),
            P(None, GZ, None),
            P(GZ),
            P(GZ, None),
            P(GZ, None),
        ),
        out_specs=(P(GX, GY, GZ), P(GX, GY, GZ), P(None, GZ, None)),
        check_vma=False,
    )
```

```python
import functools
import math

import jax
import jax.numpy as jnp
from jax import lax
from jax.experimental import pallas as pl
from jax.experimental.pallas import tpu as pltpu
from jax.sharding import Mesh, PartitionSpec as P

ITERS = 2
EPSILON = 1e-06
F32 = jnp.float32
BF16 = jnp.bfloat16

AXES = ("y", "z", "xlo", "xhi", "core")
SIZES = {"y": 4, "z": 8, "xlo": 2, "xhi": 2, "core": 2}
GX = ("y",)
GY = ("z", "xlo")
GZ = ("xhi", "core")
PLANE = ("y", "xlo", "xhi")
VMEM_LIMIT = 16 * 1024 * 1024

BINS = 16
TENSORS = 12
FIELDS = 96
PLANES = 16
LANES = 128
ROWS = 384
BLOCKS = ((0, 0), (0, 1), (0, 2), (1, 1), (1, 2), (2, 2))


def vmem():
    return pl.BlockSpec(memory_space=pltpu.VMEM)


def smem():
    return pl.BlockSpec(memory_space=pltpu.SMEM)


def lane_ids(shape):
    return lax.broadcasted_iota(jnp.int32, shape, len(shape) - 1)


def pack_kernel(src, x_lo, x_hi, y_lo, y_hi, z_lo, z_hi):
    x_lo[...] = src[:, 0:8, :]
    x_hi[...] = src[:, 8:16, :]
    lane = lane_ids((FIELDS, LANES))
    low = jnp.zeros((FIELDS, LANES), F32)
    high = jnp.zeros((FIELDS, LANES), F32)
    for plane in range(PLANES):
        value = src[:, plane, :]
        x, y = divmod(plane, 4)
        if y < 2:
            y_lo[x * 2 + y] = value
        else:
            y_hi[x * 2 + y - 2] = value
        turned = pltpu.roll(value, 8 * plane, 1) if plane else value
        place = (lane - 8 * plane) & (LANES - 1)
        low = jnp.where(place < 2, turned, low)
        high = jnp.where(place >= LANES - 2, turned, high)
    z_lo[...] = low
    z_hi[...] = high


def pack(src):
    face = jax.ShapeDtypeStruct((FIELDS, 8, LANES), F32)
    side = jax.ShapeDtypeStruct((8, FIELDS, LANES), F32)
    ends = jax.ShapeDtypeStruct((FIELDS, LANES), F32)
    return pl.pallas_call(
        pack_kernel,
        out_shape=(face, face, side, side, ends, ends),
        in_specs=[vmem()],
        out_specs=(vmem(),) * 6,
        compiler_params=pltpu.CompilerParams(vmem_limit_bytes=VMEM_LIMIT),
        name="pack",
    )(src)


def spread(values, bins, tensor):
    parts = []
    for b in range(BINS):
        here = bins == b
        for k in range(2):
            parts.append(jnp.sum(jnp.where(here, values[k], 0.0), axis=0, keepdims=True))
    table = jnp.concatenate(parts, axis=0)
    return jnp.concatenate(
        [
            jnp.sum(jnp.where(tensor == r, table, 0.0), axis=1, keepdims=True)
            for r in range(TENSORS)
        ],
        axis=0,
    )


def pick(column, bins, tensor):
    table = jnp.zeros((2 * BINS, bins.shape[1]), F32)
    for r in range(TENSORS):
        table = jnp.where(tensor == r, column[r * 32 : (r + 1) * 32, :], table)
    out = [jnp.zeros(bins.shape, F32), jnp.zeros(bins.shape, F32)]
    for b in range(BINS):
        here = bins == b
        for k in range(2):
            out[k] = jnp.where(here, table[2 * b + k : 2 * b + k + 1, :], out[k])
    return out


def data_kernel(observed, tensor_ref, bins_ref, window, stats):
    tensor, bins = tensor_ref[...], bins_ref[...]
    mask = window[...].astype(F32)
    rhs = [observed[k] * mask for k in range(2)]
    total = spread(rhs, bins, tensor)
    count = spread([mask, mask], bins, tensor)
    mean = total / jnp.maximum(count, 1.0)
    near = pick(mean, bins, tensor)
    rest = [rhs[k] - near[k] * mask for k in range(2)]
    square = jnp.sum(rest[0] * rest[0] + rest[1] * rest[1], axis=(0, 1), keepdims=True)
    lane = lane_ids((ROWS, LANES))
    wide = jnp.where(lane == 0, total, jnp.where(lane == 1, count, square))
    for j in range(3):
        stats[:, j * LANES : (j + 1) * LANES] = wide[j * LANES : (j + 1) * LANES, :].T[:8]


def data_sums(observed, tensor, bins, window):
    return pl.pallas_call(
        data_kernel,
        out_shape=jax.ShapeDtypeStruct((8, ROWS), F32),
        in_specs=[vmem()] * 4,
        out_specs=vmem(),
        compiler_params=pltpu.CompilerParams(vmem_limit_bytes=VMEM_LIMIT),
        name="data_sums",
    )(observed, tensor, bins, window)


def merge_sums(one, two):
    total, count = one[0:1] + two[0:1], one[1:2] + two[1:2]
    gap = one[0:1] / jnp.maximum(one[1:2], 1.0) - two[0:1] / jnp.maximum(two[1:2], 1.0)
    apart = jnp.sum(one[1:2] * two[1:2] / jnp.maximum(count, 1.0) * gap * gap)
    rest = one[2:3] + two[2:3] + apart
    return jnp.concatenate([total, count, rest, jnp.zeros((5, ROWS), F32)], axis=0)


def ends_of(axes):
    at = lax.axis_index(axes)
    last = math.prod(SIZES[a] for a in axes) - 1
    return jnp.where(at > 0, 1.0, 0.0).astype(F32), jnp.where(at < last, 1.0, 0.0).astype(F32)


def scale_of(table, marks, p):
    scale = jnp.zeros((PLANES, LANES), F32)
    for m in range(8):
        scale = jnp.where(marks == m, table[p, m], scale)
    return scale * (1.0 / 12.0)


def tile(ref, at):
    return ref[pl.ds(pl.multiple_of(at * PLANES, PLANES), PLANES), :]


def set_tile(ref, at, value):
    ref[pl.ds(pl.multiple_of(at * PLANES, PLANES), PLANES), :] = value


def rows_of(start, strains, first):
    re, im = start
    for rec_re, rec_im, real, imag in strains:
        rec_re, rec_im = rec_re.astype(F32), rec_im.astype(F32)
        add_re, add_im = rec_re * real - rec_im * imag, rec_re * imag + rec_im * real
        re, im = (add_re, add_im) if first else (re + add_re, im + add_im)
        first = False
    return re, im


def cells_kernel(table, src, ids, xb, xa, zb, za, receiver, cells, grads, scales):
    step = pl.program_id(0)

    @pl.when(step == 0)
    def _():
        for p in range(3):
            scales[p * PLANES : (p + 1) * PLANES, :] = scale_of(table, ids[...], p)
        lane = lane_ids((FIELDS, LANES))
        x_before, x_after = ends_of(GX)
        z_before, z_after = ends_of(GZ)
        halo = zb[...] * z_before + za[...] * z_after

        def at(x, y):
            if x < 0:
                return xb[pl.ds((x + 2) * 4 + y, FIELDS, stride=8), :] * x_before
            if x > 3:
                return xa[pl.ds((x - 4) * 4 + y, FIELDS, stride=8), :] * x_after
            if y < 0 or y > 3:
                return 0.0
            return src[pl.ds(x * 4 + y, FIELDS, stride=PLANES), :]

        def put(p, plane, value):
            grads[pl.ds(p * FIELDS * PLANES + plane, FIELDS, stride=PLANES), :] = value

        for x in range(4):
            for y in range(4):
                plane = x * 4 + y
                put(0, plane, 8.0 * (at(x + 1, y) - at(x - 1, y)) - (at(x + 2, y) - at(x - 2, y)))
                put(1, plane, 8.0 * (at(x, y + 1) - at(x, y - 1)) - (at(x, y + 2) - at(x, y - 2)))
                mid = at(x, y)
                ends = pltpu.roll(halo, LANES - 8 * plane, 1) if plane else halo
                later = pltpu.roll(jnp.where(lane < 1, ends, mid), LANES - 1, 1)
                sooner = pltpu.roll(jnp.where(lane >= LANES - 1, ends, mid), 1, 1)
                later_two = pltpu.roll(jnp.where(lane < 2, ends, mid), LANES - 2, 1)
                sooner_two = pltpu.roll(jnp.where(lane >= LANES - 2, ends, mid), 2, 1)
                put(2, plane, 8.0 * (later - sooner) - (later_two - sooner_two))

    def grad(p, q, k):
        return tile(scales, p) * tile(grads, p * FIELDS + step * 6 + q * 2 + k)

    real, imag = [
        (
            grad(0, 0, k),
            grad(1, 1, k),
            grad(2, 2, k),
            grad(1, 2, k) + grad(2, 1, k),
            grad(0, 2, k) + grad(2, 0, k),
            grad(0, 1, k) + grad(1, 0, k),
        )
        for k in range(2)
    ]
    for r in range(TENSORS):
        terms = [
            (receiver[r, 0, 2 * j], receiver[r, 0, 2 * j + 1], real[j], imag[j]) for j in range(6)
        ]
        re, im = rows_of((None, None), terms, True)
        set_tile(cells, r * 32 + step * 2, re)
        set_tile(cells, r * 32 + step * 2 + 1, im)


def whole(*shape):
    return pl.BlockSpec(shape, lambda b: (0,) * len(shape))


def cells_within(table, src, ids, halos, receiver):
    face = whole(FIELDS * 8, LANES)
    ends = whole(FIELDS, LANES)
    return pl.pallas_call(
        cells_kernel,
        grid=(BINS,),
        out_shape=jax.ShapeDtypeStruct((ROWS * PLANES, LANES), F32),
        in_specs=[
            smem(),
            whole(FIELDS * PLANES, LANES),
            whole(PLANES, LANES),
            face,
            face,
            ends,
            ends,
            pl.BlockSpec((TENSORS, 1, 12, PLANES, LANES), lambda b: (0, b, 0, 0, 0)),
        ],
        out_specs=whole(ROWS * PLANES, LANES),
        scratch_shapes=[
            pltpu.VMEM((3 * FIELDS * PLANES, LANES), F32),
            pltpu.VMEM((3 * PLANES, LANES), F32),
        ],
        compiler_params=pltpu.CompilerParams(vmem_limit_bytes=VMEM_LIMIT),
        cost_estimate=pl.CostEstimate(
            flops=20_000_000, bytes_accessed=14_000_000, transcendentals=0
        ),
        name="cells_within",
    )(table, src, ids, *halos, receiver)


def gram_kernel(
    table, ids, yb, ya, within, receiver, s0, s1, s2, s3, keep, send, cells, stats, grads, scales
):
    step = pl.program_id(0)

    @pl.when(step == 0)
    def _():
        scales[...] = scale_of(table, ids[...], 1)
        before, after = ends_of(GY)
        for x in range(4):
            b_two, b_one = yb[x * 2] * before, yb[x * 2 + 1] * before
            a_one, a_two = ya[x * 2] * after, ya[x * 2 + 1] * after
            for y, value in enumerate(
                (b_two - 8.0 * b_one, b_one, -a_one, 8.0 * a_one - a_two)
            ):
                grads[pl.ds(x * 4 + y, FIELDS, stride=PLANES), :] = value
        stats[...] = merge_sums(merge_sums(s0[...], s1[...]), merge_sums(s2[...], s3[...]))

    def grad(q, k):
        return scales[...] * tile(grads, step * 6 + q * 2 + k)

    real, imag = [(grad(1, k), grad(2, k), grad(0, k)) for k in range(2)]
    for r in range(TENSORS):
        at = r * 32 + step * 2
        terms = [
            (receiver[r, 0, j, 0, 0], receiver[r, 0, j, 0, 1], real[j], imag[j]) for j in range(3)
        ]
        re, im = rows_of((tile(within, at), tile(within, at + 1)), terms, False)
        set_tile(cells, at, re)
        set_tile(cells, at + 1, im)

    @pl.when(step == BINS - 1)
    def _():
        total = jnp.zeros((ROWS, ROWS), F32)
        for plane in range(0, PLANES, 2):
            both = jnp.concatenate(
                [cells[pl.ds(plane + i, ROWS, stride=PLANES), :] for i in range(2)], axis=1
            )
            high = both.astype(BF16)
            low = (both - high.astype(F32)).astype(BF16)
            left = jnp.concatenate([high, high], axis=1)
            right = jnp.concatenate([high * BF16(0.5), low], axis=1)
            total = total + lax.dot_general(
                left, right, (((1,), (1,)), ((), ())), preferred_element_type=F32
            )

        def block(i, j):
            return total[i * LANES : (i + 1) * LANES, j * LANES : (j + 1) * LANES]

        full = [block(i, j) + block(j, i).T for i, j in BLOCKS]
        upper = lax.axis_index("core") == 1
        for n in range(3):
            part = slice(n * LANES, (n + 1) * LANES)
            keep[part, :] = jnp.where(upper, full[n + 3], full[n])
            send[part, :] = jnp.where(upper, full[n], full[n + 3])


def gram(table, ids, halos, within, receiver, sums):
    side = whole(8, FIELDS, LANES)
    half = jax.ShapeDtypeStruct((3 * LANES, LANES), F32)
    return pl.pallas_call(
        gram_kernel,
        grid=(BINS,),
        out_shape=(
            half,
            half,
            jax.ShapeDtypeStruct((ROWS * PLANES, LANES), F32),
            jax.ShapeDtypeStruct((8, ROWS), F32),
        ),
        in_specs=[
            smem(),
            whole(PLANES, LANES),
            side,
            side,
            whole(ROWS * PLANES, LANES),
            pl.BlockSpec(
                (TENSORS, 1, 3, 1, 2, PLANES, LANES), lambda b: (0, b, 0, 1, 0, 0, 0)
            ),
        ]
        + [whole(8, ROWS)] * 4,
        out_specs=(
            whole(3 * LANES, LANES),
            whole(3 * LANES, LANES),
            whole(ROWS * PLANES, LANES),
            whole(8, ROWS),
        ),
        scratch_shapes=[
            pltpu.VMEM((FIELDS * PLANES, LANES), F32),
            pltpu.VMEM((PLANES, LANES), F32),
        ],
        compiler_params=pltpu.CompilerParams(vmem_limit_bytes=VMEM_LIMIT),
        cost_estimate=pl.CostEstimate(
            flops=1_200_000_000, bytes_accessed=8_000_000, transcendentals=0
        ),
        name="gram",
    )(table, ids, *halos, within, receiver, *sums)


def chain_kernel(
    mine, other, stats, cells, observed_in, tensor_in, bins_in, window_in, update, direction, data,
    full, coef, observed, tensor_ref, bins_ref, window, sems
):
    copies = [
        pltpu.make_async_copy(here, there, sems.at[n])
        for n, (here, there) in enumerate(
            (
                (observed_in, observed),
                (tensor_in, tensor_ref),
                (bins_in, bins_ref),
                (window_in, window),
            )
        )
    ]
    for copy in copies:
        copy.start()
    upper = lax.axis_index("core") == 1
    for n, (i, j) in enumerate(BLOCKS):
        part = slice(n % 3 * LANES, (n % 3 + 1) * LANES)
        near, far = mine[part, :], other[part, :]
        block = jnp.where(upper, far, near) if n < 3 else jnp.where(upper, near, far)
        full[i * LANES : (i + 1) * LANES, j * LANES : (j + 1) * LANES] = block
        if i != j:
            full[j * LANES : (j + 1) * LANES, i * LANES : (i + 1) * LANES] = block.T
    eye = lax.broadcasted_iota(jnp.int32, (LANES, LANES), 0) == lane_ids((LANES, LANES))

    def column(row):
        return jnp.concatenate(
            [
                jnp.sum(
                    jnp.where(eye, row[:, j * LANES : (j + 1) * LANES], 0.0), axis=1, keepdims=True
                )
                for j in range(3)
            ],
            axis=0,
        )

    def product(row):
        return jnp.sum(full[...] * column(row), axis=0, keepdims=True)

    def total(row):
        return jnp.sum(row, axis=1, keepdims=True)

    def norm_of(square):
        return jnp.sqrt(square + EPSILON)

    sums, count, rest = stats[0:1, :], stats[1:2, :], stats[2:3, 0:1]
    mean = sums / jnp.maximum(count, 1.0)

    def data_norm(scale, row):
        inside = scale * mean + row
        return norm_of(scale * scale * rest + total(count * inside * inside))

    one = jnp.ones((1, 1), F32)
    row = jnp.zeros((1, ROWS), F32)
    beta = data_norm(one, row)
    beta_first = beta
    scale = one / beta
    raw = scale * sums
    image = product(raw)
    alpha = norm_of(total(raw * image))
    alpha_first = alpha
    model = raw / alpha
    search = model
    answer = jnp.zeros((1, ROWS), F32)
    phi_bar, rho_bar = beta, alpha
    for _ in range(ITERS):
        scale, row = -alpha * scale, image / alpha - alpha * row
        beta = data_norm(scale, row)
        scale, row = scale / beta, row / beta
        raw = scale * sums + count * row - beta * model
        image = product(raw)
        alpha = norm_of(total(raw * image))
        model = raw / alpha
        rho = jnp.sqrt(rho_bar * rho_bar + beta * beta)
        cosine, sine = rho_bar / rho, beta / rho
        theta = sine * alpha
        rho_bar = -cosine * alpha
        phi = cosine * phi_bar
        phi_bar = sine * phi_bar
        answer = answer + phi / rho * search
        search = model - theta / rho * search
    cell_scale = math.sqrt(PLANES * LANES * math.prod(SIZES.values()))
    coef[0] = jnp.broadcast_to(
        column(answer * (alpha_first * cell_scale / beta_first)), (ROWS, LANES)
    )
    coef[1] = jnp.broadcast_to(column(model * cell_scale), (ROWS, LANES))

    def body(n, sums_of):
        value = tile(cells, n)
        return (
            sums_of[0] + coef[0, pl.ds(n, 1), :] * value,
            sums_of[1] + coef[1, pl.ds(n, 1), :] * value,
        )

    start = (jnp.zeros((PLANES, LANES), F32), jnp.zeros((PLANES, LANES), F32))
    first, second = lax.fori_loop(0, ROWS, body, start, unroll=16)
    update[...] = first
    direction[...] = second

    for copy in copies:
        copy.wait()
    mask = window[...].astype(F32)
    size = math.sqrt(math.prod(observed.shape) * SIZES["xhi"] * SIZES["core"])
    near = pick(column(row * size), bins_ref[...], tensor_ref[...])
    for k in range(2):
        data[k] = (observed[k] * (scale * size) + near[k]) * mask


def chain(mine, other, stats, cells, observed, tensor, bins, window):
    field = jax.ShapeDtypeStruct((PLANES, LANES), F32)
    given = (observed, tensor, bins, window)
    return pl.pallas_call(
        chain_kernel,
        out_shape=(field, field, jax.ShapeDtypeStruct(observed.shape, F32)),
        in_specs=[vmem()] * 4 + [pl.BlockSpec(memory_space=pl.ANY)] * 4,
        out_specs=(vmem(),) * 3,
        scratch_shapes=[pltpu.VMEM((ROWS, ROWS), F32), pltpu.VMEM((2, ROWS, LANES), F32)]
        + [pltpu.VMEM(x.shape, x.dtype) for x in given]
        + [pltpu.SemaphoreType.DMA((4,))],
        compiler_params=pltpu.CompilerParams(vmem_limit_bytes=VMEM_LIMIT),
        name="chain",
    )(mine, other, stats, cells, *given)


def shift(value, axes, step):
    count = math.prod(SIZES[a] for a in axes)
    return lax.ppermute(value, axes, [(i, (i + step) % count) for i in range(count)])


def swap(value, axis):
    return lax.ppermute(value, axis, [(0, 1), (1, 0)])


def exchange(value, axes):
    return lax.all_to_all(value, axes, 0, 0, tiled=True)


def scatter_sum(value, axes):
    count = math.prod(SIZES[a] for a in axes)
    return jnp.sum(exchange(value.reshape(count, -1, LANES), axes), axis=0)


def whole_sum(value, axes):
    count = math.prod(SIZES[a] for a in axes)
    return jnp.sum(exchange(jnp.broadcast_to(value, (count,) + value.shape), axes), axis=0)


def gather(value, axes):
    count = math.prod(SIZES[a] for a in axes)
    return exchange(jnp.broadcast_to(value, (count,) + value.shape), axes).reshape(-1, LANES)


def per_device(
    source_field,
    receiver_tensor,
    metric_ids,
    metric_table,
    observed,
    receiver_index,
    bin_ids,
    window,
):
    src = source_field.reshape(FIELDS, PLANES, LANES)
    receiver = receiver_tensor.reshape(TENSORS, BINS, 12, PLANES, LANES)
    by_pairs = receiver_tensor.reshape(TENSORS, BINS, 3, 2, 2, PLANES, LANES)
    ids = metric_ids.reshape(PLANES, LANES)
    table = metric_table.T
    x_lo, x_hi, y_lo, y_hi, z_lo, z_hi = pack(src)
    zb, za = shift(z_hi, GZ, 1), shift(z_lo, GZ, -1)
    xb, xa = shift(x_hi, GX, 1), shift(x_lo, GX, -1)
    yb, ya = shift(y_hi, GY, 1), shift(y_lo, GY, -1)

    values = observed.transpose(0, 2, 1)
    tensor = receiver_index.reshape(1, -1)
    bins, marks = bin_ids.T, window.T
    stats = data_sums(values, tensor, bins, marks)
    near = swap(stats, "core")
    sums = (stats, near, swap(stats, "xhi"), swap(near, "xhi"))

    flat = (FIELDS * 8, LANES)
    within = cells_within(
        table,
        src.reshape(FIELDS * PLANES, LANES),
        ids,
        (xb.reshape(flat), xa.reshape(flat), zb, za),
        receiver,
    )
    keep, send, cells, stats = gram(table, ids, (yb, ya), within, by_pairs, sums)
    packed = keep + swap(send, "core")
    packed = scatter_sum(packed, PLANE)
    packed = whole_sum(packed, ("z",))
    packed = gather(packed, PLANE)
    other = swap(packed, "core")
    update, direction, data = chain(packed, other, stats, cells, values, tensor, bins, marks)
    return (
        update.reshape(metric_ids.shape),
        direction.reshape(metric_ids.shape),
        data.transpose(0, 2, 1),
    )


def solution(mesh):
    fine = Mesh(mesh.devices.reshape([SIZES[a] for a in AXES]), AXES)
    return jax.shard_map(
        per_device,
        mesh=fine,
        in_specs=(
            P(None, None, None, GX, GY, GZ),
            P(None, None, None, None, GX, GY, GZ),
            P(GX, GY, GZ),
            P(),
            P(None, GZ, None),
            P(GZ),
            P(GZ, None),
            P(GZ, None),
        ),
        out_specs=(P(GX, GY, GZ), P(GX, GY, GZ), P(None, GZ, None)),
        check_vma=False,
    )
```

```python
import functools
import math

import jax
import jax.numpy as jnp
from jax import lax
from jax.experimental import pallas as pl
from jax.experimental.pallas import tpu as pltpu
from jax.sharding import Mesh, PartitionSpec as P

ITERS = 2
EPSILON = 1e-06
F32 = jnp.float32
BF16 = jnp.bfloat16

AXES = ("y", "z", "xlo", "xhi", "core")
SIZES = {"y": 4, "z": 8, "xlo": 2, "xhi": 2, "core": 2}
GX = ("y",)
GY = ("z", "xlo")
GZ = ("xhi", "core")
PLANE = ("y", "xlo", "xhi")
VMEM_LIMIT = 16 * 1024 * 1024

BINS = 16
TENSORS = 12
FIELDS = 96
PLANES = 16
LANES = 128
ROWS = 384
BLOCKS = ((0, 0), (0, 1), (0, 2), (1, 1), (1, 2), (2, 2))


def vmem():
    return pl.BlockSpec(memory_space=pltpu.VMEM)


def hbm():
    return pl.BlockSpec(memory_space=pltpu.HBM)


def lane_ids(shape):
    return lax.broadcasted_iota(jnp.int32, shape, len(shape) - 1)


def spread(values, bins, tensor):
    parts = []
    for b in range(BINS):
        here = bins == b
        for k in range(2):
            parts.append(jnp.sum(jnp.where(here, values[k], 0.0), axis=0, keepdims=True))
    table = jnp.concatenate(parts, axis=0)
    return jnp.concatenate(
        [
            jnp.sum(jnp.where(tensor == r, table, 0.0), axis=1, keepdims=True)
            for r in range(TENSORS)
        ],
        axis=0,
    )


def pick(column, bins, tensor):
    table = jnp.zeros((2 * BINS, bins.shape[1]), F32)
    for r in range(TENSORS):
        table = jnp.where(tensor == r, column[r * 32 : (r + 1) * 32, :], table)
    out = [jnp.zeros(bins.shape, F32), jnp.zeros(bins.shape, F32)]
    for b in range(BINS):
        here = bins == b
        for k in range(2):
            out[k] = jnp.where(here, table[2 * b + k : 2 * b + k + 1, :], out[k])
    return out


def data_sums(observed, tensor, bins, window):
    mask = window.astype(F32)
    rhs = [observed[k] * mask for k in range(2)]
    total = spread(rhs, bins, tensor)
    count = spread([mask, mask], bins, tensor)
    mean = total / jnp.maximum(count, 1.0)
    near = pick(mean, bins, tensor)
    rest = [rhs[k] - near[k] * mask for k in range(2)]
    square = jnp.sum(rest[0] * rest[0] + rest[1] * rest[1], axis=(0, 1), keepdims=True)
    lane = lane_ids((ROWS, LANES))
    wide = jnp.where(lane == 0, total, jnp.where(lane == 1, count, square))
    return jnp.concatenate([wide[j * LANES : (j + 1) * LANES, :].T[:8] for j in range(3)], axis=0)


def merge_sums(one, two):
    total, count = one[0:1] + two[0:1], one[1:2] + two[1:2]
    gap = one[0:1] / jnp.maximum(one[1:2], 1.0) - two[0:1] / jnp.maximum(two[1:2], 1.0)
    apart = jnp.sum(
        one[1:2] * two[1:2] / jnp.maximum(count, 1.0) * gap * gap, axis=1, keepdims=True
    )
    rest = one[2:3] + two[2:3] + apart
    return jnp.concatenate([total, count, rest, jnp.zeros((5, ROWS), F32)], axis=0)


def pack_kernel(
    src_in, ids_in, table_in, observed_in, tensor_in, bins_in, window_in,
    src, x_lo, x_hi, y_lo, y_hi, to_core, to_cross, stats, scales,
    ids, table, observed, tensor, bins, window, sems,
):
    copies = [
        pltpu.make_async_copy(here, there, sems.at[n])
        for n, (here, there) in enumerate(
            (
                (src_in, src),
                (ids_in, ids),
                (table_in, table),
                (observed_in, observed),
                (tensor_in, tensor),
                (bins_in, bins),
                (window_in, window),
            )
        )
    ]
    for copy in copies:
        copy.start()
    for copy in copies[1:]:
        copy.wait()
    for p in range(3):
        scale = jnp.zeros((PLANES, LANES), F32)
        for m in range(8):
            scale = jnp.where(ids[...] == m, table[p, m], scale)
        scales[p * PLANES : (p + 1) * PLANES, :] = scale * (1.0 / 12.0)
    sums = data_sums(observed, tensor[...], bins[...], window[...])
    stats[...] = sums
    to_core[FIELDS:, :] = sums
    to_cross[FIELDS:, :] = sums

    copies[0].wait()
    x_lo[...] = src[:, 0:8, :]
    x_hi[...] = src[:, 8:16, :]
    lane = lane_ids((FIELDS, LANES))
    low = jnp.zeros((FIELDS, LANES), F32)
    high = jnp.zeros((FIELDS, LANES), F32)
    for plane in range(PLANES):
        value = src[:, plane, :]
        x, y = divmod(plane, 4)
        if y < 2:
            y_lo[x * 2 + y] = value
        else:
            y_hi[x * 2 + y - 2] = value
        turned = pltpu.roll(value, 8 * plane, 1) if plane else value
        place = (lane - 8 * plane) & (LANES - 1)
        low = jnp.where(place < 2, turned, low)
        high = jnp.where(place >= LANES - 2, turned, high)
    upper = lax.axis_index("core") == 1
    to_core[:FIELDS, :] = jnp.where(upper, low, high)
    to_cross[:FIELDS, :] = jnp.where(upper, high, low)


def pack(src, ids, table, observed, tensor, bins, window):
    face = jax.ShapeDtypeStruct((FIELDS, 8, LANES), F32)
    side = jax.ShapeDtypeStruct((8, FIELDS, LANES), F32)
    ends = jax.ShapeDtypeStruct((FIELDS + 24, LANES), F32)
    given = (src, ids, table, observed, tensor, bins, window)
    return pl.pallas_call(
        pack_kernel,
        out_shape=(
            jax.ShapeDtypeStruct(src.shape, F32),
            face,
            face,
            side,
            side,
            ends,
            ends,
            jax.ShapeDtypeStruct((24, LANES), F32),
            jax.ShapeDtypeStruct((3 * PLANES, LANES), F32),
        ),
        in_specs=[hbm()] * 7,
        out_specs=(vmem(),) * 9,
        scratch_shapes=[pltpu.VMEM(ids.shape, ids.dtype), pltpu.SMEM(table.shape, table.dtype)]
        + [pltpu.VMEM(x.shape, x.dtype) for x in given[3:]]
        + [pltpu.SemaphoreType.DMA((7,))],
        compiler_params=pltpu.CompilerParams(vmem_limit_bytes=VMEM_LIMIT),
        name="pack",
    )(*given)


def ends_of(axes):
    at = lax.axis_index(axes)
    last = math.prod(SIZES[a] for a in axes) - 1
    return jnp.where(at > 0, 1.0, 0.0).astype(F32), jnp.where(at < last, 1.0, 0.0).astype(F32)


def tile(ref, at):
    return ref[pl.ds(pl.multiple_of(at * PLANES, PLANES), PLANES), :]


def set_tile(ref, at, value):
    ref[pl.ds(pl.multiple_of(at * PLANES, PLANES), PLANES), :] = value


def rows_of(start, strains, first):
    re, im = start
    for rec_re, rec_im, real, imag in strains:
        rec_re, rec_im = rec_re.astype(F32), rec_im.astype(F32)
        add_re, add_im = rec_re * real - rec_im * imag, rec_re * imag + rec_im * real
        re, im = (add_re, add_im) if first else (re + add_re, im + add_im)
        first = False
    return re, im


def cells_kernel(scales, src, xb, xa, from_core, from_cross, receiver, cells, grads, slots, sems):
    def fetch(b, slot):
        return pltpu.make_async_copy(receiver.at[:, b], slots.at[slot], sems.at[slot])

    fetch(0, 0).start()
    lane = lane_ids((FIELDS, LANES))
    x_before, x_after = ends_of(GX)
    crossing = jnp.where(lax.axis_index("xhi") != lax.axis_index("core"), 1.0, 0.0).astype(F32)
    halo = from_core[:FIELDS, :] + from_cross[:FIELDS, :] * crossing

    def at(x, y):
        if x < 0:
            return xb[pl.ds((x + 2) * 4 + y, FIELDS, stride=8), :] * x_before
        if x > 3:
            return xa[pl.ds((x - 4) * 4 + y, FIELDS, stride=8), :] * x_after
        if y < 0 or y > 3:
            return 0.0
        return src[pl.ds(x * 4 + y, FIELDS, stride=PLANES), :]

    def put(p, plane, value):
        grads[pl.ds(p * FIELDS * PLANES + plane, FIELDS, stride=PLANES), :] = value

    for x in range(4):
        for y in range(4):
            plane = x * 4 + y
            put(0, plane, 8.0 * (at(x + 1, y) - at(x - 1, y)) - (at(x + 2, y) - at(x - 2, y)))
            put(1, plane, 8.0 * (at(x, y + 1) - at(x, y - 1)) - (at(x, y + 2) - at(x, y - 2)))
            mid = at(x, y)
            ends = pltpu.roll(halo, LANES - 8 * plane, 1) if plane else halo
            later = pltpu.roll(jnp.where(lane < 1, ends, mid), LANES - 1, 1)
            sooner = pltpu.roll(jnp.where(lane >= LANES - 1, ends, mid), 1, 1)
            later_two = pltpu.roll(jnp.where(lane < 2, ends, mid), LANES - 2, 1)
            sooner_two = pltpu.roll(jnp.where(lane >= LANES - 2, ends, mid), 2, 1)
            put(2, plane, 8.0 * (later - sooner) - (later_two - sooner_two))

    def body(b, carry):
        slot = b & 1

        @pl.when(b + 1 < BINS)
        def _():
            fetch(b + 1, 1 - slot).start()

        def grad(p, q, k):
            return tile(scales, p) * tile(grads, p * FIELDS + b * 6 + q * 2 + k)

        real, imag = [
            (
                grad(0, 0, k),
                grad(1, 1, k),
                grad(2, 2, k),
                grad(1, 2, k) + grad(2, 1, k),
                grad(0, 2, k) + grad(2, 0, k),
                grad(0, 1, k) + grad(1, 0, k),
            )
            for k in range(2)
        ]
        fetch(b, slot).wait()
        for r in range(TENSORS):
            terms = [
                (slots[slot, r, 2 * j], slots[slot, r, 2 * j + 1], real[j], imag[j])
                for j in range(6)
            ]
            re, im = rows_of((None, None), terms, True)
            set_tile(cells, r * 32 + b * 2, re)
            set_tile(cells, r * 32 + b * 2 + 1, im)
        return carry

    lax.fori_loop(0, BINS, body, 0)


def whole(*shape):
    return pl.BlockSpec(shape, lambda b: (0,) * len(shape))


def cells_within(scales, src, halos, receiver):
    return pl.pallas_call(
        cells_kernel,
        out_shape=jax.ShapeDtypeStruct((ROWS * PLANES, LANES), F32),
        in_specs=[vmem()] * 6 + [hbm()],
        out_specs=vmem(),
        scratch_shapes=[
            pltpu.VMEM((3 * FIELDS * PLANES, LANES), F32),
            pltpu.VMEM((2, TENSORS, 12, PLANES, LANES), BF16),
            pltpu.SemaphoreType.DMA((2,)),
        ],
        compiler_params=pltpu.CompilerParams(vmem_limit_bytes=VMEM_LIMIT),
        cost_estimate=pl.CostEstimate(
            flops=20_000_000, bytes_accessed=14_000_000, transcendentals=0
        ),
        name="cells_within",
    )(scales, src, *halos, receiver)


def gram_kernel(
    scales, yb, ya, within, receiver, own, from_core, from_cross, from_xhi, keep, send, cells, stats, grads
):
    step = pl.program_id(0)

    @pl.when(step == 0)
    def _():
        before, after = ends_of(GY)
        for x in range(4):
            b_two, b_one = yb[x * 2] * before, yb[x * 2 + 1] * before
            a_one, a_two = ya[x * 2] * after, ya[x * 2 + 1] * after
            for y, value in enumerate(
                (b_two - 8.0 * b_one, b_one, -a_one, 8.0 * a_one - a_two)
            ):
                grads[pl.ds(x * 4 + y, FIELDS, stride=PLANES), :] = value

        def sums_of(value):
            return jnp.concatenate([value[8 * j : 8 * j + 8, :] for j in range(3)], axis=1)

        stats[...] = merge_sums(
            merge_sums(sums_of(own[...]), sums_of(from_core[FIELDS:, :])),
            merge_sums(sums_of(from_cross[FIELDS:, :]), sums_of(from_xhi[...])),
        )

    def grad(q, k):
        return tile(scales, 1) * tile(grads, step * 6 + q * 2 + k)

    real, imag = [(grad(1, k), grad(2, k), grad(0, k)) for k in range(2)]
    for r in range(TENSORS):
        at = r * 32 + step * 2
        terms = [
            (receiver[r, 0, j, 0, 0], receiver[r, 0, j, 0, 1], real[j], imag[j]) for j in range(3)
        ]
        re, im = rows_of((tile(within, at), tile(within, at + 1)), terms, False)
        set_tile(cells, at, re)
        set_tile(cells, at + 1, im)

    @pl.when(step == BINS - 1)
    def _():
        total = jnp.zeros((ROWS, ROWS), F32)
        for plane in range(0, PLANES, 2):
            both = jnp.concatenate(
                [cells[pl.ds(plane + i, ROWS, stride=PLANES), :] for i in range(2)], axis=1
            )
            high = both.astype(BF16)
            low = (both - high.astype(F32)).astype(BF16)
            left = jnp.concatenate([high, high], axis=1)
            right = jnp.concatenate([high * BF16(0.5), low], axis=1)
            total = total + lax.dot_general(
                left, right, (((1,), (1,)), ((), ())), preferred_element_type=F32
            )

        def block(i, j):
            return total[i * LANES : (i + 1) * LANES, j * LANES : (j + 1) * LANES]

        full = [block(i, j) + block(j, i).T for i, j in BLOCKS]
        upper = lax.axis_index("core") == 1
        for n in range(3):
            part = slice(n * LANES, (n + 1) * LANES)
            keep[part, :] = jnp.where(upper, full[n + 3], full[n])
            send[part, :] = jnp.where(upper, full[n], full[n + 3])


def gram(scales, halos, within, receiver, sums):
    side = whole(8, FIELDS, LANES)
    half = jax.ShapeDtypeStruct((3 * LANES, LANES), F32)
    return pl.pallas_call(
        gram_kernel,
        grid=(BINS,),
        out_shape=(
            half,
            half,
            jax.ShapeDtypeStruct((ROWS * PLANES, LANES), F32),
            jax.ShapeDtypeStruct((8, ROWS), F32),
        ),
        in_specs=[
            whole(3 * PLANES, LANES),
            side,
            side,
            whole(ROWS * PLANES, LANES),
            pl.BlockSpec(
                (TENSORS, 1, 3, 1, 2, PLANES, LANES), lambda b: (0, b, 0, 1, 0, 0, 0)
            ),
        ]
        + [whole(24, LANES), whole(120, LANES), whole(120, LANES), whole(24, LANES)],
        out_specs=(
            whole(3 * LANES, LANES),
            whole(3 * LANES, LANES),
            whole(ROWS * PLANES, LANES),
            whole(8, ROWS),
        ),
        scratch_shapes=[pltpu.VMEM((FIELDS * PLANES, LANES), F32)],
        compiler_params=pltpu.CompilerParams(vmem_limit_bytes=VMEM_LIMIT),
        cost_estimate=pl.CostEstimate(
            flops=1_200_000_000, bytes_accessed=8_000_000, transcendentals=0
        ),
        name="gram",
    )(scales, *halos, within, receiver, *sums)


def chain_kernel(
    mine, other, stats, cells, observed_in, tensor_in, bins_in, window_in, update, direction, data,
    full, coef, observed, tensor_ref, bins_ref, window, sems
):
    copies = [
        pltpu.make_async_copy(here, there, sems.at[n])
        for n, (here, there) in enumerate(
            (
                (observed_in, observed),
                (tensor_in, tensor_ref),
                (bins_in, bins_ref),
                (window_in, window),
            )
        )
    ]
    for copy in copies:
        copy.start()
    upper = lax.axis_index("core") == 1
    for n, (i, j) in enumerate(BLOCKS):
        part = slice(n % 3 * LANES, (n % 3 + 1) * LANES)
        near, far = mine[part, :], other[part, :]
        block = jnp.where(upper, far, near) if n < 3 else jnp.where(upper, near, far)
        full[i * LANES : (i + 1) * LANES, j * LANES : (j + 1) * LANES] = block
        if i != j:
            full[j * LANES : (j + 1) * LANES, i * LANES : (i + 1) * LANES] = block.T
    eye = lax.broadcasted_iota(jnp.int32, (LANES, LANES), 0) == lane_ids((LANES, LANES))

    def column(row):
        return jnp.concatenate(
            [
                jnp.sum(
                    jnp.where(eye, row[:, j * LANES : (j + 1) * LANES], 0.0), axis=1, keepdims=True
                )
                for j in range(3)
            ],
            axis=0,
        )

    def product(row):
        return jnp.sum(full[...] * column(row), axis=0, keepdims=True)

    def total(row):
        return jnp.sum(row, axis=1, keepdims=True)

    def norm_of(square):
        return jnp.sqrt(square + EPSILON)

    sums, count, rest = stats[0:1, :], stats[1:2, :], stats[2:3, 0:1]
    mean = sums / jnp.maximum(count, 1.0)

    def data_norm(scale, row):
        inside = scale * mean + row
        return norm_of(scale * scale * rest + total(count * inside * inside))

    one = jnp.ones((1, 1), F32)
    row = jnp.zeros((1, ROWS), F32)
    beta = data_norm(one, row)
    beta_first = beta
    scale = one / beta
    raw = scale * sums
    image = product(raw)
    alpha = norm_of(total(raw * image))
    alpha_first = alpha
    model = raw / alpha
    search = model
    answer = jnp.zeros((1, ROWS), F32)
    phi_bar, rho_bar = beta, alpha
    for _ in range(ITERS):
        scale, row = -alpha * scale, image / alpha - alpha * row
        beta = data_norm(scale, row)
        scale, row = scale / beta, row / beta
        raw = scale * sums + count * row - beta * model
        image = product(raw)
        alpha = norm_of(total(raw * image))
        model = raw / alpha
        rho = jnp.sqrt(rho_bar * rho_bar + beta * beta)
        cosine, sine = rho_bar / rho, beta / rho
        theta = sine * alpha
        rho_bar = -cosine * alpha
        phi = cosine * phi_bar
        phi_bar = sine * phi_bar
        answer = answer + phi / rho * search
        search = model - theta / rho * search
    cell_scale = math.sqrt(PLANES * LANES * math.prod(SIZES.values()))
    coef[0] = jnp.broadcast_to(
        column(answer * (alpha_first * cell_scale / beta_first)), (ROWS, LANES)
    )
    coef[1] = jnp.broadcast_to(column(model * cell_scale), (ROWS, LANES))

    def body(n, sums_of):
        value = tile(cells, n)
        return (
            sums_of[0] + coef[0, pl.ds(n, 1), :] * value,
            sums_of[1] + coef[1, pl.ds(n, 1), :] * value,
        )

    start = (jnp.zeros((PLANES, LANES), F32), jnp.zeros((PLANES, LANES), F32))
    first, second = lax.fori_loop(0, ROWS, body, start, unroll=16)
    update[...] = first
    direction[...] = second

    for copy in copies:
        copy.wait()
    mask = window[...].astype(F32)
    size = math.sqrt(math.prod(observed.shape) * SIZES["xhi"] * SIZES["core"])
    near = pick(column(row * size), bins_ref[...], tensor_ref[...])
    for k in range(2):
        data[k] = (observed[k] * (scale * size) + near[k]) * mask


def chain(mine, other, stats, cells, observed, tensor, bins, window):
    field = jax.ShapeDtypeStruct((PLANES, LANES), F32)
    given = (observed, tensor, bins, window)
    return pl.pallas_call(
        chain_kernel,
        out_shape=(field, field, jax.ShapeDtypeStruct(observed.shape, F32)),
        in_specs=[vmem()] * 4 + [pl.BlockSpec(memory_space=pl.ANY)] * 4,
        out_specs=(vmem(),) * 3,
        scratch_shapes=[pltpu.VMEM((ROWS, ROWS), F32), pltpu.VMEM((2, ROWS, LANES), F32)]
        + [pltpu.VMEM(x.shape, x.dtype) for x in given]
        + [pltpu.SemaphoreType.DMA((4,))],
        compiler_params=pltpu.CompilerParams(vmem_limit_bytes=VMEM_LIMIT),
        name="chain",
    )(mine, other, stats, cells, *given)


def shift(value, axes, step):
    count = math.prod(SIZES[a] for a in axes)
    return lax.ppermute(value, axes, [(i, (i + step) % count) for i in range(count)])


def swap(value, axis):
    return lax.ppermute(value, axis, [(0, 1), (1, 0)])


def exchange(value, axes):
    return lax.all_to_all(value, axes, 0, 0, tiled=True)


def scatter_sum(value, axes):
    count = math.prod(SIZES[a] for a in axes)
    return jnp.sum(exchange(value.reshape(count, -1, LANES), axes), axis=0)


def whole_sum(value, axes):
    count = math.prod(SIZES[a] for a in axes)
    return jnp.sum(exchange(jnp.broadcast_to(value, (count,) + value.shape), axes), axis=0)


def gather(value, axes):
    count = math.prod(SIZES[a] for a in axes)
    return exchange(jnp.broadcast_to(value, (count,) + value.shape), axes).reshape(-1, LANES)


def per_device(
    source_field,
    receiver_tensor,
    metric_ids,
    metric_table,
    observed,
    receiver_index,
    bin_ids,
    window,
):
    src = source_field.reshape(FIELDS, PLANES, LANES)
    receiver = receiver_tensor.reshape(TENSORS, BINS, 12, PLANES, LANES)
    by_pairs = receiver_tensor.reshape(TENSORS, BINS, 3, 2, 2, PLANES, LANES)
    ids = metric_ids.reshape(PLANES, LANES)
    table = metric_table.T
    values = observed.transpose(0, 2, 1)
    tensor = receiver_index.reshape(1, -1)
    bins, marks = bin_ids.T, window.T
    src, x_lo, x_hi, y_lo, y_hi, to_core, to_cross, stats, scales = pack(
        src, ids, table, values, tensor, bins, marks
    )
    from_core = swap(to_core, "core")
    from_cross = lax.ppermute(to_cross, GZ, [(i, 3 - i) for i in range(4)])
    from_xhi = swap(stats, "xhi")
    xb, xa = shift(x_hi, GX, 1), shift(x_lo, GX, -1)
    yb, ya = shift(y_hi, GY, 1), shift(y_lo, GY, -1)

    flat = (FIELDS * 8, LANES)
    within = cells_within(
        scales,
        src.reshape(FIELDS * PLANES, LANES),
        (xb.reshape(flat), xa.reshape(flat), from_core, from_cross),
        receiver,
    )
    sums = (stats, from_core, from_cross, from_xhi)
    keep, send, cells, stats = gram(scales, (yb, ya), within, by_pairs, sums)
    packed = keep + swap(send, "core")
    packed = scatter_sum(packed, PLANE)
    packed = whole_sum(packed, ("z",))
    packed = gather(packed, PLANE)
    other = swap(packed, "core")
    update, direction, data = chain(packed, other, stats, cells, values, tensor, bins, marks)
    return (
        update.reshape(metric_ids.shape),
        direction.reshape(metric_ids.shape),
        data.transpose(0, 2, 1),
    )


def solution(mesh):
    fine = Mesh(mesh.devices.reshape([SIZES[a] for a in AXES]), AXES)
    return jax.shard_map(
        per_device,
        mesh=fine,
        in_specs=(
            P(None, None, None, GX, GY, GZ),
            P(None, None, None, None, GX, GY, GZ),
            P(GX, GY, GZ),
            P(),
            P(None, GZ, None),
            P(GZ),
            P(GZ, None),
            P(GZ, None),
        ),
        out_specs=(P(GX, GY, GZ), P(GX, GY, GZ), P(None, GZ, None)),
        check_vma=False,
    )
```

```python
import functools
import math

import jax
import jax.numpy as jnp
from jax import lax
from jax.experimental import pallas as pl
from jax.experimental.pallas import tpu as pltpu
from jax.sharding import Mesh, PartitionSpec as P

ITERS = 2
EPSILON = 1e-06
F32 = jnp.float32
BF16 = jnp.bfloat16

AXES = ("y", "z", "xlo", "xhi", "core")
SIZES = {"y": 4, "z": 8, "xlo": 2, "xhi": 2, "core": 2}
GX = ("y",)
GY = ("z", "xlo")
GZ = ("xhi", "core")
PLANE = ("y", "xlo", "xhi")
VMEM_LIMIT = 16 * 1024 * 1024

BINS = 16
TENSORS = 12
FIELDS = 96
PLANES = 16
LANES = 128
ROWS = 384
BLOCKS = ((0, 0), (0, 1), (0, 2), (1, 1), (1, 2), (2, 2))


def vmem():
    return pl.BlockSpec(memory_space=pltpu.VMEM)


def in_hbm(value):
    return pltpu.with_memory_space_constraint(value, pltpu.HBM)


def hbm():
    return pl.BlockSpec(memory_space=pltpu.HBM)


def lane_ids(shape):
    return lax.broadcasted_iota(jnp.int32, shape, len(shape) - 1)


def spread(values, bins, tensor):
    parts = []
    for b in range(BINS):
        here = bins == b
        for k in range(2):
            parts.append(jnp.sum(jnp.where(here, values[k], 0.0), axis=0, keepdims=True))
    table = jnp.concatenate(parts, axis=0)
    return jnp.concatenate(
        [
            jnp.sum(jnp.where(tensor == r, table, 0.0), axis=1, keepdims=True)
            for r in range(TENSORS)
        ],
        axis=0,
    )


def pick(column, bins, tensor):
    table = jnp.zeros((2 * BINS, bins.shape[1]), F32)
    for r in range(TENSORS):
        table = jnp.where(tensor == r, column[r * 32 : (r + 1) * 32, :], table)
    out = [jnp.zeros(bins.shape, F32), jnp.zeros(bins.shape, F32)]
    for b in range(BINS):
        here = bins == b
        for k in range(2):
            out[k] = jnp.where(here, table[2 * b + k : 2 * b + k + 1, :], out[k])
    return out


def data_sums(observed, tensor, bins, window):
    mask = window.astype(F32)
    rhs = [observed[k] * mask for k in range(2)]
    total = spread(rhs, bins, tensor)
    count = spread([mask, mask], bins, tensor)
    mean = total / jnp.maximum(count, 1.0)
    near = pick(mean, bins, tensor)
    rest = [rhs[k] - near[k] * mask for k in range(2)]
    square = jnp.sum(rest[0] * rest[0] + rest[1] * rest[1], axis=(0, 1), keepdims=True)
    lane = lane_ids((ROWS, LANES))
    wide = jnp.where(lane == 0, total, jnp.where(lane == 1, count, square))
    return jnp.concatenate([wide[j * LANES : (j + 1) * LANES, :].T[:8] for j in range(3)], axis=0)


def merge_sums(one, two):
    total, count = one[0:1] + two[0:1], one[1:2] + two[1:2]
    gap = one[0:1] / jnp.maximum(one[1:2], 1.0) - two[0:1] / jnp.maximum(two[1:2], 1.0)
    apart = jnp.sum(
        one[1:2] * two[1:2] / jnp.maximum(count, 1.0) * gap * gap, axis=1, keepdims=True
    )
    rest = one[2:3] + two[2:3] + apart
    return jnp.concatenate([total, count, rest, jnp.zeros((5, ROWS), F32)], axis=0)


def pack_kernel(
    src_in, ids_in, table_in, observed_in, tensor_in, bins_in, window_in,
    src, x_lo, x_hi, y_lo, y_hi, to_core, to_cross, stats, scales,
    ids, table, observed, tensor, bins, window, sems,
):
    copies = [
        pltpu.make_async_copy(here, there, sems.at[n])
        for n, (here, there) in enumerate(
            (
                (src_in, src),
                (ids_in, ids),
                (table_in, table),
                (observed_in, observed),
                (tensor_in, tensor),
                (bins_in, bins),
                (window_in, window),
            )
        )
    ]
    for copy in copies:
        copy.start()
    for copy in copies[1:]:
        copy.wait()
    for p in range(3):
        scale = jnp.zeros((PLANES, LANES), F32)
        for m in range(8):
            scale = jnp.where(ids[...] == m, table[p, m], scale)
        scales[p * PLANES : (p + 1) * PLANES, :] = scale * (1.0 / 12.0)
    sums = data_sums(observed, tensor[...], bins[...], window[...])
    stats[...] = sums
    to_core[FIELDS:, :] = sums
    to_cross[FIELDS:, :] = sums

    copies[0].wait()
    x_lo[...] = src[:, 0:8, :]
    x_hi[...] = src[:, 8:16, :]
    lane = lane_ids((FIELDS, LANES))
    low = jnp.zeros((FIELDS, LANES), F32)
    high = jnp.zeros((FIELDS, LANES), F32)
    for plane in range(PLANES):
        value = src[:, plane, :]
        x, y = divmod(plane, 4)
        if y < 2:
            y_lo[x * 2 + y] = value
        else:
            y_hi[x * 2 + y - 2] = value
        turned = pltpu.roll(value, 8 * plane, 1) if plane else value
        place = (lane - 8 * plane) & (LANES - 1)
        low = jnp.where(place < 2, turned, low)
        high = jnp.where(place >= LANES - 2, turned, high)
    upper = lax.axis_index("core") == 1
    to_core[:FIELDS, :] = jnp.where(upper, low, high)
    to_cross[:FIELDS, :] = jnp.where(upper, high, low)


def pack(src, ids, table, observed, tensor, bins, window):
    face = jax.ShapeDtypeStruct((FIELDS, 8, LANES), F32)
    side = jax.ShapeDtypeStruct((8, FIELDS, LANES), F32)
    ends = jax.ShapeDtypeStruct((FIELDS + 24, LANES), F32)
    given = (src, ids, table, observed, tensor, bins, window)
    return pl.pallas_call(
        pack_kernel,
        out_shape=(
            jax.ShapeDtypeStruct(src.shape, F32),
            face,
            face,
            side,
            side,
            ends,
            ends,
            jax.ShapeDtypeStruct((24, LANES), F32),
            jax.ShapeDtypeStruct((3 * PLANES, LANES), F32),
        ),
        in_specs=[hbm()] * 7,
        out_specs=(vmem(),) * 9,
        scratch_shapes=[pltpu.VMEM(ids.shape, ids.dtype), pltpu.SMEM(table.shape, table.dtype)]
        + [pltpu.VMEM(x.shape, x.dtype) for x in given[3:]]
        + [pltpu.SemaphoreType.DMA((7,))],
        compiler_params=pltpu.CompilerParams(vmem_limit_bytes=VMEM_LIMIT),
        name="pack",
    )(*(in_hbm(x) for x in given))


def ends_of(axes):
    at = lax.axis_index(axes)
    last = math.prod(SIZES[a] for a in axes) - 1
    return jnp.where(at > 0, 1.0, 0.0).astype(F32), jnp.where(at < last, 1.0, 0.0).astype(F32)


def tile(ref, at):
    return ref[pl.ds(pl.multiple_of(at * PLANES, PLANES), PLANES), :]


def set_tile(ref, at, value):
    ref[pl.ds(pl.multiple_of(at * PLANES, PLANES), PLANES), :] = value


def rows_of(start, strains, first):
    re, im = start
    for rec_re, rec_im, real, imag in strains:
        rec_re, rec_im = rec_re.astype(F32), rec_im.astype(F32)
        add_re, add_im = rec_re * real - rec_im * imag, rec_re * imag + rec_im * real
        re, im = (add_re, add_im) if first else (re + add_re, im + add_im)
        first = False
    return re, im


def cells_kernel(scales, src, xb, xa, from_core, from_cross, receiver, cells, grads, slots, sems):
    def fetch(b, slot):
        return pltpu.make_async_copy(receiver.at[:, b], slots.at[slot], sems.at[slot])

    fetch(0, 0).start()
    lane = lane_ids((FIELDS, LANES))
    x_before, x_after = ends_of(GX)
    crossing = jnp.where(lax.axis_index("xhi") != lax.axis_index("core"), 1.0, 0.0).astype(F32)
    halo = from_core[:FIELDS, :] + from_cross[:FIELDS, :] * crossing

    def at(x, y):
        if x < 0:
            return xb[pl.ds((x + 2) * 4 + y, FIELDS, stride=8), :] * x_before
        if x > 3:
            return xa[pl.ds((x - 4) * 4 + y, FIELDS, stride=8), :] * x_after
        if y < 0 or y > 3:
            return 0.0
        return src[pl.ds(x * 4 + y, FIELDS, stride=PLANES), :]

    def put(p, plane, value):
        grads[pl.ds(p * FIELDS * PLANES + plane, FIELDS, stride=PLANES), :] = value

    for x in range(4):
        for y in range(4):
            plane = x * 4 + y
            put(0, plane, 8.0 * (at(x + 1, y) - at(x - 1, y)) - (at(x + 2, y) - at(x - 2, y)))
            put(1, plane, 8.0 * (at(x, y + 1) - at(x, y - 1)) - (at(x, y + 2) - at(x, y - 2)))
            mid = at(x, y)
            ends = pltpu.roll(halo, LANES - 8 * plane, 1) if plane else halo
            later = pltpu.roll(jnp.where(lane < 1, ends, mid), LANES - 1, 1)
            sooner = pltpu.roll(jnp.where(lane >= LANES - 1, ends, mid), 1, 1)
            later_two = pltpu.roll(jnp.where(lane < 2, ends, mid), LANES - 2, 1)
            sooner_two = pltpu.roll(jnp.where(lane >= LANES - 2, ends, mid), 2, 1)
            put(2, plane, 8.0 * (later - sooner) - (later_two - sooner_two))

    def body(b, carry):
        slot = b & 1

        @pl.when(b + 1 < BINS)
        def _():
            fetch(b + 1, 1 - slot).start()

        def grad(p, q, k):
            return tile(scales, p) * tile(grads, p * FIELDS + b * 6 + q * 2 + k)

        real, imag = [
            (
                grad(0, 0, k),
                grad(1, 1, k),
                grad(2, 2, k),
                grad(1, 2, k) + grad(2, 1, k),
                grad(0, 2, k) + grad(2, 0, k),
                grad(0, 1, k) + grad(1, 0, k),
            )
            for k in range(2)
        ]
        fetch(b, slot).wait()
        for r in range(TENSORS):
            terms = [
                (slots[slot, r, 2 * j], slots[slot, r, 2 * j + 1], real[j], imag[j])
                for j in range(6)
            ]
            re, im = rows_of((None, None), terms, True)
            set_tile(cells, r * 32 + b * 2, re)
            set_tile(cells, r * 32 + b * 2 + 1, im)
        return carry

    lax.fori_loop(0, BINS, body, 0)


def whole(*shape):
    return pl.BlockSpec(shape, lambda b: (0,) * len(shape))


def cells_within(scales, src, halos, receiver):
    return pl.pallas_call(
        cells_kernel,
        out_shape=jax.ShapeDtypeStruct((ROWS * PLANES, LANES), F32),
        in_specs=[vmem()] * 6 + [hbm()],
        out_specs=vmem(),
        scratch_shapes=[
            pltpu.VMEM((3 * FIELDS * PLANES, LANES), F32),
            pltpu.VMEM((2, TENSORS, 12, PLANES, LANES), BF16),
            pltpu.SemaphoreType.DMA((2,)),
        ],
        compiler_params=pltpu.CompilerParams(vmem_limit_bytes=VMEM_LIMIT),
        cost_estimate=pl.CostEstimate(
            flops=20_000_000, bytes_accessed=14_000_000, transcendentals=0
        ),
        name="cells_within",
    )(scales, src, *halos, in_hbm(receiver))


def gram_kernel(
    scales, yb, ya, within, receiver, own, from_core, from_cross, from_xhi, keep, send, cells, stats, grads
):
    step = pl.program_id(0)

    @pl.when(step == 0)
    def _():
        before, after = ends_of(GY)
        for x in range(4):
            b_two, b_one = yb[x * 2] * before, yb[x * 2 + 1] * before
            a_one, a_two = ya[x * 2] * after, ya[x * 2 + 1] * after
            for y, value in enumerate(
                (b_two - 8.0 * b_one, b_one, -a_one, 8.0 * a_one - a_two)
            ):
                grads[pl.ds(x * 4 + y, FIELDS, stride=PLANES), :] = value

        def sums_of(value):
            return jnp.concatenate([value[8 * j : 8 * j + 8, :] for j in range(3)], axis=1)

        stats[...] = merge_sums(
            merge_sums(sums_of(own[...]), sums_of(from_core[FIELDS:, :])),
            merge_sums(sums_of(from_cross[FIELDS:, :]), sums_of(from_xhi[...])),
        )

    def grad(q, k):
        return tile(scales, 1) * tile(grads, step * 6 + q * 2 + k)

    real, imag = [(grad(1, k), grad(2, k), grad(0, k)) for k in range(2)]
    for r in range(TENSORS):
        at = r * 32 + step * 2
        terms = [
            (receiver[r, 0, j, 0, 0], receiver[r, 0, j, 0, 1], real[j], imag[j]) for j in range(3)
        ]
        re, im = rows_of((tile(within, at), tile(within, at + 1)), terms, False)
        set_tile(cells, at, re)
        set_tile(cells, at + 1, im)

    @pl.when(step == BINS - 1)
    def _():
        total = jnp.zeros((ROWS, ROWS), F32)
        for plane in range(0, PLANES, 2):
            both = jnp.concatenate(
                [cells[pl.ds(plane + i, ROWS, stride=PLANES), :] for i in range(2)], axis=1
            )
            high = both.astype(BF16)
            low = (both - high.astype(F32)).astype(BF16)
            left = jnp.concatenate([high, high], axis=1)
            right = jnp.concatenate([high * BF16(0.5), low], axis=1)
            total = total + lax.dot_general(
                left, right, (((1,), (1,)), ((), ())), preferred_element_type=F32
            )

        def block(i, j):
            return total[i * LANES : (i + 1) * LANES, j * LANES : (j + 1) * LANES]

        full = [block(i, j) + block(j, i).T for i, j in BLOCKS]
        upper = lax.axis_index("core") == 1
        for n in range(3):
            part = slice(n * LANES, (n + 1) * LANES)
            keep[part, :] = jnp.where(upper, full[n + 3], full[n])
            send[part, :] = jnp.where(upper, full[n], full[n + 3])


def gram(scales, halos, within, receiver, sums):
    side = whole(8, FIELDS, LANES)
    half = jax.ShapeDtypeStruct((3 * LANES, LANES), F32)
    return pl.pallas_call(
        gram_kernel,
        grid=(BINS,),
        out_shape=(
            half,
            half,
            jax.ShapeDtypeStruct((ROWS * PLANES, LANES), F32),
            jax.ShapeDtypeStruct((8, ROWS), F32),
        ),
        in_specs=[
            whole(3 * PLANES, LANES),
            side,
            side,
            whole(ROWS * PLANES, LANES),
            pl.BlockSpec(
                (TENSORS, 1, 3, 1, 2, PLANES, LANES), lambda b: (0, b, 0, 1, 0, 0, 0)
            ),
        ]
        + [whole(24, LANES), whole(120, LANES), whole(120, LANES), whole(24, LANES)],
        out_specs=(
            whole(3 * LANES, LANES),
            whole(3 * LANES, LANES),
            whole(ROWS * PLANES, LANES),
            whole(8, ROWS),
        ),
        scratch_shapes=[pltpu.VMEM((FIELDS * PLANES, LANES), F32)],
        compiler_params=pltpu.CompilerParams(vmem_limit_bytes=VMEM_LIMIT),
        cost_estimate=pl.CostEstimate(
            flops=1_200_000_000, bytes_accessed=8_000_000, transcendentals=0
        ),
        name="gram",
    )(scales, *halos, within, receiver, *sums)


def chain_kernel(
    mine, other, stats, cells, observed_in, tensor_in, bins_in, window_in, update, direction, data,
    full, coef, observed, tensor_ref, bins_ref, window, sems
):
    copies = [
        pltpu.make_async_copy(here, there, sems.at[n])
        for n, (here, there) in enumerate(
            (
                (observed_in, observed),
                (tensor_in, tensor_ref),
                (bins_in, bins_ref),
                (window_in, window),
            )
        )
    ]
    for copy in copies:
        copy.start()
    upper = lax.axis_index("core") == 1
    for n, (i, j) in enumerate(BLOCKS):
        part = slice(n % 3 * LANES, (n % 3 + 1) * LANES)
        near, far = mine[part, :], other[part, :]
        block = jnp.where(upper, far, near) if n < 3 else jnp.where(upper, near, far)
        full[i * LANES : (i + 1) * LANES, j * LANES : (j + 1) * LANES] = block
        if i != j:
            full[j * LANES : (j + 1) * LANES, i * LANES : (i + 1) * LANES] = block.T
    eye = lax.broadcasted_iota(jnp.int32, (LANES, LANES), 0) == lane_ids((LANES, LANES))

    def column(row):
        return jnp.concatenate(
            [
                jnp.sum(
                    jnp.where(eye, row[:, j * LANES : (j + 1) * LANES], 0.0), axis=1, keepdims=True
                )
                for j in range(3)
            ],
            axis=0,
        )

    def product(row):
        return jnp.sum(full[...] * column(row), axis=0, keepdims=True)

    def total(row):
        return jnp.sum(row, axis=1, keepdims=True)

    def norm_of(square):
        return jnp.sqrt(square + EPSILON)

    sums, count, rest = stats[0:1, :], stats[1:2, :], stats[2:3, 0:1]
    mean = sums / jnp.maximum(count, 1.0)

    def data_norm(scale, row):
        inside = scale * mean + row
        return norm_of(scale * scale * rest + total(count * inside * inside))

    one = jnp.ones((1, 1), F32)
    row = jnp.zeros((1, ROWS), F32)
    beta = data_norm(one, row)
    beta_first = beta
    scale = one / beta
    raw = scale * sums
    image = product(raw)
    alpha = norm_of(total(raw * image))
    alpha_first = alpha
    model = raw / alpha
    search = model
    answer = jnp.zeros((1, ROWS), F32)
    phi_bar, rho_bar = beta, alpha
    for _ in range(ITERS):
        scale, row = -alpha * scale, image / alpha - alpha * row
        beta = data_norm(scale, row)
        scale, row = scale / beta, row / beta
        raw = scale * sums + count * row - beta * model
        image = product(raw)
        alpha = norm_of(total(raw * image))
        model = raw / alpha
        rho = jnp.sqrt(rho_bar * rho_bar + beta * beta)
        cosine, sine = rho_bar / rho, beta / rho
        theta = sine * alpha
        rho_bar = -cosine * alpha
        phi = cosine * phi_bar
        phi_bar = sine * phi_bar
        answer = answer + phi / rho * search
        search = model - theta / rho * search
    cell_scale = math.sqrt(PLANES * LANES * math.prod(SIZES.values()))
    coef[0] = jnp.broadcast_to(
        column(answer * (alpha_first * cell_scale / beta_first)), (ROWS, LANES)
    )
    coef[1] = jnp.broadcast_to(column(model * cell_scale), (ROWS, LANES))

    def body(n, sums_of):
        value = tile(cells, n)
        return (
            sums_of[0] + coef[0, pl.ds(n, 1), :] * value,
            sums_of[1] + coef[1, pl.ds(n, 1), :] * value,
        )

    start = (jnp.zeros((PLANES, LANES), F32), jnp.zeros((PLANES, LANES), F32))
    first, second = lax.fori_loop(0, ROWS, body, start, unroll=16)
    update[...] = first
    direction[...] = second

    for copy in copies:
        copy.wait()
    mask = window[...].astype(F32)
    size = math.sqrt(math.prod(observed.shape) * SIZES["xhi"] * SIZES["core"])
    near = pick(column(row * size), bins_ref[...], tensor_ref[...])
    for k in range(2):
        data[k] = (observed[k] * (scale * size) + near[k]) * mask


def chain(mine, other, stats, cells, observed, tensor, bins, window):
    field = jax.ShapeDtypeStruct((PLANES, LANES), F32)
    given = (observed, tensor, bins, window)
    return pl.pallas_call(
        chain_kernel,
        out_shape=(field, field, jax.ShapeDtypeStruct(observed.shape, F32)),
        in_specs=[vmem()] * 4 + [pl.BlockSpec(memory_space=pl.ANY)] * 4,
        out_specs=(vmem(),) * 3,
        scratch_shapes=[pltpu.VMEM((ROWS, ROWS), F32), pltpu.VMEM((2, ROWS, LANES), F32)]
        + [pltpu.VMEM(x.shape, x.dtype) for x in given]
        + [pltpu.SemaphoreType.DMA((4,))],
        compiler_params=pltpu.CompilerParams(vmem_limit_bytes=VMEM_LIMIT),
        name="chain",
    )(mine, other, stats, cells, *given)


def shift(value, axes, step):
    count = math.prod(SIZES[a] for a in axes)
    return lax.ppermute(value, axes, [(i, (i + step) % count) for i in range(count)])


def swap(value, axis):
    return lax.ppermute(value, axis, [(0, 1), (1, 0)])


def exchange(value, axes):
    return lax.all_to_all(value, axes, 0, 0, tiled=True)


def scatter_sum(value, axes):
    count = math.prod(SIZES[a] for a in axes)
    return jnp.sum(exchange(value.reshape(count, -1, LANES), axes), axis=0)


def whole_sum(value, axes):
    count = math.prod(SIZES[a] for a in axes)
    return jnp.sum(exchange(jnp.broadcast_to(value, (count,) + value.shape), axes), axis=0)


def gather(value, axes):
    count = math.prod(SIZES[a] for a in axes)
    return exchange(jnp.broadcast_to(value, (count,) + value.shape), axes).reshape(-1, LANES)


def per_device(
    source_field,
    receiver_tensor,
    metric_ids,
    metric_table,
    observed,
    receiver_index,
    bin_ids,
    window,
):
    src = source_field.reshape(FIELDS, PLANES, LANES)
    receiver = receiver_tensor.reshape(TENSORS, BINS, 12, PLANES, LANES)
    by_pairs = receiver_tensor.reshape(TENSORS, BINS, 3, 2, 2, PLANES, LANES)
    ids = metric_ids.reshape(PLANES, LANES)
    table = metric_table.T
    values = observed.transpose(0, 2, 1)
    tensor = receiver_index.reshape(1, -1)
    bins, marks = bin_ids.T, window.T
    src, x_lo, x_hi, y_lo, y_hi, to_core, to_cross, stats, scales = pack(
        src, ids, table, values, tensor, bins, marks
    )
    from_core = swap(to_core, "core")
    from_cross = lax.ppermute(to_cross, GZ, [(i, 3 - i) for i in range(4)])
    from_xhi = swap(stats, "xhi")
    xb, xa = shift(x_hi, GX, 1), shift(x_lo, GX, -1)
    yb, ya = shift(y_hi, GY, 1), shift(y_lo, GY, -1)

    flat = (FIELDS * 8, LANES)
    within = cells_within(
        scales,
        src.reshape(FIELDS * PLANES, LANES),
        (xb.reshape(flat), xa.reshape(flat), from_core, from_cross),
        receiver,
    )
    sums = (stats, from_core, from_cross, from_xhi)
    keep, send, cells, stats = gram(scales, (yb, ya), within, by_pairs, sums)
    packed = keep + swap(send, "core")
    packed = scatter_sum(packed, PLANE)
    packed = whole_sum(packed, ("z",))
    packed = gather(packed, PLANE)
    other = swap(packed, "core")
    update, direction, data = chain(packed, other, stats, cells, values, tensor, bins, marks)
    return (
        update.reshape(metric_ids.shape),
        direction.reshape(metric_ids.shape),
        data.transpose(0, 2, 1),
    )


def solution(mesh):
    fine = Mesh(mesh.devices.reshape([SIZES[a] for a in AXES]), AXES)
    return jax.shard_map(
        per_device,
        mesh=fine,
        in_specs=(
            P(None, None, None, GX, GY, GZ),
            P(None, None, None, None, GX, GY, GZ),
            P(GX, GY, GZ),
            P(),
            P(None, GZ, None),
            P(GZ),
            P(GZ, None),
            P(GZ, None),
        ),
        out_specs=(P(GX, GY, GZ), P(GX, GY, GZ), P(None, GZ, None)),
        check_vma=False,
    )
```

```python
import functools
import math

import jax
import jax.numpy as jnp
from jax import lax
from jax.experimental import pallas as pl
from jax.experimental.pallas import tpu as pltpu
from jax.sharding import Mesh, PartitionSpec as P

ITERS = 2
EPSILON = 1e-06
F32 = jnp.float32
BF16 = jnp.bfloat16

AXES = ("y", "z", "xlo", "xhi", "core")
SIZES = {"y": 4, "z": 8, "xlo": 2, "xhi": 2, "core": 2}
GX = ("y",)
GY = ("z", "xlo")
GZ = ("xhi", "core")
PLANE = ("y", "xlo", "xhi")
VMEM_LIMIT = 16 * 1024 * 1024

BINS = 16
TENSORS = 12
FIELDS = 96
PLANES = 16
LANES = 128
ROWS = 384
BLOCKS = ((0, 0), (0, 1), (0, 2), (1, 1), (1, 2), (2, 2))


def vmem():
    return pl.BlockSpec(memory_space=pltpu.VMEM)


def in_hbm(value):
    return pltpu.with_memory_space_constraint(value, pltpu.HBM)


def hbm():
    return pl.BlockSpec(memory_space=pltpu.HBM)


def lane_ids(shape):
    return lax.broadcasted_iota(jnp.int32, shape, len(shape) - 1)


def spread(values, bins, tensor):
    parts = []
    for b in range(BINS):
        here = bins == b
        for k in range(2):
            parts.append(jnp.sum(jnp.where(here, values[k], 0.0), axis=0, keepdims=True))
    table = jnp.concatenate(parts, axis=0)
    return jnp.concatenate(
        [
            jnp.sum(jnp.where(tensor == r, table, 0.0), axis=1, keepdims=True)
            for r in range(TENSORS)
        ],
        axis=0,
    )


def pick(column, bins, tensor):
    table = jnp.zeros((2 * BINS, bins.shape[1]), F32)
    for r in range(TENSORS):
        table = jnp.where(tensor == r, column[r * 32 : (r + 1) * 32, :], table)
    out = [jnp.zeros(bins.shape, F32), jnp.zeros(bins.shape, F32)]
    for b in range(BINS):
        here = bins == b
        for k in range(2):
            out[k] = jnp.where(here, table[2 * b + k : 2 * b + k + 1, :], out[k])
    return out


def data_sums(observed, tensor, bins, window):
    mask = window.astype(F32)
    rhs = [observed[k] * mask for k in range(2)]
    total = spread(rhs, bins, tensor)
    count = spread([mask, mask], bins, tensor)
    mean = total / jnp.maximum(count, 1.0)
    near = pick(mean, bins, tensor)
    rest = [rhs[k] - near[k] * mask for k in range(2)]
    square = jnp.sum(rest[0] * rest[0] + rest[1] * rest[1], axis=(0, 1), keepdims=True)
    lane = lane_ids((ROWS, LANES))
    wide = jnp.where(lane == 0, total, jnp.where(lane == 1, count, square))
    return jnp.concatenate([wide[j * LANES : (j + 1) * LANES, :].T[:8] for j in range(3)], axis=0)


def merge_sums(one, two):
    total, count = one[0:1] + two[0:1], one[1:2] + two[1:2]
    gap = one[0:1] / jnp.maximum(one[1:2], 1.0) - two[0:1] / jnp.maximum(two[1:2], 1.0)
    apart = jnp.sum(
        one[1:2] * two[1:2] / jnp.maximum(count, 1.0) * gap * gap, axis=1, keepdims=True
    )
    rest = one[2:3] + two[2:3] + apart
    return jnp.concatenate([total, count, rest, jnp.zeros((5, ROWS), F32)], axis=0)


def pack_kernel(
    src_in, ids_in, table_in, observed_in, tensor_in, bins_in, window_in,
    src, x_lo, x_hi, to_core, to_cross, stats, scales,
    ids, table, observed, tensor, bins, window, sems,
):
    copies = [
        pltpu.make_async_copy(here, there, sems.at[n])
        for n, (here, there) in enumerate(
            (
                (src_in, src),
                (ids_in, ids),
                (table_in, table),
                (observed_in, observed),
                (tensor_in, tensor),
                (bins_in, bins),
                (window_in, window),
            )
        )
    ]
    for copy in copies:
        copy.start()
    for copy in copies[1:]:
        copy.wait()
    for p in range(3):
        scale = jnp.zeros((PLANES, LANES), F32)
        for m in range(8):
            scale = jnp.where(ids[...] == m, table[p, m], scale)
        scales[p * PLANES : (p + 1) * PLANES, :] = scale * (1.0 / 12.0)
    sums = data_sums(observed, tensor[...], bins[...], window[...])
    stats[...] = sums
    to_core[FIELDS:, :] = sums
    to_cross[FIELDS:, :] = sums

    copies[0].wait()
    x_lo[...] = src[:, 0:8, :]
    x_hi[...] = src[:, 8:16, :]
    lane = lane_ids((FIELDS, LANES))
    low = jnp.zeros((FIELDS, LANES), F32)
    high = jnp.zeros((FIELDS, LANES), F32)
    for plane in range(PLANES):
        value = src[:, plane, :]
        turned = pltpu.roll(value, 8 * plane, 1) if plane else value
        place = (lane - 8 * plane) & (LANES - 1)
        low = jnp.where(place < 2, turned, low)
        high = jnp.where(place >= LANES - 2, turned, high)
    upper = lax.axis_index("core") == 1
    to_core[:FIELDS, :] = jnp.where(upper, low, high)
    to_cross[:FIELDS, :] = jnp.where(upper, high, low)


def sides_kernel(src, arrived, y_lo, y_hi):
    for plane in range(PLANES):
        x, y = divmod(plane, 4)
        if y < 2:
            y_lo[x * 2 + y] = src[:, plane, :]
        else:
            y_hi[x * 2 + y - 2] = src[:, plane, :]


def sides(src, arrived):
    side = jax.ShapeDtypeStruct((8, FIELDS, LANES), F32)
    return pl.pallas_call(
        sides_kernel,
        out_shape=(side, side),
        in_specs=[vmem(), vmem()],
        out_specs=(vmem(), vmem()),
        compiler_params=pltpu.CompilerParams(vmem_limit_bytes=VMEM_LIMIT),
        name="sides",
    )(src, arrived)


def pack(src, ids, table, observed, tensor, bins, window):
    face = jax.ShapeDtypeStruct((FIELDS, 8, LANES), F32)
    ends = jax.ShapeDtypeStruct((FIELDS + 24, LANES), F32)
    given = (src, ids, table, observed, tensor, bins, window)
    return pl.pallas_call(
        pack_kernel,
        out_shape=(
            jax.ShapeDtypeStruct(src.shape, F32),
            face,
            face,
            ends,
            ends,
            jax.ShapeDtypeStruct((24, LANES), F32),
            jax.ShapeDtypeStruct((3 * PLANES, LANES), F32),
        ),
        in_specs=[hbm()] * 7,
        out_specs=(vmem(),) * 7,
        scratch_shapes=[pltpu.VMEM(ids.shape, ids.dtype), pltpu.SMEM(table.shape, table.dtype)]
        + [pltpu.VMEM(x.shape, x.dtype) for x in given[3:]]
        + [pltpu.SemaphoreType.DMA((7,))],
        compiler_params=pltpu.CompilerParams(vmem_limit_bytes=VMEM_LIMIT),
        name="pack",
    )(*(in_hbm(x) for x in given))


def ends_of(axes):
    at = lax.axis_index(axes)
    last = math.prod(SIZES[a] for a in axes) - 1
    return jnp.where(at > 0, 1.0, 0.0).astype(F32), jnp.where(at < last, 1.0, 0.0).astype(F32)


def tile(ref, at):
    return ref[pl.ds(pl.multiple_of(at * PLANES, PLANES), PLANES), :]


def set_tile(ref, at, value):
    ref[pl.ds(pl.multiple_of(at * PLANES, PLANES), PLANES), :] = value


def rows_of(start, strains, first):
    re, im = start
    for rec_re, rec_im, real, imag in strains:
        rec_re, rec_im = rec_re.astype(F32), rec_im.astype(F32)
        add_re, add_im = rec_re * real - rec_im * imag, rec_re * imag + rec_im * real
        re, im = (add_re, add_im) if first else (re + add_re, im + add_im)
        first = False
    return re, im


def cells_kernel(scales, src, xb, xa, from_core, from_cross, receiver_in, cells, receiver, grads, sems):
    def fetch(b):
        return pltpu.make_async_copy(receiver_in.at[:, b], receiver.at[:, b], sems.at[b])

    for b in range(BINS):
        fetch(b).start()
    lane = lane_ids((FIELDS, LANES))
    x_before, x_after = ends_of(GX)
    crossing = jnp.where(lax.axis_index("xhi") != lax.axis_index("core"), 1.0, 0.0).astype(F32)
    halo = from_core[:FIELDS, :] + from_cross[:FIELDS, :] * crossing

    def at(x, y):
        if x < 0:
            return xb[pl.ds((x + 2) * 4 + y, FIELDS, stride=8), :] * x_before
        if x > 3:
            return xa[pl.ds((x - 4) * 4 + y, FIELDS, stride=8), :] * x_after
        if y < 0 or y > 3:
            return 0.0
        return src[pl.ds(x * 4 + y, FIELDS, stride=PLANES), :]

    def put(p, plane, value):
        grads[pl.ds(p * FIELDS * PLANES + plane, FIELDS, stride=PLANES), :] = value

    for x in range(4):
        for y in range(4):
            plane = x * 4 + y
            put(0, plane, 8.0 * (at(x + 1, y) - at(x - 1, y)) - (at(x + 2, y) - at(x - 2, y)))
            put(1, plane, 8.0 * (at(x, y + 1) - at(x, y - 1)) - (at(x, y + 2) - at(x, y - 2)))
            mid = at(x, y)
            ends = pltpu.roll(halo, LANES - 8 * plane, 1) if plane else halo
            later = pltpu.roll(jnp.where(lane < 1, ends, mid), LANES - 1, 1)
            sooner = pltpu.roll(jnp.where(lane >= LANES - 1, ends, mid), 1, 1)
            later_two = pltpu.roll(jnp.where(lane < 2, ends, mid), LANES - 2, 1)
            sooner_two = pltpu.roll(jnp.where(lane >= LANES - 2, ends, mid), 2, 1)
            put(2, plane, 8.0 * (later - sooner) - (later_two - sooner_two))

    def body(b, carry):
        def grad(p, q, k):
            return tile(scales, p) * tile(grads, p * FIELDS + b * 6 + q * 2 + k)

        real, imag = [
            (
                grad(0, 0, k),
                grad(1, 1, k),
                grad(2, 2, k),
                grad(1, 2, k) + grad(2, 1, k),
                grad(0, 2, k) + grad(2, 0, k),
                grad(0, 1, k) + grad(1, 0, k),
            )
            for k in range(2)
        ]
        fetch(b).wait()
        for r in range(TENSORS):
            terms = [
                (receiver[r, b, 2 * j], receiver[r, b, 2 * j + 1], real[j], imag[j])
                for j in range(6)
            ]
            re, im = rows_of((None, None), terms, True)
            set_tile(cells, r * 32 + b * 2, re)
            set_tile(cells, r * 32 + b * 2 + 1, im)
        return carry

    lax.fori_loop(0, BINS, body, 0)


def cells_within(scales, src, halos, receiver):
    return pl.pallas_call(
        cells_kernel,
        out_shape=(
            jax.ShapeDtypeStruct((ROWS * PLANES, LANES), F32),
            jax.ShapeDtypeStruct(receiver.shape, receiver.dtype),
        ),
        in_specs=[vmem()] * 6 + [hbm()],
        out_specs=(vmem(), vmem()),
        scratch_shapes=[
            pltpu.VMEM((3 * FIELDS * PLANES, LANES), F32),
            pltpu.SemaphoreType.DMA((BINS,)),
        ],
        compiler_params=pltpu.CompilerParams(vmem_limit_bytes=VMEM_LIMIT),
        cost_estimate=pl.CostEstimate(
            flops=20_000_000, bytes_accessed=14_000_000, transcendentals=0
        ),
        name="cells_within",
    )(scales, src, *halos, in_hbm(receiver))


def gram_kernel(
    scales, yb, ya, within, receiver, own, from_core, from_cross, from_xhi, keep, send, cells, stats, grads
):
    before, after = ends_of(GY)
    for x in range(4):
        b_two, b_one = yb[x * 2] * before, yb[x * 2 + 1] * before
        a_one, a_two = ya[x * 2] * after, ya[x * 2 + 1] * after
        for y, value in enumerate((b_two - 8.0 * b_one, b_one, -a_one, 8.0 * a_one - a_two)):
            grads[pl.ds(x * 4 + y, FIELDS, stride=PLANES), :] = value

    def body(b, carry):
        def grad(q, k):
            return tile(scales, 1) * tile(grads, b * 6 + q * 2 + k)

        real, imag = [(grad(1, k), grad(2, k), grad(0, k)) for k in range(2)]
        for r in range(TENSORS):
            at = r * 32 + b * 2
            terms = [
                (receiver[r, b, 4 * j + 2], receiver[r, b, 4 * j + 3], real[j], imag[j])
                for j in range(3)
            ]
            re, im = rows_of((tile(within, at), tile(within, at + 1)), terms, False)
            set_tile(cells, at, re)
            set_tile(cells, at + 1, im)
        return carry

    lax.fori_loop(0, BINS, body, 0)

    total = jnp.zeros((ROWS, ROWS), F32)
    for plane in range(0, PLANES, 2):
        both = jnp.concatenate(
            [cells[pl.ds(plane + i, ROWS, stride=PLANES), :] for i in range(2)], axis=1
        )
        high = both.astype(BF16)
        low = (both - high.astype(F32)).astype(BF16)
        left = jnp.concatenate([high, high], axis=1)
        right = jnp.concatenate([high * BF16(0.5), low], axis=1)
        total = total + lax.dot_general(
            left, right, (((1,), (1,)), ((), ())), preferred_element_type=F32
        )

    def block(i, j):
        return total[i * LANES : (i + 1) * LANES, j * LANES : (j + 1) * LANES]

    full = [block(i, j) + block(j, i).T for i, j in BLOCKS]
    upper = lax.axis_index("core") == 1
    for n in range(3):
        part = slice(n * LANES, (n + 1) * LANES)
        keep[part, :] = jnp.where(upper, full[n + 3], full[n])
        send[part, :] = jnp.where(upper, full[n], full[n + 3])

    def sums_of(value):
        return jnp.concatenate([value[8 * j : 8 * j + 8, :] for j in range(3)], axis=1)

    stats[...] = merge_sums(
        merge_sums(sums_of(own[...]), sums_of(from_core[FIELDS:, :])),
        merge_sums(sums_of(from_cross[FIELDS:, :]), sums_of(from_xhi[...])),
    )


def gram(scales, halos, within, receiver, sums):
    half = jax.ShapeDtypeStruct((3 * LANES, LANES), F32)
    return pl.pallas_call(
        gram_kernel,
        out_shape=(
            half,
            half,
            jax.ShapeDtypeStruct((ROWS * PLANES, LANES), F32),
            jax.ShapeDtypeStruct((8, ROWS), F32),
        ),
        in_specs=[vmem()] * 9,
        out_specs=(vmem(),) * 4,
        scratch_shapes=[pltpu.VMEM((FIELDS * PLANES, LANES), F32)],
        compiler_params=pltpu.CompilerParams(vmem_limit_bytes=VMEM_LIMIT),
        cost_estimate=pl.CostEstimate(
            flops=1_200_000_000, bytes_accessed=8_000_000, transcendentals=0
        ),
        name="gram",
    )(scales, *halos, within, receiver, *sums)


def chain_kernel(
    mine, other, stats, cells, observed_in, tensor_in, bins_in, window_in, update, direction, data,
    full, coef, observed, tensor_ref, bins_ref, window, sems
):
    copies = [
        pltpu.make_async_copy(here, there, sems.at[n])
        for n, (here, there) in enumerate(
            (
                (observed_in, observed),
                (tensor_in, tensor_ref),
                (bins_in, bins_ref),
                (window_in, window),
            )
        )
    ]
    for copy in copies:
        copy.start()
    upper = lax.axis_index("core") == 1
    for n, (i, j) in enumerate(BLOCKS):
        part = slice(n % 3 * LANES, (n % 3 + 1) * LANES)
        near, far = mine[part, :], other[part, :]
        block = jnp.where(upper, far, near) if n < 3 else jnp.where(upper, near, far)
        full[i * LANES : (i + 1) * LANES, j * LANES : (j + 1) * LANES] = block
        if i != j:
            full[j * LANES : (j + 1) * LANES, i * LANES : (i + 1) * LANES] = block.T
    eye = lax.broadcasted_iota(jnp.int32, (LANES, LANES), 0) == lane_ids((LANES, LANES))

    def column(row):
        return jnp.concatenate(
            [
                jnp.sum(
                    jnp.where(eye, row[:, j * LANES : (j + 1) * LANES], 0.0), axis=1, keepdims=True
                )
                for j in range(3)
            ],
            axis=0,
        )

    def product(row):
        return jnp.sum(full[...] * column(row), axis=0, keepdims=True)

    def total(row):
        return jnp.sum(row, axis=1, keepdims=True)

    def norm_of(square):
        return jnp.sqrt(square + EPSILON)

    sums, count, rest = stats[0:1, :], stats[1:2, :], stats[2:3, 0:1]
    mean = sums / jnp.maximum(count, 1.0)

    def data_norm(scale, row):
        inside = scale * mean + row
        return norm_of(scale * scale * rest + total(count * inside * inside))

    one = jnp.ones((1, 1), F32)
    row = jnp.zeros((1, ROWS), F32)
    beta = data_norm(one, row)
    beta_first = beta
    scale = one / beta
    raw = scale * sums
    image = product(raw)
    alpha = norm_of(total(raw * image))
    alpha_first = alpha
    model = raw / alpha
    search = model
    answer = jnp.zeros((1, ROWS), F32)
    phi_bar, rho_bar = beta, alpha
    for _ in range(ITERS):
        scale, row = -alpha * scale, image / alpha - alpha * row
        beta = data_norm(scale, row)
        scale, row = scale / beta, row / beta
        raw = scale * sums + count * row - beta * model
        image = product(raw)
        alpha = norm_of(total(raw * image))
        model = raw / alpha
        rho = jnp.sqrt(rho_bar * rho_bar + beta * beta)
        cosine, sine = rho_bar / rho, beta / rho
        theta = sine * alpha
        rho_bar = -cosine * alpha
        phi = cosine * phi_bar
        phi_bar = sine * phi_bar
        answer = answer + phi / rho * search
        search = model - theta / rho * search
    cell_scale = math.sqrt(PLANES * LANES * math.prod(SIZES.values()))
    coef[0] = jnp.broadcast_to(
        column(answer * (alpha_first * cell_scale / beta_first)), (ROWS, LANES)
    )
    coef[1] = jnp.broadcast_to(column(model * cell_scale), (ROWS, LANES))

    def body(n, sums_of):
        value = tile(cells, n)
        return (
            sums_of[0] + coef[0, pl.ds(n, 1), :] * value,
            sums_of[1] + coef[1, pl.ds(n, 1), :] * value,
        )

    start = (jnp.zeros((PLANES, LANES), F32), jnp.zeros((PLANES, LANES), F32))
    first, second = lax.fori_loop(0, ROWS, body, start, unroll=16)
    update[...] = first
    direction[...] = second

    for copy in copies:
        copy.wait()
    mask = window[...].astype(F32)
    size = math.sqrt(math.prod(observed.shape) * SIZES["xhi"] * SIZES["core"])
    near = pick(column(row * size), bins_ref[...], tensor_ref[...])
    for k in range(2):
        data[k] = (observed[k] * (scale * size) + near[k]) * mask


def chain(mine, other, stats, cells, observed, tensor, bins, window):
    field = jax.ShapeDtypeStruct((PLANES, LANES), F32)
    given = (observed, tensor, bins, window)
    return pl.pallas_call(
        chain_kernel,
        out_shape=(field, field, jax.ShapeDtypeStruct(observed.shape, F32)),
        in_specs=[vmem()] * 4 + [pl.BlockSpec(memory_space=pl.ANY)] * 4,
        out_specs=(vmem(),) * 3,
        scratch_shapes=[pltpu.VMEM((ROWS, ROWS), F32), pltpu.VMEM((2, ROWS, LANES), F32)]
        + [pltpu.VMEM(x.shape, x.dtype) for x in given]
        + [pltpu.SemaphoreType.DMA((4,))],
        compiler_params=pltpu.CompilerParams(vmem_limit_bytes=VMEM_LIMIT),
        name="chain",
    )(mine, other, stats, cells, *given)


def shift(value, axes, step):
    count = math.prod(SIZES[a] for a in axes)
    return lax.ppermute(value, axes, [(i, (i + step) % count) for i in range(count)])


def swap(value, axis):
    return lax.ppermute(value, axis, [(0, 1), (1, 0)])


def exchange(value, axes):
    return lax.all_to_all(value, axes, 0, 0, tiled=True)


def scatter_sum(value, axes):
    count = math.prod(SIZES[a] for a in axes)
    return jnp.sum(exchange(value.reshape(count, -1, LANES), axes), axis=0)


def whole_sum(value, axes):
    count = math.prod(SIZES[a] for a in axes)
    return jnp.sum(exchange(jnp.broadcast_to(value, (count,) + value.shape), axes), axis=0)


def gather(value, axes):
    count = math.prod(SIZES[a] for a in axes)
    return exchange(jnp.broadcast_to(value, (count,) + value.shape), axes).reshape(-1, LANES)


def per_device(
    source_field,
    receiver_tensor,
    metric_ids,
    metric_table,
    observed,
    receiver_index,
    bin_ids,
    window,
):
    src = source_field.reshape(FIELDS, PLANES, LANES)
    receiver = receiver_tensor.reshape(TENSORS, BINS, 12, PLANES, LANES)
    ids = metric_ids.reshape(PLANES, LANES)
    table = metric_table.T
    values = observed.transpose(0, 2, 1)
    tensor = receiver_index.reshape(1, -1)
    bins, marks = bin_ids.T, window.T
    src, x_lo, x_hi, to_core, to_cross, stats, scales = pack(
        src, ids, table, values, tensor, bins, marks
    )
    from_core = swap(to_core, "core")
    from_cross = lax.ppermute(to_cross, GZ, [(i, 3 - i) for i in range(4)])
    from_xhi = swap(stats, "xhi")
    xb, xa = shift(x_hi, GX, 1), shift(x_lo, GX, -1)
    y_lo, y_hi = sides(src, from_cross)
    yb, ya = shift(y_hi, GY, 1), shift(y_lo, GY, -1)

    flat = (FIELDS * 8, LANES)
    within, receiver = cells_within(
        scales,
        src.reshape(FIELDS * PLANES, LANES),
        (xb.reshape(flat), xa.reshape(flat), from_core, from_cross),
        receiver,
    )
    sums = (stats, from_core, from_cross, from_xhi)
    keep, send, cells, stats = gram(scales, (yb, ya), within, receiver, sums)
    packed = keep + swap(send, "core")
    packed = scatter_sum(packed, PLANE)
    packed = whole_sum(packed, ("z",))
    packed = gather(packed, PLANE)
    other = swap(packed, "core")
    update, direction, data = chain(packed, other, stats, cells, values, tensor, bins, marks)
    return (
        update.reshape(metric_ids.shape),
        direction.reshape(metric_ids.shape),
        data.transpose(0, 2, 1),
    )


def solution(mesh):
    fine = Mesh(mesh.devices.reshape([SIZES[a] for a in AXES]), AXES)
    return jax.shard_map(
        per_device,
        mesh=fine,
        in_specs=(
            P(None, None, None, GX, GY, GZ),
            P(None, None, None, None, GX, GY, GZ),
            P(GX, GY, GZ),
            P(),
            P(None, GZ, None),
            P(GZ),
            P(GZ, None),
            P(GZ, None),
        ),
        out_specs=(P(GX, GY, GZ), P(GX, GY, GZ), P(None, GZ, None)),
        check_vma=False,
    )
```

```python
import functools
import math

import jax
import jax.numpy as jnp
from jax import lax
from jax.experimental import pallas as pl
from jax.experimental.pallas import tpu as pltpu
from jax.sharding import Mesh, PartitionSpec as P

ITERS = 2
EPSILON = 1e-06
F32 = jnp.float32
BF16 = jnp.bfloat16

AXES = ("y", "z", "xlo", "xhi", "core")
SIZES = {"y": 4, "z": 8, "xlo": 2, "xhi": 2, "core": 2}
GX = ("y",)
GY = ("z", "xlo")
GZ = ("xhi", "core")
PLANE = ("y", "xlo", "xhi")
VMEM_LIMIT = 16 * 1024 * 1024

BINS = 16
TENSORS = 12
FIELDS = 96
PLANES = 16
LANES = 128
ROWS = 384
BLOCKS = ((0, 0), (0, 1), (0, 2), (1, 1), (1, 2), (2, 2))


def vmem():
    return pl.BlockSpec(memory_space=pltpu.VMEM)


def in_hbm(value):
    return pltpu.with_memory_space_constraint(value, pltpu.HBM)


def hbm():
    return pl.BlockSpec(memory_space=pltpu.HBM)


def lane_ids(shape):
    return lax.broadcasted_iota(jnp.int32, shape, len(shape) - 1)


def spread(values, bins, tensor):
    parts = []
    for b in range(BINS):
        here = bins == b
        for k in range(2):
            parts.append(jnp.sum(jnp.where(here, values[k], 0.0), axis=0, keepdims=True))
    table = jnp.concatenate(parts, axis=0)
    return jnp.concatenate(
        [
            jnp.sum(jnp.where(tensor == r, table, 0.0), axis=1, keepdims=True)
            for r in range(TENSORS)
        ],
        axis=0,
    )


def pick(column, bins, tensor):
    table = jnp.zeros((2 * BINS, bins.shape[1]), F32)
    for r in range(TENSORS):
        table = jnp.where(tensor == r, column[r * 32 : (r + 1) * 32, :], table)
    out = [jnp.zeros(bins.shape, F32), jnp.zeros(bins.shape, F32)]
    for b in range(BINS):
        here = bins == b
        for k in range(2):
            out[k] = jnp.where(here, table[2 * b + k : 2 * b + k + 1, :], out[k])
    return out


def data_sums(observed, tensor, bins, window):
    mask = window.astype(F32)
    rhs = [observed[k] * mask for k in range(2)]
    total = spread(rhs, bins, tensor)
    count = spread([mask, mask], bins, tensor)
    mean = total / jnp.maximum(count, 1.0)
    near = pick(mean, bins, tensor)
    rest = [rhs[k] - near[k] * mask for k in range(2)]
    square = jnp.sum(rest[0] * rest[0] + rest[1] * rest[1], axis=(0, 1), keepdims=True)
    lane = lane_ids((ROWS, LANES))
    wide = jnp.where(lane == 0, total, jnp.where(lane == 1, count, square))
    return jnp.concatenate([wide[j * LANES : (j + 1) * LANES, :].T[:8] for j in range(3)], axis=0)


def merge_sums(one, two):
    total, count = one[0:1] + two[0:1], one[1:2] + two[1:2]
    gap = one[0:1] / jnp.maximum(one[1:2], 1.0) - two[0:1] / jnp.maximum(two[1:2], 1.0)
    apart = jnp.sum(
        one[1:2] * two[1:2] / jnp.maximum(count, 1.0) * gap * gap, axis=1, keepdims=True
    )
    rest = one[2:3] + two[2:3] + apart
    return jnp.concatenate([total, count, rest, jnp.zeros((5, ROWS), F32)], axis=0)


def pack_kernel(
    src_in, ids_in, table_in, observed_in, tensor_in, bins_in, window_in,
    src, y_lo, y_hi, to_core, to_cross, stats, scales,
    ids, table, observed, tensor, bins, window, sems,
):
    copies = [
        pltpu.make_async_copy(here, there, sems.at[n])
        for n, (here, there) in enumerate(
            (
                (src_in, src),
                (ids_in, ids),
                (table_in, table),
                (observed_in, observed),
                (tensor_in, tensor),
                (bins_in, bins),
                (window_in, window),
            )
        )
    ]
    for copy in copies:
        copy.start()
    for copy in copies[1:]:
        copy.wait()
    for p in range(3):
        scale = jnp.zeros((PLANES, LANES), F32)
        for m in range(8):
            scale = jnp.where(ids[...] == m, table[p, m], scale)
        scales[p * PLANES : (p + 1) * PLANES, :] = scale * (1.0 / 12.0)
    sums = data_sums(observed, tensor[...], bins[...], window[...])
    stats[...] = sums
    to_core[FIELDS:, :] = sums
    to_cross[FIELDS:, :] = sums

    copies[0].wait()
    y = lax.broadcasted_iota(jnp.int32, (FIELDS, 8, LANES), 1) & 3
    first, second = src[:, 0:8, :], src[:, 8:16, :]
    low = [
        jnp.where(y == 1, 8.0 * pltpu.roll(half, 1, 1), 0.0) - half for half in (first, second)
    ]
    high = [
        half - jnp.where(y == 2, 8.0 * pltpu.roll(half, 7, 1), 0.0) for half in (first, second)
    ]
    y_lo[...] = jnp.where(y < 2, low[1], pltpu.roll(low[0], 2, 1))
    y_hi[...] = jnp.where(y < 2, pltpu.roll(high[0], 6, 1), high[1])

    lane = lane_ids((FIELDS, LANES))
    low = jnp.zeros((FIELDS, LANES), F32)
    high = jnp.zeros((FIELDS, LANES), F32)
    for plane in range(PLANES):
        value = src[:, plane, :]
        turned = pltpu.roll(value, 8 * plane, 1) if plane else value
        place = (lane - 8 * plane) & (LANES - 1)
        low = jnp.where(place < 2, turned, low)
        high = jnp.where(place >= LANES - 2, turned, high)
    place = lane & 7
    low = jnp.where(place == 1, 8.0 * pltpu.roll(low, 1, 1), 0.0) - low
    high = high - jnp.where(place == 6, 8.0 * pltpu.roll(high, LANES - 1, 1), 0.0)
    low = pltpu.roll(low, LANES - 2, 1)
    high = pltpu.roll(high, 2, 1)
    upper = lax.axis_index("core") == 1
    to_core[:FIELDS, :] = jnp.where(upper, low, high)
    to_cross[:FIELDS, :] = jnp.where(upper, high, low)


def pack(src, ids, table, observed, tensor, bins, window):
    face = jax.ShapeDtypeStruct((FIELDS, 8, LANES), F32)
    ends = jax.ShapeDtypeStruct((FIELDS + 24, LANES), F32)
    given = (src, ids, table, observed, tensor, bins, window)
    return pl.pallas_call(
        pack_kernel,
        out_shape=(
            jax.ShapeDtypeStruct(src.shape, F32),
            face,
            face,
            ends,
            ends,
            jax.ShapeDtypeStruct((24, LANES), F32),
            jax.ShapeDtypeStruct((3 * PLANES, LANES), F32),
        ),
        in_specs=[hbm()] * 7,
        out_specs=(vmem(),) * 7,
        scratch_shapes=[pltpu.VMEM(ids.shape, ids.dtype), pltpu.SMEM(table.shape, table.dtype)]
        + [pltpu.VMEM(x.shape, x.dtype) for x in given[3:]]
        + [pltpu.SemaphoreType.DMA((7,))],
        compiler_params=pltpu.CompilerParams(vmem_limit_bytes=VMEM_LIMIT),
        name="pack",
    )(*(in_hbm(x) for x in given))


def strike_kernel(src, part, from_core, x_lo, x_hi, to_cross):
    to_cross[: FIELDS + 24, :] = part[...]
    to_cross[FIELDS + 24 :, :] = from_core[FIELDS:, :]
    first, second = src[:, 0:8, :], src[:, 8:16, :]
    row = lax.broadcasted_iota(jnp.int32, (FIELDS, 8, LANES), 1)
    x_lo[...] = jnp.where(row < 4, 0.0, 8.0 * pltpu.roll(first, 4, 1)) - first
    x_hi[...] = second - jnp.where(row < 4, 8.0 * pltpu.roll(second, 4, 1), 0.0)


def strike_faces(src, part, from_core):
    face = jax.ShapeDtypeStruct((FIELDS, 8, LANES), F32)
    return pl.pallas_call(
        strike_kernel,
        out_shape=(face, face, jax.ShapeDtypeStruct((FIELDS + 48, LANES), F32)),
        in_specs=[vmem()] * 3,
        out_specs=(vmem(),) * 3,
        compiler_params=pltpu.CompilerParams(vmem_limit_bytes=VMEM_LIMIT),
        name="strike_faces",
    )(src, part, from_core)


def ends_of(axes):
    at = lax.axis_index(axes)
    last = math.prod(SIZES[a] for a in axes) - 1
    return jnp.where(at > 0, 1.0, 0.0).astype(F32), jnp.where(at < last, 1.0, 0.0).astype(F32)


def tile(ref, at):
    return ref[pl.ds(pl.multiple_of(at * PLANES, PLANES), PLANES), :]


def set_tile(ref, at, value):
    ref[pl.ds(pl.multiple_of(at * PLANES, PLANES), PLANES), :] = value


def within_kernel(src, from_core, receiver_in, grads, receiver, sem):
    load = pltpu.make_async_copy(receiver_in, receiver, sem)
    load.start()
    lane = lane_ids((FIELDS, LANES))
    halo = from_core[:FIELDS, :]

    def at(x, y):
        if min(x, y) < 0 or max(x, y) > 3:
            return 0.0
        return src[pl.ds(x * 4 + y, FIELDS, stride=PLANES), :]

    def put(p, plane, value):
        grads[pl.ds(p * FIELDS * PLANES + plane, FIELDS, stride=PLANES), :] = value

    for x in range(4):
        for y in range(4):
            plane = x * 4 + y
            put(0, plane, 8.0 * (at(x + 1, y) - at(x - 1, y)) - (at(x + 2, y) - at(x - 2, y)))
            put(1, plane, 8.0 * (at(x, y + 1) - at(x, y - 1)) - (at(x, y + 2) - at(x, y - 2)))
            mid = at(x, y)
            later = jnp.where(lane < LANES - 1, pltpu.roll(mid, LANES - 1, 1), 0.0)
            sooner = jnp.where(lane > 0, pltpu.roll(mid, 1, 1), 0.0)
            later_two = jnp.where(lane < LANES - 2, pltpu.roll(mid, LANES - 2, 1), 0.0)
            sooner_two = jnp.where(lane > 1, pltpu.roll(mid, 2, 1), 0.0)
            value = 8.0 * (later - sooner) - (later_two - sooner_two)
            put(2, plane, value + ends_at(halo, plane, lane))
    load.wait()


def ends_at(halo, plane, lane):
    turned = pltpu.roll(halo, LANES - 8 * plane, 1) if plane else halo
    return jnp.where((lane < 2) | (lane >= LANES - 2), turned, 0.0)


def within(src, from_core, receiver):
    return pl.pallas_call(
        within_kernel,
        out_shape=(
            jax.ShapeDtypeStruct((3 * FIELDS * PLANES, LANES), F32),
            jax.ShapeDtypeStruct(receiver.shape, receiver.dtype),
        ),
        in_specs=[vmem(), vmem(), hbm()],
        out_specs=(vmem(), vmem()),
        scratch_shapes=[pltpu.SemaphoreType.DMA],
        compiler_params=pltpu.CompilerParams(vmem_limit_bytes=VMEM_LIMIT),
        cost_estimate=pl.CostEstimate(
            flops=4_000_000, bytes_accessed=14_000_000, transcendentals=0
        ),
        name="within",
    )(src, from_core, in_hbm(receiver))


def gram_kernel(
    scales, grads, receiver, xb, xa, yb, ya, own, from_core, from_cross,
    keep, send, cells, stats, ends
):
    lane = lane_ids((FIELDS, LANES))
    crossing = jnp.where(lax.axis_index("xhi") != lax.axis_index("core"), 1.0, 0.0).astype(F32)
    halo = from_cross[:FIELDS, :] * crossing
    for plane in range(PLANES):
        ends[pl.ds(plane, FIELDS, stride=PLANES), :] = ends_at(halo, plane, lane)
    x_before, x_after = ends_of(GX)
    y_before, y_after = ends_of(GY)
    low_y = (lax.broadcasted_iota(jnp.int32, (8, LANES), 0) & 3) < 2

    def body(b, carry):
        def grad(p, q, k):
            field = b * 6 + q * 2 + k
            value = tile(grads, p * FIELDS + field)
            if p == 0:
                value = value + jnp.concatenate([xb[field] * x_before, xa[field] * x_after], axis=0)
            elif p == 1:
                below, above = yb[field] * y_before, ya[field] * y_after
                value = value + jnp.concatenate(
                    [
                        jnp.where(low_y, below, above),
                        jnp.where(low_y, pltpu.roll(below, 6, 0), pltpu.roll(above, 2, 0)),
                    ],
                    axis=0,
                )
            else:
                value = value + tile(ends, field)
            return tile(scales, p) * value

        real, imag = [
            (
                grad(0, 0, k),
                grad(1, 1, k),
                grad(2, 2, k),
                grad(1, 2, k) + grad(2, 1, k),
                grad(0, 2, k) + grad(2, 0, k),
                grad(0, 1, k) + grad(1, 0, k),
            )
            for k in range(2)
        ]
        for r in range(TENSORS):
            re = im = None
            for j in range(6):
                rec_re = receiver[r, b, 2 * j].astype(F32)
                rec_im = receiver[r, b, 2 * j + 1].astype(F32)
                add_re = rec_re * real[j] - rec_im * imag[j]
                add_im = rec_re * imag[j] + rec_im * real[j]
                re, im = (re + add_re, im + add_im) if j else (add_re, add_im)
            set_tile(cells, r * 32 + b * 2, re)
            set_tile(cells, r * 32 + b * 2 + 1, im)
        return carry

    lax.fori_loop(0, BINS, body, 0)

    total = jnp.zeros((ROWS, ROWS), F32)
    for plane in range(0, PLANES, 2):
        both = jnp.concatenate(
            [cells[pl.ds(plane + i, ROWS, stride=PLANES), :] for i in range(2)], axis=1
        )
        high = both.astype(BF16)
        low = (both - high.astype(F32)).astype(BF16)
        left = jnp.concatenate([high, high], axis=1)
        right = jnp.concatenate([high * BF16(0.5), low], axis=1)
        total = total + lax.dot_general(
            left, right, (((1,), (1,)), ((), ())), preferred_element_type=F32
        )

    def block(i, j):
        return total[i * LANES : (i + 1) * LANES, j * LANES : (j + 1) * LANES]

    full = [block(i, j) + block(j, i).T for i, j in BLOCKS]
    upper = lax.axis_index("core") == 1
    for n in range(3):
        part = slice(n * LANES, (n + 1) * LANES)
        keep[part, :] = jnp.where(upper, full[n + 3], full[n])
        send[part, :] = jnp.where(upper, full[n], full[n + 3])

    def sums_of(value):
        return jnp.concatenate([value[8 * j : 8 * j + 8, :] for j in range(3)], axis=1)

    stats[...] = merge_sums(
        merge_sums(sums_of(own[...]), sums_of(from_core[FIELDS:, :])),
        merge_sums(sums_of(from_cross[FIELDS : FIELDS + 24, :]), sums_of(from_cross[FIELDS + 24 :, :])),
    )


def gram(scales, grads, receiver, halos, sums):
    half = jax.ShapeDtypeStruct((3 * LANES, LANES), F32)
    return pl.pallas_call(
        gram_kernel,
        out_shape=(
            half,
            half,
            jax.ShapeDtypeStruct((ROWS * PLANES, LANES), F32),
            jax.ShapeDtypeStruct((8, ROWS), F32),
        ),
        in_specs=[vmem()] * 10,
        out_specs=(vmem(),) * 4,
        scratch_shapes=[pltpu.VMEM((FIELDS * PLANES, LANES), F32)],
        compiler_params=pltpu.CompilerParams(vmem_limit_bytes=VMEM_LIMIT),
        cost_estimate=pl.CostEstimate(
            flops=1_200_000_000, bytes_accessed=8_000_000, transcendentals=0
        ),
        name="gram",
    )(scales, grads, receiver, *halos, *sums)


def chain_kernel(
    mine, other, stats, cells, observed_in, tensor_in, bins_in, window_in, update, direction, data,
    full, coef, observed, tensor_ref, bins_ref, window, sems
):
    copies = [
        pltpu.make_async_copy(here, there, sems.at[n])
        for n, (here, there) in enumerate(
            (
                (observed_in, observed),
                (tensor_in, tensor_ref),
                (bins_in, bins_ref),
                (window_in, window),
            )
        )
    ]
    for copy in copies:
        copy.start()
    upper = lax.axis_index("core") == 1
    for n, (i, j) in enumerate(BLOCKS):
        part = slice(n % 3 * LANES, (n % 3 + 1) * LANES)
        near, far = mine[part, :], other[part, :]
        block = jnp.where(upper, far, near) if n < 3 else jnp.where(upper, near, far)
        full[i * LANES : (i + 1) * LANES, j * LANES : (j + 1) * LANES] = block
        if i != j:
            full[j * LANES : (j + 1) * LANES, i * LANES : (i + 1) * LANES] = block.T
    eye = lax.broadcasted_iota(jnp.int32, (LANES, LANES), 0) == lane_ids((LANES, LANES))

    def column(row):
        return jnp.concatenate(
            [
                jnp.sum(
                    jnp.where(eye, row[:, j * LANES : (j + 1) * LANES], 0.0), axis=1, keepdims=True
                )
                for j in range(3)
            ],
            axis=0,
        )

    def product(row):
        return jnp.sum(full[...] * column(row), axis=0, keepdims=True)

    def total(row):
        return jnp.sum(row, axis=1, keepdims=True)

    def norm_of(square):
        return jnp.sqrt(square + EPSILON)

    sums, count, rest = stats[0:1, :], stats[1:2, :], stats[2:3, 0:1]
    mean = sums / jnp.maximum(count, 1.0)

    def data_norm(scale, row):
        inside = scale * mean + row
        return norm_of(scale * scale * rest + total(count * inside * inside))

    one = jnp.ones((1, 1), F32)
    row = jnp.zeros((1, ROWS), F32)
    beta = data_norm(one, row)
    beta_first = beta
    scale = one / beta
    raw = scale * sums
    image = product(raw)
    alpha = norm_of(total(raw * image))
    alpha_first = alpha
    model = raw / alpha
    search = model
    answer = jnp.zeros((1, ROWS), F32)
    phi_bar, rho_bar = beta, alpha
    for _ in range(ITERS):
        scale, row = -alpha * scale, image / alpha - alpha * row
        beta = data_norm(scale, row)
        scale, row = scale / beta, row / beta
        raw = scale * sums + count * row - beta * model
        image = product(raw)
        alpha = norm_of(total(raw * image))
        model = raw / alpha
        rho = jnp.sqrt(rho_bar * rho_bar + beta * beta)
        cosine, sine = rho_bar / rho, beta / rho
        theta = sine * alpha
        rho_bar = -cosine * alpha
        phi = cosine * phi_bar
        phi_bar = sine * phi_bar
        answer = answer + phi / rho * search
        search = model - theta / rho * search
    cell_scale = math.sqrt(PLANES * LANES * math.prod(SIZES.values()))
    coef[0] = jnp.broadcast_to(
        column(answer * (alpha_first * cell_scale / beta_first)), (ROWS, LANES)
    )
    coef[1] = jnp.broadcast_to(column(model * cell_scale), (ROWS, LANES))

    def body(n, sums_of):
        value = tile(cells, n)
        return (
            sums_of[0] + coef[0, pl.ds(n, 1), :] * value,
            sums_of[1] + coef[1, pl.ds(n, 1), :] * value,
        )

    start = (jnp.zeros((PLANES, LANES), F32), jnp.zeros((PLANES, LANES), F32))
    first, second = lax.fori_loop(0, ROWS, body, start, unroll=16)
    update[...] = first
    direction[...] = second

    for copy in copies:
        copy.wait()
    mask = window[...].astype(F32)
    size = math.sqrt(math.prod(observed.shape) * SIZES["xhi"] * SIZES["core"])
    near = pick(column(row * size), bins_ref[...], tensor_ref[...])
    for k in range(2):
        data[k] = (observed[k] * (scale * size) + near[k]) * mask


def chain(mine, other, stats, cells, observed, tensor, bins, window):
    field = jax.ShapeDtypeStruct((PLANES, LANES), F32)
    given = (observed, tensor, bins, window)
    return pl.pallas_call(
        chain_kernel,
        out_shape=(field, field, jax.ShapeDtypeStruct(observed.shape, F32)),
        in_specs=[vmem()] * 4 + [pl.BlockSpec(memory_space=pl.ANY)] * 4,
        out_specs=(vmem(),) * 3,
        scratch_shapes=[pltpu.VMEM((ROWS, ROWS), F32), pltpu.VMEM((2, ROWS, LANES), F32)]
        + [pltpu.VMEM(x.shape, x.dtype) for x in given]
        + [pltpu.SemaphoreType.DMA((4,))],
        compiler_params=pltpu.CompilerParams(vmem_limit_bytes=VMEM_LIMIT),
        name="chain",
    )(mine, other, stats, cells, *given)


def shift(value, axes, step):
    count = math.prod(SIZES[a] for a in axes)
    return lax.ppermute(value, axes, [(i, (i + step) % count) for i in range(count)])


def swap(value, axis):
    return lax.ppermute(value, axis, [(0, 1), (1, 0)])


def exchange(value, axes):
    return lax.all_to_all(value, axes, 0, 0, tiled=True)


def scatter_sum(value, axes):
    count = math.prod(SIZES[a] for a in axes)
    return jnp.sum(exchange(value.reshape(count, -1, LANES), axes), axis=0)


def whole_sum(value, axes):
    count = math.prod(SIZES[a] for a in axes)
    return jnp.sum(exchange(jnp.broadcast_to(value, (count,) + value.shape), axes), axis=0)


def gather(value, axes):
    count = math.prod(SIZES[a] for a in axes)
    return exchange(jnp.broadcast_to(value, (count,) + value.shape), axes).reshape(-1, LANES)


def per_device(
    source_field,
    receiver_tensor,
    metric_ids,
    metric_table,
    observed,
    receiver_index,
    bin_ids,
    window,
):
    src = source_field.reshape(FIELDS, PLANES, LANES)
    receiver = receiver_tensor.reshape(TENSORS, BINS, 12, PLANES, LANES)
    ids = metric_ids.reshape(PLANES, LANES)
    table = metric_table.T
    values = observed.transpose(0, 2, 1)
    tensor = receiver_index.reshape(1, -1)
    bins, marks = bin_ids.T, window.T
    src, y_lo, y_hi, to_core, to_cross, stats, scales = pack(
        src, ids, table, values, tensor, bins, marks
    )
    yb, ya = shift(y_hi, GY, 1), shift(y_lo, GY, -1)
    from_core = swap(to_core, "core")
    x_lo, x_hi, to_cross = strike_faces(src, to_cross, from_core)
    xb, xa = shift(x_hi, GX, 1), shift(x_lo, GX, -1)
    from_cross = lax.ppermute(to_cross, GZ, [(i, 3 - i) for i in range(4)])

    grads, receiver = within(src.reshape(FIELDS * PLANES, LANES), from_core, receiver)
    sums = (stats, from_core, from_cross)
    keep, send, cells, stats = gram(scales, grads, receiver, (xb, xa, yb, ya), sums)
    packed = keep + swap(send, "core")
    packed = scatter_sum(packed, PLANE)
    packed = whole_sum(packed, ("z",))
    packed = gather(packed, PLANE)
    other = swap(packed, "core")
    update, direction, data = chain(packed, other, stats, cells, values, tensor, bins, marks)
    return (
        update.reshape(metric_ids.shape),
        direction.reshape(metric_ids.shape),
        data.transpose(0, 2, 1),
    )


def solution(mesh):
    fine = Mesh(mesh.devices.reshape([SIZES[a] for a in AXES]), AXES)
    return jax.shard_map(
        per_device,
        mesh=fine,
        in_specs=(
            P(None, None, None, GX, GY, GZ),
            P(None, None, None, None, GX, GY, GZ),
            P(GX, GY, GZ),
            P(),
            P(None, GZ, None),
            P(GZ),
            P(GZ, None),
            P(GZ, None),
        ),
        out_specs=(P(GX, GY, GZ), P(GX, GY, GZ), P(None, GZ, None)),
        check_vma=False,
    )
```

```python
import functools
import math

import jax
import jax.numpy as jnp
from jax import lax
from jax.experimental import pallas as pl
from jax.experimental.pallas import tpu as pltpu
from jax.sharding import Mesh, PartitionSpec as P

ITERS = 2
EPSILON = 1e-06
F32 = jnp.float32
BF16 = jnp.bfloat16

AXES = ("y", "z", "xlo", "xhi", "core")
SIZES = {"y": 4, "z": 8, "xlo": 2, "xhi": 2, "core": 2}
GX = ("y",)
GY = ("z", "xlo")
GZ = ("xhi", "core")
PLANE = ("y", "xlo", "xhi")
VMEM_LIMIT = 16 * 1024 * 1024

BINS = 16
TENSORS = 12
FIELDS = 96
PLANES = 16
LANES = 128
ROWS = 384
BLOCKS = ((0, 0), (0, 1), (0, 2), (1, 1), (1, 2), (2, 2))


def vmem():
    return pl.BlockSpec(memory_space=pltpu.VMEM)


def in_hbm(value):
    return pltpu.with_memory_space_constraint(value, pltpu.HBM)


def hbm():
    return pl.BlockSpec(memory_space=pltpu.HBM)


def lane_ids(shape):
    return lax.broadcasted_iota(jnp.int32, shape, len(shape) - 1)


def spread(values, bins, tensor):
    parts = []
    for b in range(BINS):
        here = bins == b
        for k in range(2):
            parts.append(jnp.sum(jnp.where(here, values[k], 0.0), axis=0, keepdims=True))
    table = jnp.concatenate(parts, axis=0)
    return jnp.concatenate(
        [
            jnp.sum(jnp.where(tensor == r, table, 0.0), axis=1, keepdims=True)
            for r in range(TENSORS)
        ],
        axis=0,
    )


def pick(column, bins, tensor):
    table = jnp.zeros((2 * BINS, bins.shape[1]), F32)
    for r in range(TENSORS):
        table = jnp.where(tensor == r, column[r * 32 : (r + 1) * 32, :], table)
    out = [jnp.zeros(bins.shape, F32), jnp.zeros(bins.shape, F32)]
    for b in range(BINS):
        here = bins == b
        for k in range(2):
            out[k] = jnp.where(here, table[2 * b + k : 2 * b + k + 1, :], out[k])
    return out


def data_sums(observed, tensor, bins, window):
    mask = window.astype(F32)
    rhs = [observed[k] * mask for k in range(2)]
    total = spread(rhs, bins, tensor)
    count = spread([mask, mask], bins, tensor)
    mean = total / jnp.maximum(count, 1.0)
    near = pick(mean, bins, tensor)
    rest = [rhs[k] - near[k] * mask for k in range(2)]
    square = jnp.sum(rest[0] * rest[0] + rest[1] * rest[1], axis=(0, 1), keepdims=True)
    lane = lane_ids((ROWS, LANES))
    wide = jnp.where(lane == 0, total, jnp.where(lane == 1, count, square))
    return jnp.concatenate([wide[j * LANES : (j + 1) * LANES, :].T[:8] for j in range(3)], axis=0)


def merge_sums(one, two):
    total, count = one[0:1] + two[0:1], one[1:2] + two[1:2]
    gap = one[0:1] / jnp.maximum(one[1:2], 1.0) - two[0:1] / jnp.maximum(two[1:2], 1.0)
    apart = jnp.sum(
        one[1:2] * two[1:2] / jnp.maximum(count, 1.0) * gap * gap, axis=1, keepdims=True
    )
    rest = one[2:3] + two[2:3] + apart
    return jnp.concatenate([total, count, rest, jnp.zeros((5, ROWS), F32)], axis=0)


def pack_kernel(
    src_in, ids_in, table_in, observed_in, tensor_in, bins_in, window_in,
    src, y_lo, y_hi, to_core, to_cross, stats, scales,
    ids, table, observed, tensor, bins, window, sems,
):
    copies = [
        pltpu.make_async_copy(here, there, sems.at[n])
        for n, (here, there) in enumerate(
            (
                (src_in, src),
                (ids_in, ids),
                (table_in, table),
                (observed_in, observed),
                (tensor_in, tensor),
                (bins_in, bins),
                (window_in, window),
            )
        )
    ]
    for copy in copies:
        copy.start()
    for copy in copies[1:]:
        copy.wait()
    for p in range(3):
        scale = jnp.zeros((PLANES, LANES), F32)
        for m in range(8):
            scale = jnp.where(ids[...] == m, table[p, m], scale)
        scales[p * PLANES : (p + 1) * PLANES, :] = scale * (1.0 / 12.0)
    sums = data_sums(observed, tensor[...], bins[...], window[...])
    stats[...] = sums
    to_core[FIELDS:, :] = sums
    to_cross[FIELDS:, :] = sums

    copies[0].wait()
    y = lax.broadcasted_iota(jnp.int32, (FIELDS, 8, LANES), 1) & 3
    first, second = src[:, 0:8, :], src[:, 8:16, :]
    low = [
        jnp.where(y == 1, 8.0 * pltpu.roll(half, 1, 1), 0.0) - half for half in (first, second)
    ]
    high = [
        half - jnp.where(y == 2, 8.0 * pltpu.roll(half, 7, 1), 0.0) for half in (first, second)
    ]
    y_lo[...] = jnp.where(y < 2, low[1], pltpu.roll(low[0], 2, 1))
    y_hi[...] = jnp.where(y < 2, pltpu.roll(high[0], 6, 1), high[1])

    lane = lane_ids((FIELDS, LANES))
    low = jnp.zeros((FIELDS, LANES), F32)
    high = jnp.zeros((FIELDS, LANES), F32)
    for plane in range(PLANES):
        value = src[:, plane, :]
        turned = pltpu.roll(value, 8 * plane, 1) if plane else value
        place = (lane - 8 * plane) & (LANES - 1)
        low = jnp.where(place < 2, turned, low)
        high = jnp.where(place >= LANES - 2, turned, high)
    place = lane & 7
    low = jnp.where(place == 1, 8.0 * pltpu.roll(low, 1, 1), 0.0) - low
    high = high - jnp.where(place == 6, 8.0 * pltpu.roll(high, LANES - 1, 1), 0.0)
    low = pltpu.roll(low, LANES - 2, 1)
    high = pltpu.roll(high, 2, 1)
    upper = lax.axis_index("core") == 1
    to_core[:FIELDS, :] = jnp.where(upper, low, high)
    to_cross[:FIELDS, :] = jnp.where(upper, high, low)


def pack(src, ids, table, observed, tensor, bins, window):
    face = jax.ShapeDtypeStruct((FIELDS, 8, LANES), F32)
    ends = jax.ShapeDtypeStruct((FIELDS + 24, LANES), F32)
    given = (src, ids, table, observed, tensor, bins, window)
    return pl.pallas_call(
        pack_kernel,
        out_shape=(
            jax.ShapeDtypeStruct(src.shape, F32),
            face,
            face,
            ends,
            ends,
            jax.ShapeDtypeStruct((24, LANES), F32),
            jax.ShapeDtypeStruct((3 * PLANES, LANES), F32),
        ),
        in_specs=[hbm()] * 7,
        out_specs=(vmem(),) * 7,
        scratch_shapes=[pltpu.VMEM(ids.shape, ids.dtype), pltpu.SMEM(table.shape, table.dtype)]
        + [pltpu.VMEM(x.shape, x.dtype) for x in given[3:]]
        + [pltpu.SemaphoreType.DMA((7,))],
        compiler_params=pltpu.CompilerParams(vmem_limit_bytes=VMEM_LIMIT),
        name="pack",
    )(*(in_hbm(x) for x in given))


def strike_kernel(src, part, from_core, x_lo, x_hi, to_cross):
    to_cross[: FIELDS + 24, :] = part[...]
    to_cross[FIELDS + 24 :, :] = from_core[FIELDS:, :]
    first, second = src[:, 0:8, :], src[:, 8:16, :]
    row = lax.broadcasted_iota(jnp.int32, (FIELDS, 8, LANES), 1)
    x_lo[...] = jnp.where(row < 4, 0.0, 8.0 * pltpu.roll(first, 4, 1)) - first
    x_hi[...] = second - jnp.where(row < 4, 8.0 * pltpu.roll(second, 4, 1), 0.0)


def strike_faces(src, part, from_core):
    face = jax.ShapeDtypeStruct((FIELDS, 8, LANES), F32)
    return pl.pallas_call(
        strike_kernel,
        out_shape=(face, face, jax.ShapeDtypeStruct((FIELDS + 48, LANES), F32)),
        in_specs=[vmem()] * 3,
        out_specs=(vmem(),) * 3,
        compiler_params=pltpu.CompilerParams(vmem_limit_bytes=VMEM_LIMIT),
        name="strike_faces",
    )(src, part, from_core)


def ends_of(axes):
    at = lax.axis_index(axes)
    last = math.prod(SIZES[a] for a in axes) - 1
    return jnp.where(at > 0, 1.0, 0.0).astype(F32), jnp.where(at < last, 1.0, 0.0).astype(F32)


def tile(ref, at):
    return ref[pl.ds(pl.multiple_of(at * PLANES, PLANES), PLANES), :]


def set_tile(ref, at, value):
    ref[pl.ds(pl.multiple_of(at * PLANES, PLANES), PLANES), :] = value


def within_kernel(scales, src, from_core, receiver_in, strain, receiver, grads, slots, sems):
    def fetch(b):
        return pltpu.make_async_copy(receiver_in.at[:, b], slots.at[b], sems.at[b])

    for b in range(BINS):
        fetch(b).start()
    lane = lane_ids((FIELDS, LANES))
    halo = from_core[:FIELDS, :]

    def at(x, y):
        if min(x, y) < 0 or max(x, y) > 3:
            return 0.0
        return src[pl.ds(x * 4 + y, FIELDS, stride=PLANES), :]

    def put(p, plane, value):
        grads[pl.ds(p * FIELDS * PLANES + plane, FIELDS, stride=PLANES), :] = value

    for x in range(4):
        for y in range(4):
            plane = x * 4 + y
            put(0, plane, 8.0 * (at(x + 1, y) - at(x - 1, y)) - (at(x + 2, y) - at(x - 2, y)))
            put(1, plane, 8.0 * (at(x, y + 1) - at(x, y - 1)) - (at(x, y + 2) - at(x, y - 2)))
            mid = at(x, y)
            later = jnp.where(lane < LANES - 1, pltpu.roll(mid, LANES - 1, 1), 0.0)
            sooner = jnp.where(lane > 0, pltpu.roll(mid, 1, 1), 0.0)
            later_two = jnp.where(lane < LANES - 2, pltpu.roll(mid, LANES - 2, 1), 0.0)
            sooner_two = jnp.where(lane > 1, pltpu.roll(mid, 2, 1), 0.0)
            value = 8.0 * (later - sooner) - (later_two - sooner_two)
            put(2, plane, value + ends_at(halo, plane, lane))

    def body(b, carry):
        def grad(p, q, k):
            return tile(scales, p) * tile(grads, p * FIELDS + b * 6 + q * 2 + k)

        for k in range(2):
            for j, value in enumerate(
                (
                    grad(0, 0, k),
                    grad(1, 1, k),
                    grad(2, 2, k),
                    grad(1, 2, k) + grad(2, 1, k),
                    grad(0, 2, k) + grad(2, 0, k),
                    grad(0, 1, k) + grad(1, 0, k),
                )
            ):
                set_tile(strain, b * 12 + j * 2 + k, value)
        fetch(b).wait()
        for r in range(TENSORS):
            receiver[r, b] = slots[b, r].astype(F32)
        return carry

    lax.fori_loop(0, BINS, body, 0)


def ends_at(halo, plane, lane):
    turned = pltpu.roll(halo, LANES - 8 * plane, 1) if plane else halo
    return jnp.where((lane < 2) | (lane >= LANES - 2), turned, 0.0)


def within(scales, src, from_core, receiver):
    return pl.pallas_call(
        within_kernel,
        out_shape=(
            jax.ShapeDtypeStruct((BINS * 12 * PLANES, LANES), F32),
            jax.ShapeDtypeStruct(receiver.shape, F32),
        ),
        in_specs=[vmem(), vmem(), vmem(), hbm()],
        out_specs=(vmem(), vmem()),
        scratch_shapes=[
            pltpu.VMEM((3 * FIELDS * PLANES, LANES), F32),
            pltpu.VMEM((BINS, TENSORS, 12, PLANES, LANES), BF16),
            pltpu.SemaphoreType.DMA((BINS,)),
        ],
        compiler_params=pltpu.CompilerParams(vmem_limit_bytes=VMEM_LIMIT),
        cost_estimate=pl.CostEstimate(
            flops=4_000_000, bytes_accessed=14_000_000, transcendentals=0
        ),
        name="within",
    )(scales, src, from_core, in_hbm(receiver))


def gram_kernel(
    scales, within, receiver, xb, xa, yb, ya, own, from_core, from_cross,
    keep, send, cells, stats, ends
):
    lane = lane_ids((FIELDS, LANES))
    crossing = jnp.where(lax.axis_index("xhi") != lax.axis_index("core"), 1.0, 0.0).astype(F32)
    halo = from_cross[:FIELDS, :] * crossing
    for plane in range(PLANES):
        ends[pl.ds(plane, FIELDS, stride=PLANES), :] = ends_at(halo, plane, lane)
    x_before, x_after = ends_of(GX)
    y_before, y_after = ends_of(GY)
    low_y = (lax.broadcasted_iota(jnp.int32, (8, LANES), 0) & 3) < 2
    side = jnp.where(low_y, y_before, y_after)
    scale_x = (scales[0:8, :] * x_before, scales[8:16, :] * x_after)
    scale_y = (scales[16:24, :] * side, scales[24:32, :] * side)
    scale_z = tile(scales, 2)

    def body(b, carry):
        def from_x(field):
            return jnp.concatenate([scale_x[0] * xb[field], scale_x[1] * xa[field]], axis=0)

        def from_y(field):
            below, above = yb[field], ya[field]
            first = jnp.where(low_y, below, above)
            second = jnp.where(low_y, pltpu.roll(below, 6, 0), pltpu.roll(above, 2, 0))
            return jnp.concatenate([scale_y[0] * first, scale_y[1] * second], axis=0)

        def from_z(field):
            return scale_z * tile(ends, field)

        strain = []
        for k in range(2):
            inner = [tile(within, b * 12 + j * 2 + k) for j in range(6)]
            ux, uy, uz = [b * 6 + q * 2 + k for q in range(3)]
            strain.append(
                (
                    inner[0] + from_x(ux),
                    inner[1] + from_y(uy),
                    inner[2] + from_z(uz),
                    inner[3] + (from_y(uz) + from_z(uy)),
                    inner[4] + (from_x(uz) + from_z(ux)),
                    inner[5] + (from_x(uy) + from_y(ux)),
                )
            )
        real, imag = strain
        for r in range(TENSORS):
            re = im = None
            for j in range(6):
                rec_re, rec_im = receiver[r, b, 2 * j], receiver[r, b, 2 * j + 1]
                add_re = rec_re * real[j] - rec_im * imag[j]
                add_im = rec_re * imag[j] + rec_im * real[j]
                re, im = (re + add_re, im + add_im) if j else (add_re, add_im)
            set_tile(cells, r * 32 + b * 2, re)
            set_tile(cells, r * 32 + b * 2 + 1, im)
        return carry

    lax.fori_loop(0, BINS, body, 0)

    total = jnp.zeros((ROWS, ROWS), F32)
    for plane in range(0, PLANES, 2):
        both = jnp.concatenate(
            [cells[pl.ds(plane + i, ROWS, stride=PLANES), :] for i in range(2)], axis=1
        )
        high = both.astype(BF16)
        low = (both - high.astype(F32)).astype(BF16)
        left = jnp.concatenate([high, high], axis=1)
        right = jnp.concatenate([high * BF16(0.5), low], axis=1)
        total = total + lax.dot_general(
            left, right, (((1,), (1,)), ((), ())), preferred_element_type=F32
        )

    def block(i, j):
        return total[i * LANES : (i + 1) * LANES, j * LANES : (j + 1) * LANES]

    full = [block(i, j) + block(j, i).T for i, j in BLOCKS]
    upper = lax.axis_index("core") == 1
    for n in range(3):
        part = slice(n * LANES, (n + 1) * LANES)
        keep[part, :] = jnp.where(upper, full[n + 3], full[n])
        send[part, :] = jnp.where(upper, full[n], full[n + 3])

    def sums_of(value):
        return jnp.concatenate([value[8 * j : 8 * j + 8, :] for j in range(3)], axis=1)

    stats[...] = merge_sums(
        merge_sums(sums_of(own[...]), sums_of(from_core[FIELDS:, :])),
        merge_sums(sums_of(from_cross[FIELDS : FIELDS + 24, :]), sums_of(from_cross[FIELDS + 24 :, :])),
    )


def gram(scales, within, receiver, halos, sums):
    half = jax.ShapeDtypeStruct((3 * LANES, LANES), F32)
    return pl.pallas_call(
        gram_kernel,
        out_shape=(
            half,
            half,
            jax.ShapeDtypeStruct((ROWS * PLANES, LANES), F32),
            jax.ShapeDtypeStruct((8, ROWS), F32),
        ),
        in_specs=[vmem()] * 10,
        out_specs=(vmem(),) * 4,
        scratch_shapes=[pltpu.VMEM((FIELDS * PLANES, LANES), F32)],
        compiler_params=pltpu.CompilerParams(vmem_limit_bytes=VMEM_LIMIT),
        cost_estimate=pl.CostEstimate(
            flops=1_200_000_000, bytes_accessed=8_000_000, transcendentals=0
        ),
        name="gram",
    )(scales, within, receiver, *halos, *sums)


def chain_kernel(
    mine, other, stats, cells, observed_in, tensor_in, bins_in, window_in, update, direction, data,
    full, coef, observed, tensor_ref, bins_ref, window, sems
):
    copies = [
        pltpu.make_async_copy(here, there, sems.at[n])
        for n, (here, there) in enumerate(
            (
                (observed_in, observed),
                (tensor_in, tensor_ref),
                (bins_in, bins_ref),
                (window_in, window),
            )
        )
    ]
    for copy in copies:
        copy.start()
    upper = lax.axis_index("core") == 1
    for n, (i, j) in enumerate(BLOCKS):
        part = slice(n % 3 * LANES, (n % 3 + 1) * LANES)
        near, far = mine[part, :], other[part, :]
        block = jnp.where(upper, far, near) if n < 3 else jnp.where(upper, near, far)
        full[i * LANES : (i + 1) * LANES, j * LANES : (j + 1) * LANES] = block
        if i != j:
            full[j * LANES : (j + 1) * LANES, i * LANES : (i + 1) * LANES] = block.T
    eye = lax.broadcasted_iota(jnp.int32, (LANES, LANES), 0) == lane_ids((LANES, LANES))

    def column(row):
        return jnp.concatenate(
            [
                jnp.sum(
                    jnp.where(eye, row[:, j * LANES : (j + 1) * LANES], 0.0), axis=1, keepdims=True
                )
                for j in range(3)
            ],
            axis=0,
        )

    def product(row):
        return jnp.sum(full[...] * column(row), axis=0, keepdims=True)

    def total(row):
        return jnp.sum(row, axis=1, keepdims=True)

    def norm_of(square):
        return jnp.sqrt(square + EPSILON)

    sums, count, rest = stats[0:1, :], stats[1:2, :], stats[2:3, 0:1]
    mean = sums / jnp.maximum(count, 1.0)

    def data_norm(scale, row):
        inside = scale * mean + row
        return norm_of(scale * scale * rest + total(count * inside * inside))

    one = jnp.ones((1, 1), F32)
    row = jnp.zeros((1, ROWS), F32)
    beta = data_norm(one, row)
    beta_first = beta
    scale = one / beta
    raw = scale * sums
    image = product(raw)
    alpha = norm_of(total(raw * image))
    alpha_first = alpha
    model = raw / alpha
    search = model
    answer = jnp.zeros((1, ROWS), F32)
    phi_bar, rho_bar = beta, alpha
    for _ in range(ITERS):
        scale, row = -alpha * scale, image / alpha - alpha * row
        beta = data_norm(scale, row)
        scale, row = scale / beta, row / beta
        raw = scale * sums + count * row - beta * model
        image = product(raw)
        alpha = norm_of(total(raw * image))
        model = raw / alpha
        rho = jnp.sqrt(rho_bar * rho_bar + beta * beta)
        cosine, sine = rho_bar / rho, beta / rho
        theta = sine * alpha
        rho_bar = -cosine * alpha
        phi = cosine * phi_bar
        phi_bar = sine * phi_bar
        answer = answer + phi / rho * search
        search = model - theta / rho * search
    cell_scale = math.sqrt(PLANES * LANES * math.prod(SIZES.values()))
    coef[0] = jnp.broadcast_to(
        column(answer * (alpha_first * cell_scale / beta_first)), (ROWS, LANES)
    )
    coef[1] = jnp.broadcast_to(column(model * cell_scale), (ROWS, LANES))

    def body(n, sums_of):
        value = tile(cells, n)
        return (
            sums_of[0] + coef[0, pl.ds(n, 1), :] * value,
            sums_of[1] + coef[1, pl.ds(n, 1), :] * value,
        )

    start = (jnp.zeros((PLANES, LANES), F32), jnp.zeros((PLANES, LANES), F32))
    first, second = lax.fori_loop(0, ROWS, body, start, unroll=16)
    update[...] = first
    direction[...] = second

    for copy in copies:
        copy.wait()
    mask = window[...].astype(F32)
    size = math.sqrt(math.prod(observed.shape) * SIZES["xhi"] * SIZES["core"])
    near = pick(column(row * size), bins_ref[...], tensor_ref[...])
    for k in range(2):
        data[k] = (observed[k] * (scale * size) + near[k]) * mask


def chain(mine, other, stats, cells, observed, tensor, bins, window):
    field = jax.ShapeDtypeStruct((PLANES, LANES), F32)
    given = (observed, tensor, bins, window)
    return pl.pallas_call(
        chain_kernel,
        out_shape=(field, field, jax.ShapeDtypeStruct(observed.shape, F32)),
        in_specs=[vmem()] * 4 + [pl.BlockSpec(memory_space=pl.ANY)] * 4,
        out_specs=(vmem(),) * 3,
        scratch_shapes=[pltpu.VMEM((ROWS, ROWS), F32), pltpu.VMEM((2, ROWS, LANES), F32)]
        + [pltpu.VMEM(x.shape, x.dtype) for x in given]
        + [pltpu.SemaphoreType.DMA((4,))],
        compiler_params=pltpu.CompilerParams(vmem_limit_bytes=VMEM_LIMIT),
        name="chain",
    )(mine, other, stats, cells, *given)


def shift(value, axes, step):
    count = math.prod(SIZES[a] for a in axes)
    return lax.ppermute(value, axes, [(i, (i + step) % count) for i in range(count)])


def swap(value, axis):
    return lax.ppermute(value, axis, [(0, 1), (1, 0)])


def exchange(value, axes):
    return lax.all_to_all(value, axes, 0, 0, tiled=True)


def scatter_sum(value, axes):
    count = math.prod(SIZES[a] for a in axes)
    return jnp.sum(exchange(value.reshape(count, -1, LANES), axes), axis=0)


def whole_sum(value, axes):
    count = math.prod(SIZES[a] for a in axes)
    return jnp.sum(exchange(jnp.broadcast_to(value, (count,) + value.shape), axes), axis=0)


def gather(value, axes):
    count = math.prod(SIZES[a] for a in axes)
    return exchange(jnp.broadcast_to(value, (count,) + value.shape), axes).reshape(-1, LANES)


def per_device(
    source_field,
    receiver_tensor,
    metric_ids,
    metric_table,
    observed,
    receiver_index,
    bin_ids,
    window,
):
    src = source_field.reshape(FIELDS, PLANES, LANES)
    receiver = receiver_tensor.reshape(TENSORS, BINS, 12, PLANES, LANES)
    ids = metric_ids.reshape(PLANES, LANES)
    table = metric_table.T
    values = observed.transpose(0, 2, 1)
    tensor = receiver_index.reshape(1, -1)
    bins, marks = bin_ids.T, window.T
    src, y_lo, y_hi, to_core, to_cross, stats, scales = pack(
        src, ids, table, values, tensor, bins, marks
    )
    yb, ya = shift(y_hi, GY, 1), shift(y_lo, GY, -1)
    from_core = swap(to_core, "core")
    x_lo, x_hi, to_cross = strike_faces(src, to_cross, from_core)
    xb, xa = shift(x_hi, GX, 1), shift(x_lo, GX, -1)
    from_cross = lax.ppermute(to_cross, GZ, [(i, 3 - i) for i in range(4)])

    strain, receiver = within(scales, src.reshape(FIELDS * PLANES, LANES), from_core, receiver)
    sums = (stats, from_core, from_cross)
    keep, send, cells, stats = gram(scales, strain, receiver, (xb, xa, yb, ya), sums)
    packed = keep + swap(send, "core")
    packed = scatter_sum(packed, PLANE)
    packed = whole_sum(packed, ("z",))
    packed = gather(packed, PLANE)
    other = swap(packed, "core")
    update, direction, data = chain(packed, other, stats, cells, values, tensor, bins, marks)
    return (
        update.reshape(metric_ids.shape),
        direction.reshape(metric_ids.shape),
        data.transpose(0, 2, 1),
    )


def solution(mesh):
    fine = Mesh(mesh.devices.reshape([SIZES[a] for a in AXES]), AXES)
    return jax.shard_map(
        per_device,
        mesh=fine,
        in_specs=(
            P(None, None, None, GX, GY, GZ),
            P(None, None, None, None, GX, GY, GZ),
            P(GX, GY, GZ),
            P(),
            P(None, GZ, None),
            P(GZ),
            P(GZ, None),
            P(GZ, None),
        ),
        out_specs=(P(GX, GY, GZ), P(GX, GY, GZ), P(None, GZ, None)),
        check_vma=False,
    )
```

```python
import functools
import math

import jax
import jax.numpy as jnp
from jax import lax
from jax.experimental import pallas as pl
from jax.experimental.pallas import tpu as pltpu
from jax.sharding import Mesh, PartitionSpec as P

ITERS = 2
EPSILON = 1e-06
F32 = jnp.float32
BF16 = jnp.bfloat16

AXES = ("y", "z", "xlo", "xhi", "core")
SIZES = {"y": 4, "z": 8, "xlo": 2, "xhi": 2, "core": 2}
GX = ("y",)
GY = ("z", "xlo")
GZ = ("xhi", "core")
PLANE = ("y", "xlo", "xhi")
VMEM_LIMIT = 16 * 1024 * 1024

BINS = 16
TENSORS = 12
FIELDS = 96
PLANES = 16
LANES = 128
ROWS = 384
BLOCKS = ((0, 0), (0, 1), (0, 2), (1, 1), (1, 2), (2, 2))


def vmem():
    return pl.BlockSpec(memory_space=pltpu.VMEM)


def in_hbm(value):
    return pltpu.with_memory_space_constraint(value, pltpu.HBM)


def hbm():
    return pl.BlockSpec(memory_space=pltpu.HBM)


def lane_ids(shape):
    return lax.broadcasted_iota(jnp.int32, shape, len(shape) - 1)


def spread(values, bins, tensor):
    parts = []
    for b in range(BINS):
        here = bins == b
        for k in range(2):
            parts.append(jnp.sum(jnp.where(here, values[k], 0.0), axis=0, keepdims=True))
    table = jnp.concatenate(parts, axis=0)
    return jnp.concatenate(
        [
            jnp.sum(jnp.where(tensor == r, table, 0.0), axis=1, keepdims=True)
            for r in range(TENSORS)
        ],
        axis=0,
    )


def pick(column, bins, tensor):
    table = jnp.zeros((2 * BINS, bins.shape[1]), F32)
    for r in range(TENSORS):
        table = jnp.where(tensor == r, column[r * 32 : (r + 1) * 32, :], table)
    out = [jnp.zeros(bins.shape, F32), jnp.zeros(bins.shape, F32)]
    for b in range(BINS):
        here = bins == b
        for k in range(2):
            out[k] = jnp.where(here, table[2 * b + k : 2 * b + k + 1, :], out[k])
    return out


def data_sums(observed, tensor, bins, window):
    mask = window.astype(F32)
    rhs = [observed[k] * mask for k in range(2)]
    total = spread(rhs, bins, tensor)
    count = spread([mask, mask], bins, tensor)
    mean = total / jnp.maximum(count, 1.0)
    near = pick(mean, bins, tensor)
    rest = [rhs[k] - near[k] * mask for k in range(2)]
    square = jnp.sum(rest[0] * rest[0] + rest[1] * rest[1], axis=(0, 1), keepdims=True)
    lane = lane_ids((ROWS, LANES))
    wide = jnp.where(lane == 0, total, jnp.where(lane == 1, count, square))
    return jnp.concatenate([wide[j * LANES : (j + 1) * LANES, :].T[:8] for j in range(3)], axis=0)


def merge_sums(one, two):
    total, count = one[0:1] + two[0:1], one[1:2] + two[1:2]
    gap = one[0:1] / jnp.maximum(one[1:2], 1.0) - two[0:1] / jnp.maximum(two[1:2], 1.0)
    apart = jnp.sum(
        one[1:2] * two[1:2] / jnp.maximum(count, 1.0) * gap * gap, axis=1, keepdims=True
    )
    rest = one[2:3] + two[2:3] + apart
    return jnp.concatenate([total, count, rest, jnp.zeros((5, ROWS), F32)], axis=0)


def pack_kernel(
    src_in, ids_in, table_in, observed_in, tensor_in, bins_in, window_in,
    src, y_lo, y_hi, to_core, to_cross, stats, scales,
    ids, table, observed, tensor, bins, window, sems,
):
    copies = [
        pltpu.make_async_copy(here, there, sems.at[n])
        for n, (here, there) in enumerate(
            (
                (src_in, src),
                (ids_in, ids),
                (table_in, table),
                (observed_in, observed),
                (tensor_in, tensor),
                (bins_in, bins),
                (window_in, window),
            )
        )
    ]
    for copy in copies:
        copy.start()
    for copy in copies[1:]:
        copy.wait()
    for p in range(3):
        scale = jnp.zeros((PLANES, LANES), F32)
        for m in range(8):
            scale = jnp.where(ids[...] == m, table[p, m], scale)
        scales[p * PLANES : (p + 1) * PLANES, :] = scale * (1.0 / 12.0)
    sums = data_sums(observed, tensor[...], bins[...], window[...])
    stats[...] = sums
    to_core[FIELDS:, :] = sums
    to_cross[FIELDS:, :] = sums

    copies[0].wait()
    y = lax.broadcasted_iota(jnp.int32, (FIELDS, 8, LANES), 1) & 3
    first, second = src[:, 0:8, :], src[:, 8:16, :]
    low = [
        jnp.where(y == 1, 8.0 * pltpu.roll(half, 1, 1), 0.0) - half for half in (first, second)
    ]
    high = [
        half - jnp.where(y == 2, 8.0 * pltpu.roll(half, 7, 1), 0.0) for half in (first, second)
    ]
    y_lo[...] = jnp.where(y < 2, low[1], pltpu.roll(low[0], 2, 1))
    y_hi[...] = jnp.where(y < 2, pltpu.roll(high[0], 6, 1), high[1])

    lane = lane_ids((FIELDS, LANES))
    low = jnp.zeros((FIELDS, LANES), F32)
    high = jnp.zeros((FIELDS, LANES), F32)
    for plane in range(PLANES):
        value = src[:, plane, :]
        turned = pltpu.roll(value, 8 * plane, 1) if plane else value
        place = (lane - 8 * plane) & (LANES - 1)
        low = jnp.where(place < 2, turned, low)
        high = jnp.where(place >= LANES - 2, turned, high)
    place = lane & 7
    low = jnp.where(place == 1, 8.0 * pltpu.roll(low, 1, 1), 0.0) - low
    high = high - jnp.where(place == 6, 8.0 * pltpu.roll(high, LANES - 1, 1), 0.0)
    low = pltpu.roll(low, LANES - 2, 1)
    high = pltpu.roll(high, 2, 1)
    upper = lax.axis_index("core") == 1
    to_core[:FIELDS, :] = jnp.where(upper, low, high)
    to_cross[:FIELDS, :] = jnp.where(upper, high, low)


def pack(src, ids, table, observed, tensor, bins, window):
    face = jax.ShapeDtypeStruct((FIELDS, 8, LANES), F32)
    ends = jax.ShapeDtypeStruct((FIELDS + 24, LANES), F32)
    given = (src, ids, table, observed, tensor, bins, window)
    return pl.pallas_call(
        pack_kernel,
        out_shape=(
            jax.ShapeDtypeStruct(src.shape, F32),
            face,
            face,
            ends,
            ends,
            jax.ShapeDtypeStruct((24, LANES), F32),
            jax.ShapeDtypeStruct((3 * PLANES, LANES), F32),
        ),
        in_specs=[hbm()] * 7,
        out_specs=(vmem(),) * 7,
        scratch_shapes=[pltpu.VMEM(ids.shape, ids.dtype), pltpu.SMEM(table.shape, table.dtype)]
        + [pltpu.VMEM(x.shape, x.dtype) for x in given[3:]]
        + [pltpu.SemaphoreType.DMA((7,))],
        compiler_params=pltpu.CompilerParams(vmem_limit_bytes=VMEM_LIMIT),
        name="pack",
    )(*(in_hbm(x) for x in given))


def strike_kernel(src, arrived, x_lo, x_hi):
    first, second = src[:, 0:8, :], src[:, 8:16, :]
    row = lax.broadcasted_iota(jnp.int32, (FIELDS, 8, LANES), 1)
    x_lo[...] = jnp.where(row < 4, 0.0, 8.0 * pltpu.roll(first, 4, 1)) - first
    x_hi[...] = second - jnp.where(row < 4, 8.0 * pltpu.roll(second, 4, 1), 0.0)


def strike_faces(src, arrived):
    face = jax.ShapeDtypeStruct((FIELDS, 8, LANES), F32)
    return pl.pallas_call(
        strike_kernel,
        out_shape=(face, face),
        in_specs=[vmem()] * 2,
        out_specs=(vmem(),) * 2,
        compiler_params=pltpu.CompilerParams(vmem_limit_bytes=VMEM_LIMIT),
        name="strike_faces",
    )(src, arrived)


def ends_of(axes):
    at = lax.axis_index(axes)
    last = math.prod(SIZES[a] for a in axes) - 1
    return jnp.where(at > 0, 1.0, 0.0).astype(F32), jnp.where(at < last, 1.0, 0.0).astype(F32)


def tile(ref, at):
    return ref[pl.ds(pl.multiple_of(at * PLANES, PLANES), PLANES), :]


def set_tile(ref, at, value):
    ref[pl.ds(pl.multiple_of(at * PLANES, PLANES), PLANES), :] = value


def within_kernel(
    scales, src, from_core, from_cross, receiver_in, strain, receiver, grads, slots, sems
):
    def fetch(b):
        return pltpu.make_async_copy(receiver_in.at[:, b], slots.at[b], sems.at[b])

    for b in range(BINS):
        fetch(b).start()
    lane = lane_ids((FIELDS, LANES))
    crossing = jnp.where(lax.axis_index("xhi") != lax.axis_index("core"), 1.0, 0.0).astype(F32)
    halo = from_core[:FIELDS, :] + from_cross[:FIELDS, :] * crossing

    def at(x, y):
        if min(x, y) < 0 or max(x, y) > 3:
            return 0.0
        return src[pl.ds(x * 4 + y, FIELDS, stride=PLANES), :]

    def put(p, plane, value):
        grads[pl.ds(p * FIELDS * PLANES + plane, FIELDS, stride=PLANES), :] = value

    for x in range(4):
        for y in range(4):
            plane = x * 4 + y
            put(0, plane, 8.0 * (at(x + 1, y) - at(x - 1, y)) - (at(x + 2, y) - at(x - 2, y)))
            put(1, plane, 8.0 * (at(x, y + 1) - at(x, y - 1)) - (at(x, y + 2) - at(x, y - 2)))
            mid = at(x, y)
            later = jnp.where(lane < LANES - 1, pltpu.roll(mid, LANES - 1, 1), 0.0)
            sooner = jnp.where(lane > 0, pltpu.roll(mid, 1, 1), 0.0)
            later_two = jnp.where(lane < LANES - 2, pltpu.roll(mid, LANES - 2, 1), 0.0)
            sooner_two = jnp.where(lane > 1, pltpu.roll(mid, 2, 1), 0.0)
            value = 8.0 * (later - sooner) - (later_two - sooner_two)
            put(2, plane, value + ends_at(halo, plane, lane))

    def body(b, carry):
        def grad(p, q, k):
            return tile(scales, p) * tile(grads, p * FIELDS + b * 6 + q * 2 + k)

        for k in range(2):
            for j, value in enumerate(
                (
                    grad(0, 0, k),
                    grad(1, 1, k),
                    grad(2, 2, k),
                    grad(1, 2, k) + grad(2, 1, k),
                    grad(0, 2, k) + grad(2, 0, k),
                    grad(0, 1, k) + grad(1, 0, k),
                )
            ):
                set_tile(strain, b * 12 + j * 2 + k, value)
        fetch(b).wait()
        for r in range(TENSORS):
            receiver[r, b] = slots[b, r].astype(F32)
        return carry

    lax.fori_loop(0, BINS, body, 0)


def ends_at(halo, plane, lane):
    turned = pltpu.roll(halo, LANES - 8 * plane, 1) if plane else halo
    return jnp.where((lane < 2) | (lane >= LANES - 2), turned, 0.0)


def within(scales, src, from_core, from_cross, receiver):
    return pl.pallas_call(
        within_kernel,
        out_shape=(
            jax.ShapeDtypeStruct((BINS * 12 * PLANES, LANES), F32),
            jax.ShapeDtypeStruct(receiver.shape, F32),
        ),
        in_specs=[vmem()] * 4 + [hbm()],
        out_specs=(vmem(), vmem()),
        scratch_shapes=[
            pltpu.VMEM((3 * FIELDS * PLANES, LANES), F32),
            pltpu.VMEM((BINS, TENSORS, 12, PLANES, LANES), BF16),
            pltpu.SemaphoreType.DMA((BINS,)),
        ],
        compiler_params=pltpu.CompilerParams(vmem_limit_bytes=VMEM_LIMIT),
        cost_estimate=pl.CostEstimate(
            flops=4_000_000, bytes_accessed=14_000_000, transcendentals=0
        ),
        name="within",
    )(scales, src, from_core, from_cross, in_hbm(receiver))


def gram_kernel(scales, within, receiver, xb, xa, yb, ya, from_cross, keep, send, cells):
    x_before, x_after = ends_of(GX)
    y_before, y_after = ends_of(GY)
    low_y = (lax.broadcasted_iota(jnp.int32, (8, LANES), 0) & 3) < 2
    side = jnp.where(low_y, y_before, y_after)
    scale_x = (scales[0:8, :] * x_before, scales[8:16, :] * x_after)
    scale_y = (scales[16:24, :] * side, scales[24:32, :] * side)

    def body(b, carry):
        def from_x(field):
            return jnp.concatenate([scale_x[0] * xb[field], scale_x[1] * xa[field]], axis=0)

        def from_y(field):
            below, above = yb[field], ya[field]
            first = jnp.where(low_y, below, above)
            second = jnp.where(low_y, pltpu.roll(below, 6, 0), pltpu.roll(above, 2, 0))
            return jnp.concatenate([scale_y[0] * first, scale_y[1] * second], axis=0)

        strain = []
        for k in range(2):
            inner = [tile(within, b * 12 + j * 2 + k) for j in range(6)]
            ux, uy, uz = [b * 6 + q * 2 + k for q in range(3)]
            strain.append(
                (
                    inner[0] + from_x(ux),
                    inner[1] + from_y(uy),
                    inner[2],
                    inner[3] + from_y(uz),
                    inner[4] + from_x(uz),
                    inner[5] + (from_x(uy) + from_y(ux)),
                )
            )
        real, imag = strain
        for r in range(TENSORS):
            re = im = None
            for j in range(6):
                rec_re, rec_im = receiver[r, b, 2 * j], receiver[r, b, 2 * j + 1]
                add_re = rec_re * real[j] - rec_im * imag[j]
                add_im = rec_re * imag[j] + rec_im * real[j]
                re, im = (re + add_re, im + add_im) if j else (add_re, add_im)
            set_tile(cells, r * 32 + b * 2, re)
            set_tile(cells, r * 32 + b * 2 + 1, im)
        return carry

    lax.fori_loop(0, BINS, body, 0)

    total = jnp.zeros((ROWS, ROWS), F32)
    for plane in range(0, PLANES, 2):
        both = jnp.concatenate(
            [cells[pl.ds(plane + i, ROWS, stride=PLANES), :] for i in range(2)], axis=1
        )
        high = both.astype(BF16)
        low = (both - high.astype(F32)).astype(BF16)
        left = jnp.concatenate([high, high], axis=1)
        right = jnp.concatenate([high * BF16(0.5), low], axis=1)
        total = total + lax.dot_general(
            left, right, (((1,), (1,)), ((), ())), preferred_element_type=F32
        )

    def block(i, j):
        return total[i * LANES : (i + 1) * LANES, j * LANES : (j + 1) * LANES]

    full = [block(i, j) + block(j, i).T for i, j in BLOCKS]
    upper = lax.axis_index("core") == 1
    for n in range(3):
        part = slice(n * LANES, (n + 1) * LANES)
        keep[part, :] = jnp.where(upper, full[n + 3], full[n])
        send[part, :] = jnp.where(upper, full[n], full[n + 3])
    send[ROWS:, :] = from_cross[FIELDS:, :]


def gram(scales, within, receiver, halos, from_cross):
    return pl.pallas_call(
        gram_kernel,
        out_shape=(
            jax.ShapeDtypeStruct((ROWS, LANES), F32),
            jax.ShapeDtypeStruct((ROWS + 24, LANES), F32),
            jax.ShapeDtypeStruct((ROWS * PLANES, LANES), F32),
        ),
        in_specs=[vmem()] * 8,
        out_specs=(vmem(),) * 3,
        compiler_params=pltpu.CompilerParams(vmem_limit_bytes=VMEM_LIMIT),
        cost_estimate=pl.CostEstimate(
            flops=1_200_000_000, bytes_accessed=8_000_000, transcendentals=0
        ),
        name="gram",
    )(scales, within, receiver, *halos, from_cross)


def chain_kernel(
    mine, other, own, from_core, from_cross, received, cells, observed_in, tensor_in, bins_in, window_in, update, direction, data,
    full, coef, observed, tensor_ref, bins_ref, window, sems
):
    copies = [
        pltpu.make_async_copy(here, there, sems.at[n])
        for n, (here, there) in enumerate(
            (
                (observed_in, observed),
                (tensor_in, tensor_ref),
                (bins_in, bins_ref),
                (window_in, window),
            )
        )
    ]
    for copy in copies:
        copy.start()
    upper = lax.axis_index("core") == 1
    for n, (i, j) in enumerate(BLOCKS):
        part = slice(n % 3 * LANES, (n % 3 + 1) * LANES)
        near, far = mine[part, :], other[part, :]
        block = jnp.where(upper, far, near) if n < 3 else jnp.where(upper, near, far)
        full[i * LANES : (i + 1) * LANES, j * LANES : (j + 1) * LANES] = block
        if i != j:
            full[j * LANES : (j + 1) * LANES, i * LANES : (i + 1) * LANES] = block.T
    eye = lax.broadcasted_iota(jnp.int32, (LANES, LANES), 0) == lane_ids((LANES, LANES))

    def column(row):
        return jnp.concatenate(
            [
                jnp.sum(
                    jnp.where(eye, row[:, j * LANES : (j + 1) * LANES], 0.0), axis=1, keepdims=True
                )
                for j in range(3)
            ],
            axis=0,
        )

    def product(row):
        return jnp.sum(full[...] * column(row), axis=0, keepdims=True)

    def total(row):
        return jnp.sum(row, axis=1, keepdims=True)

    def norm_of(square):
        return jnp.sqrt(square + EPSILON)

    def sums_of(value):
        return jnp.concatenate([value[8 * j : 8 * j + 8, :] for j in range(3)], axis=1)

    stats = merge_sums(
        merge_sums(sums_of(own[...]), sums_of(from_core[FIELDS:, :])),
        merge_sums(sums_of(from_cross[FIELDS:, :]), sums_of(received[ROWS:, :])),
    )
    sums, count, rest = stats[0:1, :], stats[1:2, :], stats[2:3, 0:1]
    mean = sums / jnp.maximum(count, 1.0)

    def data_norm(scale, row):
        inside = scale * mean + row
        return norm_of(scale * scale * rest + total(count * inside * inside))

    one = jnp.ones((1, 1), F32)
    row = jnp.zeros((1, ROWS), F32)
    beta = data_norm(one, row)
    beta_first = beta
    scale = one / beta
    raw = scale * sums
    image = product(raw)
    alpha = norm_of(total(raw * image))
    alpha_first = alpha
    model = raw / alpha
    search = model
    answer = jnp.zeros((1, ROWS), F32)
    phi_bar, rho_bar = beta, alpha
    for _ in range(ITERS):
        scale, row = -alpha * scale, image / alpha - alpha * row
        beta = data_norm(scale, row)
        scale, row = scale / beta, row / beta
        raw = scale * sums + count * row - beta * model
        image = product(raw)
        alpha = norm_of(total(raw * image))
        model = raw / alpha
        rho = jnp.sqrt(rho_bar * rho_bar + beta * beta)
        cosine, sine = rho_bar / rho, beta / rho
        theta = sine * alpha
        rho_bar = -cosine * alpha
        phi = cosine * phi_bar
        phi_bar = sine * phi_bar
        answer = answer + phi / rho * search
        search = model - theta / rho * search
    cell_scale = math.sqrt(PLANES * LANES * math.prod(SIZES.values()))
    coef[0] = jnp.broadcast_to(
        column(answer * (alpha_first * cell_scale / beta_first)), (ROWS, LANES)
    )
    coef[1] = jnp.broadcast_to(column(model * cell_scale), (ROWS, LANES))

    def body(n, sums_of):
        value = tile(cells, n)
        return (
            sums_of[0] + coef[0, pl.ds(n, 1), :] * value,
            sums_of[1] + coef[1, pl.ds(n, 1), :] * value,
        )

    start = (jnp.zeros((PLANES, LANES), F32), jnp.zeros((PLANES, LANES), F32))
    first, second = lax.fori_loop(0, ROWS, body, start, unroll=16)
    update[...] = first
    direction[...] = second

    for copy in copies:
        copy.wait()
    mask = window[...].astype(F32)
    size = math.sqrt(math.prod(observed.shape) * SIZES["xhi"] * SIZES["core"])
    near = pick(column(row * size), bins_ref[...], tensor_ref[...])
    for k in range(2):
        data[k] = (observed[k] * (scale * size) + near[k]) * mask


def chain(halves, sums, cells, observed, tensor, bins, window):
    field = jax.ShapeDtypeStruct((PLANES, LANES), F32)
    given = (observed, tensor, bins, window)
    return pl.pallas_call(
        chain_kernel,
        out_shape=(field, field, jax.ShapeDtypeStruct(observed.shape, F32)),
        in_specs=[vmem()] * 7 + [pl.BlockSpec(memory_space=pl.ANY)] * 4,
        out_specs=(vmem(),) * 3,
        scratch_shapes=[pltpu.VMEM((ROWS, ROWS), F32), pltpu.VMEM((2, ROWS, LANES), F32)]
        + [pltpu.VMEM(x.shape, x.dtype) for x in given]
        + [pltpu.SemaphoreType.DMA((4,))],
        compiler_params=pltpu.CompilerParams(vmem_limit_bytes=VMEM_LIMIT),
        name="chain",
    )(*halves, *sums, cells, *given)


def shift(value, axes, step):
    count = math.prod(SIZES[a] for a in axes)
    return lax.ppermute(value, axes, [(i, (i + step) % count) for i in range(count)])


def swap(value, axis):
    return lax.ppermute(value, axis, [(0, 1), (1, 0)])


def exchange(value, axes):
    return lax.all_to_all(value, axes, 0, 0, tiled=True)


def scatter_sum(value, axes):
    count = math.prod(SIZES[a] for a in axes)
    return jnp.sum(exchange(value.reshape(count, -1, LANES), axes), axis=0)


def whole_sum(value, axes):
    count = math.prod(SIZES[a] for a in axes)
    return jnp.sum(exchange(jnp.broadcast_to(value, (count,) + value.shape), axes), axis=0)


def gather(value, axes):
    count = math.prod(SIZES[a] for a in axes)
    return exchange(jnp.broadcast_to(value, (count,) + value.shape), axes).reshape(-1, LANES)


def per_device(
    source_field,
    receiver_tensor,
    metric_ids,
    metric_table,
    observed,
    receiver_index,
    bin_ids,
    window,
):
    src = source_field.reshape(FIELDS, PLANES, LANES)
    receiver = receiver_tensor.reshape(TENSORS, BINS, 12, PLANES, LANES)
    ids = metric_ids.reshape(PLANES, LANES)
    table = metric_table.T
    values = observed.transpose(0, 2, 1)
    tensor = receiver_index.reshape(1, -1)
    bins, marks = bin_ids.T, window.T
    src, y_lo, y_hi, to_core, to_cross, stats, scales = pack(
        src, ids, table, values, tensor, bins, marks
    )
    from_cross = lax.ppermute(to_cross, GZ, [(i, 3 - i) for i in range(4)])
    yb, ya = shift(y_hi, GY, 1), shift(y_lo, GY, -1)
    x_lo, x_hi = strike_faces(src, from_cross)
    xb, xa = shift(x_hi, GX, 1), shift(x_lo, GX, -1)
    from_core = swap(to_core, "core")

    flat = src.reshape(FIELDS * PLANES, LANES)
    strain, receiver = within(scales, flat, from_core, from_cross, receiver)
    keep, send, cells = gram(scales, strain, receiver, (xb, xa, yb, ya), from_cross)
    received = swap(send, "core")
    packed = keep + received[:ROWS]
    packed = scatter_sum(packed, PLANE)
    packed = whole_sum(packed, ("z",))
    packed = gather(packed, PLANE)
    other = swap(packed, "core")
    sums = (stats, from_core, from_cross, received)
    update, direction, data = chain((packed, other), sums, cells, values, tensor, bins, marks)
    return (
        update.reshape(metric_ids.shape),
        direction.reshape(metric_ids.shape),
        data.transpose(0, 2, 1),
    )


def solution(mesh):
    fine = Mesh(mesh.devices.reshape([SIZES[a] for a in AXES]), AXES)
    return jax.shard_map(
        per_device,
        mesh=fine,
        in_specs=(
            P(None, None, None, GX, GY, GZ),
            P(None, None, None, None, GX, GY, GZ),
            P(GX, GY, GZ),
            P(),
            P(None, GZ, None),
            P(GZ),
            P(GZ, None),
            P(GZ, None),
        ),
        out_specs=(P(GX, GY, GZ), P(GX, GY, GZ), P(None, GZ, None)),
        check_vma=False,
    )
```

```python
import functools
import math

import jax
import jax.numpy as jnp
from jax import lax
from jax.experimental import pallas as pl
from jax.experimental.pallas import tpu as pltpu
from jax.sharding import Mesh, PartitionSpec as P

ITERS = 2
EPSILON = 1e-06
F32 = jnp.float32
BF16 = jnp.bfloat16

AXES = ("y", "z", "xlo", "xhi", "core")
SIZES = {"y": 4, "z": 8, "xlo": 2, "xhi": 2, "core": 2}
GX = ("y",)
GY = ("z", "xlo")
GZ = ("xhi", "core")
PLANE = ("y", "xlo", "xhi")
VMEM_LIMIT = 16 * 1024 * 1024

BINS = 16
TENSORS = 12
FIELDS = 96
PLANES = 16
LANES = 128
DENSE = 24
ROWS = 384
BLOCKS = ((0, 0), (0, 1), (0, 2), (1, 1), (1, 2), (2, 2))


def vmem():
    return pl.BlockSpec(memory_space=pltpu.VMEM)


def in_hbm(value):
    return pltpu.with_memory_space_constraint(value, pltpu.HBM)


def hbm():
    return pl.BlockSpec(memory_space=pltpu.HBM)


def lane_ids(shape):
    return lax.broadcasted_iota(jnp.int32, shape, len(shape) - 1)


def spread(values, bins, tensor):
    parts = []
    for b in range(BINS):
        here = bins == b
        for k in range(2):
            parts.append(jnp.sum(jnp.where(here, values[k], 0.0), axis=0, keepdims=True))
    table = jnp.concatenate(parts, axis=0)
    return jnp.concatenate(
        [
            jnp.sum(jnp.where(tensor == r, table, 0.0), axis=1, keepdims=True)
            for r in range(TENSORS)
        ],
        axis=0,
    )


def pick(column, bins, tensor):
    table = jnp.zeros((2 * BINS, bins.shape[1]), F32)
    for r in range(TENSORS):
        table = jnp.where(tensor == r, column[r * 32 : (r + 1) * 32, :], table)
    out = [jnp.zeros(bins.shape, F32), jnp.zeros(bins.shape, F32)]
    for b in range(BINS):
        here = bins == b
        for k in range(2):
            out[k] = jnp.where(here, table[2 * b + k : 2 * b + k + 1, :], out[k])
    return out


def data_sums(observed, tensor, bins, window):
    mask = window.astype(F32)
    rhs = [observed[k] * mask for k in range(2)]
    total = spread(rhs, bins, tensor)
    count = spread([mask, mask], bins, tensor)
    mean = total / jnp.maximum(count, 1.0)
    near = pick(mean, bins, tensor)
    rest = [rhs[k] - near[k] * mask for k in range(2)]
    square = jnp.sum(rest[0] * rest[0] + rest[1] * rest[1], axis=(0, 1), keepdims=True)
    lane = lane_ids((ROWS, LANES))
    wide = jnp.where(lane == 0, total, jnp.where(lane == 1, count, square))
    part = [wide[j * LANES : (j + 1) * LANES, :].T[:8] for j in range(3)]
    rows = [part[j][k : k + 1] for k in range(2) for j in range(3)] + [part[0][2:3]] * 2
    return jnp.concatenate(rows, axis=0)


def sums_of(value):
    total = jnp.concatenate([value[j : j + 1, :] for j in range(3)], axis=1)
    count = jnp.concatenate([value[j : j + 1, :] for j in range(3, 6)], axis=1)
    return jnp.concatenate([total, count, jnp.concatenate([value[6:7, :]] * 3, axis=1)], axis=0)


def merge_sums(one, two):
    total, count = one[0:1] + two[0:1], one[1:2] + two[1:2]
    gap = one[0:1] / jnp.maximum(one[1:2], 1.0) - two[0:1] / jnp.maximum(two[1:2], 1.0)
    apart = jnp.sum(
        one[1:2] * two[1:2] / jnp.maximum(count, 1.0) * gap * gap, axis=1, keepdims=True
    )
    rest = one[2:3] + two[2:3] + apart
    return jnp.concatenate([total, count, rest, jnp.zeros((5, ROWS), F32)], axis=0)


def pack_kernel(
    src_in, ids_in, table_in, observed_in, tensor_in, bins_in, window_in,
    src, y_lo, y_hi, to_core, to_cross, stats, scales,
    ids, table, observed, tensor, bins, window, sparse, sems,
):
    copies = [
        pltpu.make_async_copy(here, there, sems.at[n])
        for n, (here, there) in enumerate(
            (
                (src_in, src),
                (ids_in, ids),
                (table_in, table),
                (observed_in, observed),
                (tensor_in, tensor),
                (bins_in, bins),
                (window_in, window),
            )
        )
    ]
    for copy in copies:
        copy.start()
    for copy in copies[1:]:
        copy.wait()
    for p in range(3):
        scale = jnp.zeros((PLANES, LANES), F32)
        for m in range(8):
            scale = jnp.where(ids[...] == m, table[p, m], scale)
        scales[p * PLANES : (p + 1) * PLANES, :] = scale * (1.0 / 12.0)
    sums = data_sums(observed, tensor[...], bins[...], window[...])
    stats[...] = sums
    to_core[DENSE:, :] = sums
    to_cross[DENSE:, :] = sums

    copies[0].wait()
    y = lax.broadcasted_iota(jnp.int32, (FIELDS, 8, LANES), 1) & 3
    first, second = src[:, 0:8, :], src[:, 8:16, :]
    low = [
        jnp.where(y == 1, 8.0 * pltpu.roll(half, 1, 1), 0.0) - half for half in (first, second)
    ]
    high = [
        half - jnp.where(y == 2, 8.0 * pltpu.roll(half, 7, 1), 0.0) for half in (first, second)
    ]
    y_lo[...] = jnp.where(y < 2, low[1], pltpu.roll(low[0], 2, 1))
    y_hi[...] = jnp.where(y < 2, pltpu.roll(high[0], 6, 1), high[1])

    lane = lane_ids((FIELDS, LANES))
    low = jnp.zeros((FIELDS, LANES), F32)
    high = jnp.zeros((FIELDS, LANES), F32)
    for plane in range(PLANES):
        value = src[:, plane, :]
        turned = pltpu.roll(value, 8 * plane, 1) if plane else value
        place = (lane - 8 * plane) & (LANES - 1)
        low = jnp.where(place < 2, turned, low)
        high = jnp.where(place >= LANES - 2, turned, high)
    place = lane & 7
    low = jnp.where(place == 1, 8.0 * pltpu.roll(low, 1, 1), 0.0) - low
    high = high - jnp.where(place == 6, 8.0 * pltpu.roll(high, LANES - 1, 1), 0.0)
    high = pltpu.roll(high, 2, 1)
    upper = lax.axis_index("core") == 1
    to_core[:DENSE, :] = dense(jnp.where(upper, low, high), sparse)
    to_cross[:DENSE, :] = dense(jnp.where(upper, high, low), sparse)


def dense(value, sparse):
    sparse[...] = value
    lane = lane_ids((DENSE, LANES)) & 7
    out = jnp.zeros((DENSE, LANES), F32)
    for n in range(4):
        part = sparse[pl.ds(n, DENSE, stride=4), :]
        out = jnp.where(lane >> 1 == n, pltpu.roll(part, 2 * n, 1) if n else part, out)
    return out


def spread_out(value, sparse, lower):
    lane = lane_ids((DENSE, LANES)) & 7
    for n in range(4):
        part = pltpu.roll(value, LANES - 2 * n, 1) if n else value
        part = jnp.where(lane < 2, part, 0.0)
        sparse[pl.ds(n, DENSE, stride=4), :] = jnp.where(
            lower, part, pltpu.roll(part, LANES - 2, 1)
        )
    return sparse[...]


def pack(src, ids, table, observed, tensor, bins, window):
    face = jax.ShapeDtypeStruct((FIELDS, 8, LANES), F32)
    ends = jax.ShapeDtypeStruct((DENSE + 8, LANES), F32)
    given = (src, ids, table, observed, tensor, bins, window)
    return pl.pallas_call(
        pack_kernel,
        out_shape=(
            jax.ShapeDtypeStruct(src.shape, F32),
            face,
            face,
            ends,
            ends,
            jax.ShapeDtypeStruct((8, LANES), F32),
            jax.ShapeDtypeStruct((3 * PLANES, LANES), F32),
        ),
        in_specs=[hbm()] * 7,
        out_specs=(vmem(),) * 7,
        scratch_shapes=[pltpu.VMEM(ids.shape, ids.dtype), pltpu.SMEM(table.shape, table.dtype)]
        + [pltpu.VMEM(x.shape, x.dtype) for x in given[3:]]
        + [pltpu.VMEM((FIELDS, LANES), F32), pltpu.SemaphoreType.DMA((7,))],
        compiler_params=pltpu.CompilerParams(vmem_limit_bytes=VMEM_LIMIT),
        name="pack",
    )(*(in_hbm(x) for x in given))


def strike_kernel(src, part, from_core, x_lo, x_hi, to_cross):
    to_cross[: DENSE + 8, :] = part[...]
    to_cross[DENSE + 8 :, :] = from_core[DENSE:, :]
    first, second = src[:, 0:8, :], src[:, 8:16, :]
    row = lax.broadcasted_iota(jnp.int32, (FIELDS, 8, LANES), 1)
    x_lo[...] = jnp.where(row < 4, 0.0, 8.0 * pltpu.roll(first, 4, 1)) - first
    x_hi[...] = second - jnp.where(row < 4, 8.0 * pltpu.roll(second, 4, 1), 0.0)


def strike_faces(src, part, from_core):
    face = jax.ShapeDtypeStruct((FIELDS, 8, LANES), F32)
    return pl.pallas_call(
        strike_kernel,
        out_shape=(face, face, jax.ShapeDtypeStruct((DENSE + 16, LANES), F32)),
        in_specs=[vmem()] * 3,
        out_specs=(vmem(),) * 3,
        compiler_params=pltpu.CompilerParams(vmem_limit_bytes=VMEM_LIMIT),
        name="strike_faces",
    )(src, part, from_core)


def ends_of(axes):
    at = lax.axis_index(axes)
    last = math.prod(SIZES[a] for a in axes) - 1
    return jnp.where(at > 0, 1.0, 0.0).astype(F32), jnp.where(at < last, 1.0, 0.0).astype(F32)


def tile(ref, at):
    return ref[pl.ds(pl.multiple_of(at * PLANES, PLANES), PLANES), :]


def set_tile(ref, at, value):
    ref[pl.ds(pl.multiple_of(at * PLANES, PLANES), PLANES), :] = value


def within_kernel(
    scales, src, from_core, receiver_in, strain, receiver, grads, slots, sparse, sems
):
    def fetch(b):
        return pltpu.make_async_copy(receiver_in.at[:, b], slots.at[b], sems.at[b])

    for b in range(BINS):
        fetch(b).start()
    lane = lane_ids((FIELDS, LANES))
    halo = spread_out(from_core[:DENSE, :], sparse, lax.axis_index("core") == 1)

    def at(x, y):
        if min(x, y) < 0 or max(x, y) > 3:
            return 0.0
        return src[pl.ds(x * 4 + y, FIELDS, stride=PLANES), :]

    def put(p, plane, value):
        grads[pl.ds(p * FIELDS * PLANES + plane, FIELDS, stride=PLANES), :] = value

    for x in range(4):
        for y in range(4):
            plane = x * 4 + y
            put(0, plane, 8.0 * (at(x + 1, y) - at(x - 1, y)) - (at(x + 2, y) - at(x - 2, y)))
            put(1, plane, 8.0 * (at(x, y + 1) - at(x, y - 1)) - (at(x, y + 2) - at(x, y - 2)))
            mid = at(x, y)
            later = jnp.where(lane < LANES - 1, pltpu.roll(mid, LANES - 1, 1), 0.0)
            sooner = jnp.where(lane > 0, pltpu.roll(mid, 1, 1), 0.0)
            later_two = jnp.where(lane < LANES - 2, pltpu.roll(mid, LANES - 2, 1), 0.0)
            sooner_two = jnp.where(lane > 1, pltpu.roll(mid, 2, 1), 0.0)
            value = 8.0 * (later - sooner) - (later_two - sooner_two)
            put(2, plane, value + ends_at(halo, plane, lane))

    def body(b, carry):
        def grad(p, q, k):
            return tile(scales, p) * tile(grads, p * FIELDS + b * 6 + q * 2 + k)

        for k in range(2):
            for j, value in enumerate(
                (
                    grad(0, 0, k),
                    grad(1, 1, k),
                    grad(2, 2, k),
                    grad(1, 2, k) + grad(2, 1, k),
                    grad(0, 2, k) + grad(2, 0, k),
                    grad(0, 1, k) + grad(1, 0, k),
                )
            ):
                set_tile(strain, b * 12 + j * 2 + k, value)
        fetch(b).wait()
        for r in range(TENSORS):
            receiver[r, b] = slots[b, r].astype(F32)
        return carry

    lax.fori_loop(0, BINS, body, 0)


def ends_at(halo, plane, lane):
    turned = pltpu.roll(halo, LANES - 8 * plane, 1) if plane else halo
    return jnp.where((lane < 2) | (lane >= LANES - 2), turned, 0.0)


def within(scales, src, from_core, receiver):
    return pl.pallas_call(
        within_kernel,
        out_shape=(
            jax.ShapeDtypeStruct((BINS * 12 * PLANES, LANES), F32),
            jax.ShapeDtypeStruct(receiver.shape, F32),
        ),
        in_specs=[vmem(), vmem(), vmem(), hbm()],
        out_specs=(vmem(), vmem()),
        scratch_shapes=[
            pltpu.VMEM((3 * FIELDS * PLANES, LANES), F32),
            pltpu.VMEM((BINS, TENSORS, 12, PLANES, LANES), BF16),
            pltpu.VMEM((FIELDS, LANES), F32),
            pltpu.SemaphoreType.DMA((BINS,)),
        ],
        compiler_params=pltpu.CompilerParams(vmem_limit_bytes=VMEM_LIMIT),
        cost_estimate=pl.CostEstimate(
            flops=4_000_000, bytes_accessed=14_000_000, transcendentals=0
        ),
        name="within",
    )(scales, src, from_core, in_hbm(receiver))


def gram_kernel(
    scales, within, receiver, xb, xa, yb, ya, own, from_core, from_cross,
    keep, send, cells, stats, ends, sparse
):
    lane = lane_ids((FIELDS, LANES))
    crossing = jnp.where(lax.axis_index("xhi") != lax.axis_index("core"), 1.0, 0.0).astype(F32)
    lower = lax.axis_index("core") == 0
    halo = spread_out(from_cross[:DENSE, :] * crossing, sparse, lower)
    for plane in range(PLANES):
        ends[pl.ds(plane, FIELDS, stride=PLANES), :] = ends_at(halo, plane, lane)
    x_before, x_after = ends_of(GX)
    y_before, y_after = ends_of(GY)
    low_y = (lax.broadcasted_iota(jnp.int32, (8, LANES), 0) & 3) < 2
    side = jnp.where(low_y, y_before, y_after)
    scale_x = (scales[0:8, :] * x_before, scales[8:16, :] * x_after)
    scale_y = (scales[16:24, :] * side, scales[24:32, :] * side)
    scale_z = tile(scales, 2)

    def body(b, carry):
        def from_x(field):
            return jnp.concatenate([scale_x[0] * xb[field], scale_x[1] * xa[field]], axis=0)

        def from_y(field):
            below, above = yb[field], ya[field]
            first = jnp.where(low_y, below, above)
            second = jnp.where(low_y, pltpu.roll(below, 6, 0), pltpu.roll(above, 2, 0))
            return jnp.concatenate([scale_y[0] * first, scale_y[1] * second], axis=0)

        def from_z(field):
            return scale_z * tile(ends, field)

        strain = []
        for k in range(2):
            inner = [tile(within, b * 12 + j * 2 + k) for j in range(6)]
            ux, uy, uz = [b * 6 + q * 2 + k for q in range(3)]
            strain.append(
                (
                    inner[0] + from_x(ux),
                    inner[1] + from_y(uy),
                    inner[2] + from_z(uz),
                    inner[3] + (from_y(uz) + from_z(uy)),
                    inner[4] + (from_x(uz) + from_z(ux)),
                    inner[5] + (from_x(uy) + from_y(ux)),
                )
            )
        real, imag = strain
        for r in range(TENSORS):
            re = im = None
            for j in range(6):
                rec_re, rec_im = receiver[r, b, 2 * j], receiver[r, b, 2 * j + 1]
                add_re = rec_re * real[j] - rec_im * imag[j]
                add_im = rec_re * imag[j] + rec_im * real[j]
                re, im = (re + add_re, im + add_im) if j else (add_re, add_im)
            set_tile(cells, r * 32 + b * 2, re)
            set_tile(cells, r * 32 + b * 2 + 1, im)
        return carry

    lax.fori_loop(0, BINS, body, 0)

    total = jnp.zeros((ROWS, ROWS), F32)
    for plane in range(0, PLANES, 2):
        both = jnp.concatenate(
            [cells[pl.ds(plane + i, ROWS, stride=PLANES), :] for i in range(2)], axis=1
        )
        high = both.astype(BF16)
        low = (both - high.astype(F32)).astype(BF16)
        left = jnp.concatenate([high, high], axis=1)
        right = jnp.concatenate([high * BF16(0.5), low], axis=1)
        total = total + lax.dot_general(
            left, right, (((1,), (1,)), ((), ())), preferred_element_type=F32
        )

    def block(i, j):
        return total[i * LANES : (i + 1) * LANES, j * LANES : (j + 1) * LANES]

    full = [block(i, j) + block(j, i).T for i, j in BLOCKS]
    upper = lax.axis_index("core") == 1
    for n in range(3):
        part = slice(n * LANES, (n + 1) * LANES)
        keep[part, :] = jnp.where(upper, full[n + 3], full[n])
        send[part, :] = jnp.where(upper, full[n], full[n + 3])

    stats[...] = merge_sums(
        merge_sums(sums_of(own[...]), sums_of(from_core[DENSE:, :])),
        merge_sums(
            sums_of(from_cross[DENSE : DENSE + 8, :]), sums_of(from_cross[DENSE + 8 :, :])
        ),
    )


def gram(scales, within, receiver, halos, sums):
    half = jax.ShapeDtypeStruct((3 * LANES, LANES), F32)
    return pl.pallas_call(
        gram_kernel,
        out_shape=(
            half,
            half,
            jax.ShapeDtypeStruct((ROWS * PLANES, LANES), F32),
            jax.ShapeDtypeStruct((8, ROWS), F32),
        ),
        in_specs=[vmem()] * 10,
        out_specs=(vmem(),) * 4,
        scratch_shapes=[
            pltpu.VMEM((FIELDS * PLANES, LANES), F32),
            pltpu.VMEM((FIELDS, LANES), F32),
        ],
        compiler_params=pltpu.CompilerParams(vmem_limit_bytes=VMEM_LIMIT),
        cost_estimate=pl.CostEstimate(
            flops=1_200_000_000, bytes_accessed=8_000_000, transcendentals=0
        ),
        name="gram",
    )(scales, within, receiver, *halos, *sums)


def chain_kernel(
    mine, other, stats, cells, observed_in, tensor_in, bins_in, window_in, update, direction, data,
    full, coef, observed, tensor_ref, bins_ref, window, sems
):
    copies = [
        pltpu.make_async_copy(here, there, sems.at[n])
        for n, (here, there) in enumerate(
            (
                (observed_in, observed),
                (tensor_in, tensor_ref),
                (bins_in, bins_ref),
                (window_in, window),
            )
        )
    ]
    for copy in copies:
        copy.start()
    upper = lax.axis_index("core") == 1
    for n, (i, j) in enumerate(BLOCKS):
        part = slice(n % 3 * LANES, (n % 3 + 1) * LANES)
        near, far = mine[part, :], other[part, :]
        block = jnp.where(upper, far, near) if n < 3 else jnp.where(upper, near, far)
        full[i * LANES : (i + 1) * LANES, j * LANES : (j + 1) * LANES] = block
        if i != j:
            full[j * LANES : (j + 1) * LANES, i * LANES : (i + 1) * LANES] = block.T
    eye = lax.broadcasted_iota(jnp.int32, (LANES, LANES), 0) == lane_ids((LANES, LANES))

    def column(row):
        return jnp.concatenate(
            [
                jnp.sum(
                    jnp.where(eye, row[:, j * LANES : (j + 1) * LANES], 0.0), axis=1, keepdims=True
                )
                for j in range(3)
            ],
            axis=0,
        )

    def product(row):
        return jnp.sum(full[...] * column(row), axis=0, keepdims=True)

    def total(row):
        return jnp.sum(row, axis=1, keepdims=True)

    def norm_of(square):
        return jnp.sqrt(square + EPSILON)

    sums, count, rest = stats[0:1, :], stats[1:2, :], stats[2:3, 0:1]
    mean = sums / jnp.maximum(count, 1.0)

    def data_norm(scale, row):
        inside = scale * mean + row
        return norm_of(scale * scale * rest + total(count * inside * inside))

    one = jnp.ones((1, 1), F32)
    row = jnp.zeros((1, ROWS), F32)
    beta = data_norm(one, row)
    beta_first = beta
    scale = one / beta
    raw = scale * sums
    image = product(raw)
    alpha = norm_of(total(raw * image))
    alpha_first = alpha
    model = raw / alpha
    search = model
    answer = jnp.zeros((1, ROWS), F32)
    phi_bar, rho_bar = beta, alpha
    for _ in range(ITERS):
        scale, row = -alpha * scale, image / alpha - alpha * row
        beta = data_norm(scale, row)
        scale, row = scale / beta, row / beta
        raw = scale * sums + count * row - beta * model
        image = product(raw)
        alpha = norm_of(total(raw * image))
        model = raw / alpha
        rho = jnp.sqrt(rho_bar * rho_bar + beta * beta)
        cosine, sine = rho_bar / rho, beta / rho
        theta = sine * alpha
        rho_bar = -cosine * alpha
        phi = cosine * phi_bar
        phi_bar = sine * phi_bar
        answer = answer + phi / rho * search
        search = model - theta / rho * search
    cell_scale = math.sqrt(PLANES * LANES * math.prod(SIZES.values()))
    coef[0] = jnp.broadcast_to(
        column(answer * (alpha_first * cell_scale / beta_first)), (ROWS, LANES)
    )
    coef[1] = jnp.broadcast_to(column(model * cell_scale), (ROWS, LANES))

    def body(n, sums_of):
        value = tile(cells, n)
        return (
            sums_of[0] + coef[0, pl.ds(n, 1), :] * value,
            sums_of[1] + coef[1, pl.ds(n, 1), :] * value,
        )

    start = (jnp.zeros((PLANES, LANES), F32), jnp.zeros((PLANES, LANES), F32))
    first, second = lax.fori_loop(0, ROWS, body, start, unroll=16)
    update[...] = first
    direction[...] = second

    for copy in copies:
        copy.wait()
    mask = window[...].astype(F32)
    size = math.sqrt(math.prod(observed.shape) * SIZES["xhi"] * SIZES["core"])
    near = pick(column(row * size), bins_ref[...], tensor_ref[...])
    for k in range(2):
        data[k] = (observed[k] * (scale * size) + near[k]) * mask


def chain(mine, other, stats, cells, observed, tensor, bins, window):
    field = jax.ShapeDtypeStruct((PLANES, LANES), F32)
    given = (observed, tensor, bins, window)
    return pl.pallas_call(
        chain_kernel,
        out_shape=(field, field, jax.ShapeDtypeStruct(observed.shape, F32)),
        in_specs=[vmem()] * 4 + [pl.BlockSpec(memory_space=pl.ANY)] * 4,
        out_specs=(vmem(),) * 3,
        scratch_shapes=[pltpu.VMEM((ROWS, ROWS), F32), pltpu.VMEM((2, ROWS, LANES), F32)]
        + [pltpu.VMEM(x.shape, x.dtype) for x in given]
        + [pltpu.SemaphoreType.DMA((4,))],
        compiler_params=pltpu.CompilerParams(vmem_limit_bytes=VMEM_LIMIT),
        name="chain",
    )(mine, other, stats, cells, *given)


def shift(value, axes, step):
    count = math.prod(SIZES[a] for a in axes)
    return lax.ppermute(value, axes, [(i, (i + step) % count) for i in range(count)])


def swap(value, axis):
    return lax.ppermute(value, axis, [(0, 1), (1, 0)])


def exchange(value, axes):
    return lax.all_to_all(value, axes, 0, 0, tiled=True)


def scatter_sum(value, axes):
    count = math.prod(SIZES[a] for a in axes)
    return jnp.sum(exchange(value.reshape(count, -1, LANES), axes), axis=0)


def whole_sum(value, axes):
    count = math.prod(SIZES[a] for a in axes)
    return jnp.sum(exchange(jnp.broadcast_to(value, (count,) + value.shape), axes), axis=0)


def gather(value, axes):
    count = math.prod(SIZES[a] for a in axes)
    return exchange(jnp.broadcast_to(value, (count,) + value.shape), axes).reshape(-1, LANES)


def per_device(
    source_field,
    receiver_tensor,
    metric_ids,
    metric_table,
    observed,
    receiver_index,
    bin_ids,
    window,
):
    src = source_field.reshape(FIELDS, PLANES, LANES)
    receiver = receiver_tensor.reshape(TENSORS, BINS, 12, PLANES, LANES)
    ids = metric_ids.reshape(PLANES, LANES)
    table = metric_table.T
    values = observed.transpose(0, 2, 1)
    tensor = receiver_index.reshape(1, -1)
    bins, marks = bin_ids.T, window.T
    src, y_lo, y_hi, to_core, to_cross, stats, scales = pack(
        src, ids, table, values, tensor, bins, marks
    )
    yb, ya = shift(y_hi, GY, 1), shift(y_lo, GY, -1)
    from_core = swap(to_core, "core")
    x_lo, x_hi, to_cross = strike_faces(src, to_cross, from_core)
    xb, xa = shift(x_hi, GX, 1), shift(x_lo, GX, -1)
    from_cross = lax.ppermute(to_cross, GZ, [(i, 3 - i) for i in range(4)])

    strain, receiver = within(scales, src.reshape(FIELDS * PLANES, LANES), from_core, receiver)
    sums = (stats, from_core, from_cross)
    keep, send, cells, stats = gram(scales, strain, receiver, (xb, xa, yb, ya), sums)
    packed = keep + swap(send, "core")
    packed = scatter_sum(packed, PLANE)
    packed = whole_sum(packed, ("z",))
    packed = gather(packed, PLANE)
    other = swap(packed, "core")
    update, direction, data = chain(packed, other, stats, cells, values, tensor, bins, marks)
    return (
        update.reshape(metric_ids.shape),
        direction.reshape(metric_ids.shape),
        data.transpose(0, 2, 1),
    )


def solution(mesh):
    fine = Mesh(mesh.devices.reshape([SIZES[a] for a in AXES]), AXES)
    return jax.shard_map(
        per_device,
        mesh=fine,
        in_specs=(
            P(None, None, None, GX, GY, GZ),
            P(None, None, None, None, GX, GY, GZ),
            P(GX, GY, GZ),
            P(),
            P(None, GZ, None),
            P(GZ),
            P(GZ, None),
            P(GZ, None),
        ),
        out_specs=(P(GX, GY, GZ), P(GX, GY, GZ), P(None, GZ, None)),
        check_vma=False,
    )
```

```python
import functools
import math

import jax
import jax.numpy as jnp
from jax import lax
from jax.experimental import pallas as pl
from jax.experimental.pallas import tpu as pltpu
from jax.sharding import Mesh, PartitionSpec as P

ITERS = 2
EPSILON = 1e-06
F32 = jnp.float32
BF16 = jnp.bfloat16

AXES = ("y", "z", "xlo", "xhi", "core")
SIZES = {"y": 4, "z": 8, "xlo": 2, "xhi": 2, "core": 2}
GX = ("y",)
GY = ("z", "xlo")
GZ = ("xhi", "core")
PLANE = ("y", "xlo", "xhi")
VMEM_LIMIT = 16 * 1024 * 1024

BINS = 16
TENSORS = 12
FIELDS = 96
PLANES = 16
LANES = 128
DENSE = 24
ROWS = 384
BLOCKS = ((0, 0), (0, 1), (0, 2), (1, 1), (1, 2), (2, 2))


def vmem():
    return pl.BlockSpec(memory_space=pltpu.VMEM)


def in_hbm(value):
    return pltpu.with_memory_space_constraint(value, pltpu.HBM)


def hbm():
    return pl.BlockSpec(memory_space=pltpu.HBM)


def lane_ids(shape):
    return lax.broadcasted_iota(jnp.int32, shape, len(shape) - 1)


def spread(values, bins, tensor):
    parts = []
    for b in range(BINS):
        here = bins == b
        for k in range(2):
            if k == 0 or len(values) == 2:
                part = jnp.sum(jnp.where(here, values[k], 0.0), axis=0, keepdims=True)
            parts.append(part)
    table = jnp.concatenate(parts, axis=0)
    return jnp.concatenate(
        [
            jnp.sum(jnp.where(tensor == r, table, 0.0), axis=1, keepdims=True)
            for r in range(TENSORS)
        ],
        axis=0,
    )


def pick(column, bins, tensor):
    table = jnp.zeros((2 * BINS, bins.shape[1]), F32)
    for r in range(TENSORS):
        table = jnp.where(tensor == r, column[r * 32 : (r + 1) * 32, :], table)
    out = [jnp.zeros(bins.shape, F32), jnp.zeros(bins.shape, F32)]
    for b in range(BINS):
        here = bins == b
        for k in range(2):
            out[k] = jnp.where(here, table[2 * b + k : 2 * b + k + 1, :], out[k])
    return out


def data_sums(observed, tensor, bins, window):
    mask = window.astype(F32)
    rhs = [observed[k] * mask for k in range(2)]
    total = spread(rhs, bins, tensor)
    count = spread([mask], bins, tensor)
    mean = total / jnp.maximum(count, 1.0)
    near = pick(mean, bins, tensor)
    rest = [rhs[k] - near[k] * mask for k in range(2)]
    square = jnp.sum(rest[0] * rest[0] + rest[1] * rest[1], axis=(0, 1), keepdims=True)
    lane = lane_ids((ROWS, LANES))
    wide = jnp.where(lane == 0, total, jnp.where(lane == 1, count, square))
    part = [wide[j * LANES : (j + 1) * LANES, :].T[:8] for j in range(3)]
    rows = [part[j][k : k + 1] for k in range(2) for j in range(3)] + [part[0][2:3]] * 2
    return jnp.concatenate(rows, axis=0)


def sums_of(value):
    total = jnp.concatenate([value[j : j + 1, :] for j in range(3)], axis=1)
    count = jnp.concatenate([value[j : j + 1, :] for j in range(3, 6)], axis=1)
    return jnp.concatenate([total, count, jnp.concatenate([value[6:7, :]] * 3, axis=1)], axis=0)


def merge_sums(one, two):
    total, count = one[0:1] + two[0:1], one[1:2] + two[1:2]
    gap = one[0:1] / jnp.maximum(one[1:2], 1.0) - two[0:1] / jnp.maximum(two[1:2], 1.0)
    apart = jnp.sum(
        one[1:2] * two[1:2] / jnp.maximum(count, 1.0) * gap * gap, axis=1, keepdims=True
    )
    rest = one[2:3] + two[2:3] + apart
    return jnp.concatenate([total, count, rest, jnp.zeros((5, ROWS), F32)], axis=0)


def pack_kernel(
    src_in, ids_in, table_in, observed_in, tensor_in, bins_in, window_in,
    src, y_lo, y_hi, to_core, to_cross, stats, scales,
    ids, table, observed, tensor, bins, window, sparse, sems,
):
    copies = [
        pltpu.make_async_copy(here, there, sems.at[n])
        for n, (here, there) in enumerate(
            (
                (src_in, src),
                (ids_in, ids),
                (table_in, table),
                (observed_in, observed),
                (tensor_in, tensor),
                (bins_in, bins),
                (window_in, window),
            )
        )
    ]
    for copy in copies[1:] + copies[:1]:
        copy.start()
    for copy in copies[1:]:
        copy.wait()
    for p in range(3):
        scale = jnp.zeros((PLANES, LANES), F32)
        for m in range(8):
            scale = jnp.where(ids[...] == m, table[p, m], scale)
        scales[p * PLANES : (p + 1) * PLANES, :] = scale * (1.0 / 12.0)
    sums = data_sums(observed, tensor[...], bins[...], window[...])
    stats[...] = sums
    to_core[DENSE:, :] = sums
    to_cross[DENSE:, :] = sums

    copies[0].wait()
    y = lax.broadcasted_iota(jnp.int32, (FIELDS, 8, LANES), 1) & 3
    first, second = src[:, 0:8, :], src[:, 8:16, :]
    low = [
        jnp.where(y == 1, 8.0 * pltpu.roll(half, 1, 1), 0.0) - half for half in (first, second)
    ]
    high = [
        half - jnp.where(y == 2, 8.0 * pltpu.roll(half, 7, 1), 0.0) for half in (first, second)
    ]
    y_lo[...] = jnp.where(y < 2, low[1], pltpu.roll(low[0], 2, 1))
    y_hi[...] = jnp.where(y < 2, pltpu.roll(high[0], 6, 1), high[1])

    lane = lane_ids((FIELDS, LANES))
    low = jnp.zeros((FIELDS, LANES), F32)
    high = jnp.zeros((FIELDS, LANES), F32)
    for plane in range(PLANES):
        value = src[:, plane, :]
        turned = pltpu.roll(value, 8 * plane, 1) if plane else value
        place = (lane - 8 * plane) & (LANES - 1)
        low = jnp.where(place < 2, turned, low)
        high = jnp.where(place >= LANES - 2, turned, high)
    place = lane & 7
    low = jnp.where(place == 1, 8.0 * pltpu.roll(low, 1, 1), 0.0) - low
    high = high - jnp.where(place == 6, 8.0 * pltpu.roll(high, LANES - 1, 1), 0.0)
    high = pltpu.roll(high, 2, 1)
    upper = lax.axis_index("core") == 1
    to_core[:DENSE, :] = dense(jnp.where(upper, low, high), sparse)
    to_cross[:DENSE, :] = dense(jnp.where(upper, high, low), sparse)


def dense(value, sparse):
    sparse[...] = value
    lane = lane_ids((DENSE, LANES)) & 7
    out = jnp.zeros((DENSE, LANES), F32)
    for n in range(4):
        part = sparse[pl.ds(n, DENSE, stride=4), :]
        out = jnp.where(lane >> 1 == n, pltpu.roll(part, 2 * n, 1) if n else part, out)
    return out


def spread_out(value, sparse, lower):
    lane = lane_ids((DENSE, LANES)) & 7
    for n in range(4):
        part = pltpu.roll(value, LANES - 2 * n, 1) if n else value
        part = jnp.where(lane < 2, part, 0.0)
        sparse[pl.ds(n, DENSE, stride=4), :] = jnp.where(
            lower, part, pltpu.roll(part, LANES - 2, 1)
        )
    return sparse[...]


def pack(src, ids, table, observed, tensor, bins, window):
    face = jax.ShapeDtypeStruct((FIELDS, 8, LANES), F32)
    ends = jax.ShapeDtypeStruct((DENSE + 8, LANES), F32)
    given = (src, ids, table, observed, tensor, bins, window)
    return pl.pallas_call(
        pack_kernel,
        out_shape=(
            jax.ShapeDtypeStruct(src.shape, F32),
            face,
            face,
            ends,
            ends,
            jax.ShapeDtypeStruct((8, LANES), F32),
            jax.ShapeDtypeStruct((3 * PLANES, LANES), F32),
        ),
        in_specs=[hbm()] * 7,
        out_specs=(vmem(),) * 7,
        scratch_shapes=[pltpu.VMEM(ids.shape, ids.dtype), pltpu.SMEM(table.shape, table.dtype)]
        + [pltpu.VMEM(x.shape, x.dtype) for x in given[3:]]
        + [pltpu.VMEM((FIELDS, LANES), F32), pltpu.SemaphoreType.DMA((7,))],
        compiler_params=pltpu.CompilerParams(vmem_limit_bytes=VMEM_LIMIT),
        name="pack",
    )(*(in_hbm(x) for x in given))


def strike_kernel(src, part, from_core, x_lo, x_hi, to_cross):
    to_cross[: DENSE + 8, :] = part[...]
    to_cross[DENSE + 8 :, :] = from_core[DENSE:, :]
    first, second = src[:, 0:8, :], src[:, 8:16, :]
    row = lax.broadcasted_iota(jnp.int32, (FIELDS, 8, LANES), 1)
    x_lo[...] = jnp.where(row < 4, 0.0, 8.0 * pltpu.roll(first, 4, 1)) - first
    x_hi[...] = second - jnp.where(row < 4, 8.0 * pltpu.roll(second, 4, 1), 0.0)


def strike_faces(src, part, from_core):
    face = jax.ShapeDtypeStruct((FIELDS, 8, LANES), F32)
    return pl.pallas_call(
        strike_kernel,
        out_shape=(face, face, jax.ShapeDtypeStruct((DENSE + 16, LANES), F32)),
        in_specs=[vmem()] * 3,
        out_specs=(vmem(),) * 3,
        compiler_params=pltpu.CompilerParams(vmem_limit_bytes=VMEM_LIMIT),
        name="strike_faces",
    )(src, part, from_core)


def ends_of(axes):
    at = lax.axis_index(axes)
    last = math.prod(SIZES[a] for a in axes) - 1
    return jnp.where(at > 0, 1.0, 0.0).astype(F32), jnp.where(at < last, 1.0, 0.0).astype(F32)


def tile(ref, at):
    return ref[pl.ds(pl.multiple_of(at * PLANES, PLANES), PLANES), :]


def set_tile(ref, at, value):
    ref[pl.ds(pl.multiple_of(at * PLANES, PLANES), PLANES), :] = value


def within_kernel(
    scales, src, from_core, receiver_in, strain, receiver, grads, slots, sparse, sems
):
    def fetch(b):
        return pltpu.make_async_copy(receiver_in.at[:, b], slots.at[b], sems.at[b])

    for b in range(BINS):
        fetch(b).start()
    lane = lane_ids((FIELDS, LANES))
    halo = spread_out(from_core[:DENSE, :], sparse, lax.axis_index("core") == 1)

    def at(x, y):
        if min(x, y) < 0 or max(x, y) > 3:
            return 0.0
        return src[pl.ds(x * 4 + y, FIELDS, stride=PLANES), :]

    def put(p, plane, value):
        grads[pl.ds(p * FIELDS * PLANES + plane, FIELDS, stride=PLANES), :] = value

    for x in range(4):
        for y in range(4):
            plane = x * 4 + y
            put(0, plane, 8.0 * (at(x + 1, y) - at(x - 1, y)) - (at(x + 2, y) - at(x - 2, y)))
            put(1, plane, 8.0 * (at(x, y + 1) - at(x, y - 1)) - (at(x, y + 2) - at(x, y - 2)))
            mid = at(x, y)
            later = jnp.where(lane < LANES - 1, pltpu.roll(mid, LANES - 1, 1), 0.0)
            sooner = jnp.where(lane > 0, pltpu.roll(mid, 1, 1), 0.0)
            later_two = jnp.where(lane < LANES - 2, pltpu.roll(mid, LANES - 2, 1), 0.0)
            sooner_two = jnp.where(lane > 1, pltpu.roll(mid, 2, 1), 0.0)
            value = 8.0 * (later - sooner) - (later_two - sooner_two)
            put(2, plane, value + ends_at(halo, plane, lane))

    def body(b, carry):
        def grad(p, q, k):
            return tile(scales, p) * tile(grads, p * FIELDS + b * 6 + q * 2 + k)

        for k in range(2):
            for j, value in enumerate(
                (
                    grad(0, 0, k),
                    grad(1, 1, k),
                    grad(2, 2, k),
                    grad(1, 2, k) + grad(2, 1, k),
                    grad(0, 2, k) + grad(2, 0, k),
                    grad(0, 1, k) + grad(1, 0, k),
                )
            ):
                set_tile(strain, b * 12 + j * 2 + k, value)
        fetch(b).wait()
        for r in range(TENSORS):
            receiver[r, b] = slots[b, r].astype(F32)
        return carry

    lax.fori_loop(0, BINS, body, 0)


def ends_at(halo, plane, lane):
    turned = pltpu.roll(halo, LANES - 8 * plane, 1) if plane else halo
    return jnp.where((lane < 2) | (lane >= LANES - 2), turned, 0.0)


def within(scales, src, from_core, receiver):
    return pl.pallas_call(
        within_kernel,
        out_shape=(
            jax.ShapeDtypeStruct((BINS * 12 * PLANES, LANES), F32),
            jax.ShapeDtypeStruct(receiver.shape, F32),
        ),
        in_specs=[vmem(), vmem(), vmem(), hbm()],
        out_specs=(vmem(), vmem()),
        scratch_shapes=[
            pltpu.VMEM((3 * FIELDS * PLANES, LANES), F32),
            pltpu.VMEM((BINS, TENSORS, 12, PLANES, LANES), BF16),
            pltpu.VMEM((FIELDS, LANES), F32),
            pltpu.SemaphoreType.DMA((BINS,)),
        ],
        compiler_params=pltpu.CompilerParams(vmem_limit_bytes=VMEM_LIMIT),
        cost_estimate=pl.CostEstimate(
            flops=4_000_000, bytes_accessed=14_000_000, transcendentals=0
        ),
        name="within",
    )(scales, src, from_core, in_hbm(receiver))


def gram_kernel(
    scales, within, receiver, xb, xa, yb, ya, own, from_core, from_cross,
    keep, send, cells, stats, ends, sparse
):
    lane = lane_ids((FIELDS, LANES))
    crossing = jnp.where(lax.axis_index("xhi") != lax.axis_index("core"), 1.0, 0.0).astype(F32)
    lower = lax.axis_index("core") == 0
    halo = spread_out(from_cross[:DENSE, :] * crossing, sparse, lower)
    for plane in range(PLANES):
        ends[pl.ds(plane, FIELDS, stride=PLANES), :] = ends_at(halo, plane, lane)
    x_before, x_after = ends_of(GX)
    y_before, y_after = ends_of(GY)
    low_y = (lax.broadcasted_iota(jnp.int32, (8, LANES), 0) & 3) < 2
    side = jnp.where(low_y, y_before, y_after)
    scale_x = (scales[0:8, :] * x_before, scales[8:16, :] * x_after)
    scale_y = (scales[16:24, :] * side, scales[24:32, :] * side)
    scale_z = tile(scales, 2)

    def body(b, carry):
        def from_x(field):
            return jnp.concatenate([scale_x[0] * xb[field], scale_x[1] * xa[field]], axis=0)

        def from_y(field):
            below, above = yb[field], ya[field]
            first = jnp.where(low_y, below, above)
            second = jnp.where(low_y, pltpu.roll(below, 6, 0), pltpu.roll(above, 2, 0))
            return jnp.concatenate([scale_y[0] * first, scale_y[1] * second], axis=0)

        def from_z(field):
            return scale_z * tile(ends, field)

        strain = []
        for k in range(2):
            inner = [tile(within, b * 12 + j * 2 + k) for j in range(6)]
            ux, uy, uz = [b * 6 + q * 2 + k for q in range(3)]
            strain.append(
                (
                    inner[0] + from_x(ux),
                    inner[1] + from_y(uy),
                    inner[2] + from_z(uz),
                    inner[3] + (from_y(uz) + from_z(uy)),
                    inner[4] + (from_x(uz) + from_z(ux)),
                    inner[5] + (from_x(uy) + from_y(ux)),
                )
            )
        real, imag = strain
        for r in range(TENSORS):
            re = im = None
            for j in range(6):
                rec_re, rec_im = receiver[r, b, 2 * j], receiver[r, b, 2 * j + 1]
                add_re = rec_re * real[j] - rec_im * imag[j]
                add_im = rec_re * imag[j] + rec_im * real[j]
                re, im = (re + add_re, im + add_im) if j else (add_re, add_im)
            set_tile(cells, r * 32 + b * 2, re)
            set_tile(cells, r * 32 + b * 2 + 1, im)
        return carry

    lax.fori_loop(0, BINS, body, 0)

    total = jnp.zeros((ROWS, ROWS), F32)
    for plane in range(0, PLANES, 4):
        both = jnp.concatenate(
            [cells[pl.ds(plane + i, ROWS, stride=PLANES), :] for i in range(4)], axis=1
        )
        high = both.astype(BF16)
        low = (both - high.astype(F32)).astype(BF16)
        left = jnp.concatenate([high, high], axis=1)
        right = jnp.concatenate([high * BF16(0.5), low], axis=1)
        total = total + lax.dot_general(
            left, right, (((1,), (1,)), ((), ())), preferred_element_type=F32
        )

    def block(i, j):
        return total[i * LANES : (i + 1) * LANES, j * LANES : (j + 1) * LANES]

    full = [block(i, j) + block(j, i).T for i, j in BLOCKS]
    upper = lax.axis_index("core") == 1
    for n in range(3):
        part = slice(n * LANES, (n + 1) * LANES)
        keep[part, :] = jnp.where(upper, full[n + 3], full[n])
        send[part, :] = jnp.where(upper, full[n], full[n + 3])

    stats[...] = merge_sums(
        merge_sums(sums_of(own[...]), sums_of(from_core[DENSE:, :])),
        merge_sums(
            sums_of(from_cross[DENSE : DENSE + 8, :]), sums_of(from_cross[DENSE + 8 :, :])
        ),
    )


def gram(scales, within, receiver, halos, sums):
    half = jax.ShapeDtypeStruct((3 * LANES, LANES), F32)
    return pl.pallas_call(
        gram_kernel,
        out_shape=(
            half,
            half,
            jax.ShapeDtypeStruct((ROWS * PLANES, LANES), F32),
            jax.ShapeDtypeStruct((8, ROWS), F32),
        ),
        in_specs=[vmem()] * 10,
        out_specs=(vmem(),) * 4,
        scratch_shapes=[
            pltpu.VMEM((FIELDS * PLANES, LANES), F32),
            pltpu.VMEM((FIELDS, LANES), F32),
        ],
        compiler_params=pltpu.CompilerParams(vmem_limit_bytes=VMEM_LIMIT),
        cost_estimate=pl.CostEstimate(
            flops=1_200_000_000, bytes_accessed=8_000_000, transcendentals=0
        ),
        name="gram",
    )(scales, within, receiver, *halos, *sums)


def chain_kernel(
    mine, other, stats, cells, observed_in, tensor_in, bins_in, window_in, update, direction, data,
    full, coef, observed, tensor_ref, bins_ref, window, sems
):
    copies = [
        pltpu.make_async_copy(here, there, sems.at[n])
        for n, (here, there) in enumerate(
            (
                (observed_in, observed),
                (tensor_in, tensor_ref),
                (bins_in, bins_ref),
                (window_in, window),
            )
        )
    ]
    for copy in copies:
        copy.start()
    upper = lax.axis_index("core") == 1
    for n, (i, j) in enumerate(BLOCKS):
        part = slice(n % 3 * LANES, (n % 3 + 1) * LANES)
        near, far = mine[part, :], other[part, :]
        block = jnp.where(upper, far, near) if n < 3 else jnp.where(upper, near, far)
        full[i * LANES : (i + 1) * LANES, j * LANES : (j + 1) * LANES] = block
        if i != j:
            full[j * LANES : (j + 1) * LANES, i * LANES : (i + 1) * LANES] = block.T
    eye = lax.broadcasted_iota(jnp.int32, (LANES, LANES), 0) == lane_ids((LANES, LANES))

    def column(row):
        return jnp.concatenate(
            [
                jnp.sum(
                    jnp.where(eye, row[:, j * LANES : (j + 1) * LANES], 0.0), axis=1, keepdims=True
                )
                for j in range(3)
            ],
            axis=0,
        )

    def product(row):
        return jnp.sum(full[...] * column(row), axis=0, keepdims=True)

    def total(row):
        return jnp.sum(row, axis=1, keepdims=True)

    def norm_of(square):
        return jnp.sqrt(square + EPSILON)

    sums, count, rest = stats[0:1, :], stats[1:2, :], stats[2:3, 0:1]
    mean = sums / jnp.maximum(count, 1.0)

    def data_norm(scale, row):
        inside = scale * mean + row
        return norm_of(scale * scale * rest + total(count * inside * inside))

    one = jnp.ones((1, 1), F32)
    row = jnp.zeros((1, ROWS), F32)
    beta = data_norm(one, row)
    beta_first = beta
    scale = one / beta
    raw = scale * sums
    image = product(raw)
    alpha = norm_of(total(raw * image))
    alpha_first = alpha
    model = raw / alpha
    search = model
    answer = jnp.zeros((1, ROWS), F32)
    phi_bar, rho_bar = beta, alpha
    for _ in range(ITERS):
        model_image = image / alpha
        scale, row = -alpha * scale, model_image - alpha * row
        back = scale * sums + count * row
        back_image = product(back)
        beta = data_norm(scale, row)
        inverse = one / beta
        scale, row = scale * inverse, row * inverse
        raw = back * inverse - beta * model
        image = back_image * inverse - beta * model_image
        alpha = norm_of(total(raw * image))
        model = raw / alpha
        rho = jnp.sqrt(rho_bar * rho_bar + beta * beta)
        cosine, sine = rho_bar / rho, beta / rho
        theta = sine * alpha
        rho_bar = -cosine * alpha
        phi = cosine * phi_bar
        phi_bar = sine * phi_bar
        answer = answer + phi / rho * search
        search = model - theta / rho * search
    cell_scale = math.sqrt(PLANES * LANES * math.prod(SIZES.values()))
    coef[0] = jnp.broadcast_to(
        column(answer * (alpha_first * cell_scale / beta_first)), (ROWS, LANES)
    )
    coef[1] = jnp.broadcast_to(column(model * cell_scale), (ROWS, LANES))

    def body(n, totals):
        one, two = tile(cells, 2 * n), tile(cells, 2 * n + 1)
        return (
            totals[0] + coef[0, pl.ds(2 * n, 1), :] * one,
            totals[1] + coef[1, pl.ds(2 * n, 1), :] * one,
            totals[2] + coef[0, pl.ds(2 * n + 1, 1), :] * two,
            totals[3] + coef[1, pl.ds(2 * n + 1, 1), :] * two,
        )

    start = (jnp.zeros((PLANES, LANES), F32),) * 4
    totals = lax.fori_loop(0, ROWS // 2, body, start, unroll=16)
    first, second = totals[0] + totals[2], totals[1] + totals[3]
    update[...] = first
    direction[...] = second

    for copy in copies:
        copy.wait()
    mask = window[...].astype(F32)
    size = math.sqrt(math.prod(observed.shape) * SIZES["xhi"] * SIZES["core"])
    near = pick(column(row * size), bins_ref[...], tensor_ref[...])
    for k in range(2):
        data[k] = (observed[k] * (scale * size) + near[k]) * mask


def chain(mine, other, stats, cells, observed, tensor, bins, window):
    field = jax.ShapeDtypeStruct((PLANES, LANES), F32)
    given = (observed, tensor, bins, window)
    return pl.pallas_call(
        chain_kernel,
        out_shape=(field, field, jax.ShapeDtypeStruct(observed.shape, F32)),
        in_specs=[vmem()] * 4 + [pl.BlockSpec(memory_space=pl.ANY)] * 4,
        out_specs=(vmem(),) * 3,
        scratch_shapes=[pltpu.VMEM((ROWS, ROWS), F32), pltpu.VMEM((2, ROWS, LANES), F32)]
        + [pltpu.VMEM(x.shape, x.dtype) for x in given]
        + [pltpu.SemaphoreType.DMA((4,))],
        compiler_params=pltpu.CompilerParams(vmem_limit_bytes=VMEM_LIMIT),
        name="chain",
    )(mine, other, stats, cells, *given)


def shift(value, axes, step):
    count = math.prod(SIZES[a] for a in axes)
    return lax.ppermute(value, axes, [(i, (i + step) % count) for i in range(count)])


def swap(value, axis):
    return lax.ppermute(value, axis, [(0, 1), (1, 0)])


def exchange(value, axes):
    return lax.all_to_all(value, axes, 0, 0, tiled=True)


def scatter_sum(value, axes):
    count = math.prod(SIZES[a] for a in axes)
    return jnp.sum(exchange(value.reshape(count, -1, LANES), axes), axis=0)


def whole_sum(value, axes):
    count = math.prod(SIZES[a] for a in axes)
    return jnp.sum(exchange(jnp.broadcast_to(value, (count,) + value.shape), axes), axis=0)


def gather(value, axes):
    count = math.prod(SIZES[a] for a in axes)
    return exchange(jnp.broadcast_to(value, (count,) + value.shape), axes).reshape(-1, LANES)


def per_device(
    source_field,
    receiver_tensor,
    metric_ids,
    metric_table,
    observed,
    receiver_index,
    bin_ids,
    window,
):
    src = source_field.reshape(FIELDS, PLANES, LANES)
    receiver = receiver_tensor.reshape(TENSORS, BINS, 12, PLANES, LANES)
    ids = metric_ids.reshape(PLANES, LANES)
    table = metric_table.T
    values = observed.transpose(0, 2, 1)
    tensor = receiver_index.reshape(1, -1)
    bins, marks = bin_ids.T, window.T
    src, y_lo, y_hi, to_core, to_cross, stats, scales = pack(
        src, ids, table, values, tensor, bins, marks
    )
    yb, ya = shift(y_hi, GY, 1), shift(y_lo, GY, -1)
    from_core = swap(to_core, "core")
    x_lo, x_hi, to_cross = strike_faces(src, to_cross, from_core)
    xb, xa = shift(x_hi, GX, 1), shift(x_lo, GX, -1)
    from_cross = lax.ppermute(to_cross, GZ, [(i, 3 - i) for i in range(4)])

    strain, receiver = within(scales, src.reshape(FIELDS * PLANES, LANES), from_core, receiver)
    sums = (stats, from_core, from_cross)
    keep, send, cells, stats = gram(scales, strain, receiver, (xb, xa, yb, ya), sums)
    packed = keep + swap(send, "core")
    packed = scatter_sum(packed, PLANE)
    packed = whole_sum(packed, ("z",))
    packed = gather(packed, PLANE)
    other = swap(packed, "core")
    update, direction, data = chain(packed, other, stats, cells, values, tensor, bins, marks)
    return (
        update.reshape(metric_ids.shape),
        direction.reshape(metric_ids.shape),
        data.transpose(0, 2, 1),
    )


def solution(mesh):
    fine = Mesh(mesh.devices.reshape([SIZES[a] for a in AXES]), AXES)
    return jax.shard_map(
        per_device,
        mesh=fine,
        in_specs=(
            P(None, None, None, GX, GY, GZ),
            P(None, None, None, None, GX, GY, GZ),
            P(GX, GY, GZ),
            P(),
            P(None, GZ, None),
            P(GZ),
            P(GZ, None),
            P(GZ, None),
        ),
        out_specs=(P(GX, GY, GZ), P(GX, GY, GZ), P(None, GZ, None)),
        check_vma=False,
    )
```

```python
import functools
import math

import jax
import jax.numpy as jnp
from jax import lax
from jax.experimental import pallas as pl
from jax.experimental.pallas import tpu as pltpu
from jax.sharding import Mesh, PartitionSpec as P

ITERS = 2
EPSILON = 1e-06
F32 = jnp.float32
BF16 = jnp.bfloat16

AXES = ("y", "z", "xlo", "xhi", "core")
SIZES = {"y": 4, "z": 8, "xlo": 2, "xhi": 2, "core": 2}
GX = ("y",)
GY = ("z", "xlo")
GZ = ("xhi", "core")
PLANE = ("y", "xlo", "xhi")
VMEM_LIMIT = 16 * 1024 * 1024

BINS = 16
TENSORS = 12
FIELDS = 96
PLANES = 16
LANES = 128
DENSE = 24
ROWS = 384
BLOCKS = ((0, 0), (0, 1), (0, 2), (1, 1), (1, 2), (2, 2))


def vmem():
    return pl.BlockSpec(memory_space=pltpu.VMEM)


def in_hbm(value):
    return pltpu.with_memory_space_constraint(value, pltpu.HBM)


def hbm():
    return pl.BlockSpec(memory_space=pltpu.HBM)


def lane_ids(shape):
    return lax.broadcasted_iota(jnp.int32, shape, len(shape) - 1)


def spread(values, bins, tensor):
    parts = []
    for b in range(BINS):
        here = bins == b
        for k in range(2):
            if k == 0 or len(values) == 2:
                part = jnp.sum(jnp.where(here, values[k], 0.0), axis=0, keepdims=True)
            parts.append(part)
    table = jnp.concatenate(parts, axis=0)
    return jnp.concatenate(
        [
            jnp.sum(jnp.where(tensor == r, table, 0.0), axis=1, keepdims=True)
            for r in range(TENSORS)
        ],
        axis=0,
    )


def pick(column, bins, tensor):
    table = jnp.zeros((2 * BINS, bins.shape[1]), F32)
    for r in range(TENSORS):
        table = jnp.where(tensor == r, column[r * 32 : (r + 1) * 32, :], table)
    out = [jnp.zeros(bins.shape, F32), jnp.zeros(bins.shape, F32)]
    for b in range(BINS):
        here = bins == b
        for k in range(2):
            out[k] = jnp.where(here, table[2 * b + k : 2 * b + k + 1, :], out[k])
    return out


def data_sums(observed, tensor, bins, window):
    mask = window.astype(F32)
    rhs = [observed[k] * mask for k in range(2)]
    total = spread(rhs, bins, tensor)
    count = spread([mask], bins, tensor)
    mean = total / jnp.maximum(count, 1.0)
    near = pick(mean, bins, tensor)
    rest = [rhs[k] - near[k] * mask for k in range(2)]
    square = jnp.sum(rest[0] * rest[0] + rest[1] * rest[1], axis=(0, 1), keepdims=True)
    lane = lane_ids((ROWS, LANES))
    wide = jnp.where(lane == 0, total, jnp.where(lane == 1, count, square))
    part = [wide[j * LANES : (j + 1) * LANES, :].T[:8] for j in range(3)]
    rows = [part[j][k : k + 1] for k in range(2) for j in range(3)] + [part[0][2:3]] * 2
    return jnp.concatenate(rows, axis=0)


def sums_of(value):
    total = jnp.concatenate([value[j : j + 1, :] for j in range(3)], axis=1)
    count = jnp.concatenate([value[j : j + 1, :] for j in range(3, 6)], axis=1)
    return jnp.concatenate([total, count, jnp.concatenate([value[6:7, :]] * 3, axis=1)], axis=0)


def merge_sums(one, two):
    total, count = one[0:1] + two[0:1], one[1:2] + two[1:2]
    gap = one[0:1] / jnp.maximum(one[1:2], 1.0) - two[0:1] / jnp.maximum(two[1:2], 1.0)
    apart = jnp.sum(
        one[1:2] * two[1:2] / jnp.maximum(count, 1.0) * gap * gap, axis=1, keepdims=True
    )
    rest = one[2:3] + two[2:3] + apart
    return jnp.concatenate([total, count, rest, jnp.zeros((5, ROWS), F32)], axis=0)


def pack_kernel(
    src_in, ids_in, table_in, observed_in, tensor_in, bins_in, window_in,
    src, to_side, to_pair, to_core, to_cross, stats, scales,
    ids, table, observed, tensor, bins, window, sparse, sems,
):
    copies = [
        pltpu.make_async_copy(here, there, sems.at[n])
        for n, (here, there) in enumerate(
            (
                (src_in, src),
                (ids_in, ids),
                (table_in, table),
                (observed_in, observed),
                (tensor_in, tensor),
                (bins_in, bins),
                (window_in, window),
            )
        )
    ]
    for copy in copies[1:] + copies[:1]:
        copy.start()
    for copy in copies[1:]:
        copy.wait()
    for p in range(3):
        scale = jnp.zeros((PLANES, LANES), F32)
        for m in range(8):
            scale = jnp.where(ids[...] == m, table[p, m], scale)
        scales[p * PLANES : (p + 1) * PLANES, :] = scale * (1.0 / 12.0)
    sums = data_sums(observed, tensor[...], bins[...], window[...])
    stats[...] = sums
    to_core[DENSE:, :] = sums
    to_cross[DENSE:, :] = sums

    copies[0].wait()
    y = lax.broadcasted_iota(jnp.int32, (FIELDS, 8, LANES), 1) & 3
    first, second = src[:, 0:8, :], src[:, 8:16, :]
    low = [
        jnp.where(y == 1, 8.0 * pltpu.roll(half, 1, 1), 0.0) - half for half in (first, second)
    ]
    high = [
        half - jnp.where(y == 2, 8.0 * pltpu.roll(half, 7, 1), 0.0) for half in (first, second)
    ]
    lower = jnp.where(y < 2, low[1], pltpu.roll(low[0], 2, 1))
    higher = jnp.where(y < 2, pltpu.roll(high[0], 6, 1), pltpu.roll(high[1], 4, 1))
    odd = lax.axis_index("xlo") == 1
    to_side[...] = jnp.where(odd, higher, lower)
    to_pair[...] = jnp.where(odd, lower, higher)

    lane = lane_ids((FIELDS, LANES))
    low = jnp.zeros((FIELDS, LANES), F32)
    high = jnp.zeros((FIELDS, LANES), F32)
    for plane in range(PLANES):
        value = src[:, plane, :]
        turned = pltpu.roll(value, 8 * plane, 1) if plane else value
        place = (lane - 8 * plane) & (LANES - 1)
        low = jnp.where(place < 2, turned, low)
        high = jnp.where(place >= LANES - 2, turned, high)
    place = lane & 7
    low = jnp.where(place == 1, 8.0 * pltpu.roll(low, 1, 1), 0.0) - low
    high = high - jnp.where(place == 6, 8.0 * pltpu.roll(high, LANES - 1, 1), 0.0)
    high = pltpu.roll(high, 2, 1)
    upper = lax.axis_index("core") == 1
    to_core[:DENSE, :] = dense(jnp.where(upper, low, high), sparse)
    to_cross[:DENSE, :] = dense(jnp.where(upper, high, low), sparse)


def dense(value, sparse):
    sparse[...] = value
    lane = lane_ids((DENSE, LANES)) & 7
    out = jnp.zeros((DENSE, LANES), F32)
    for n in range(4):
        part = sparse[pl.ds(n, DENSE, stride=4), :]
        out = jnp.where(lane >> 1 == n, pltpu.roll(part, 2 * n, 1) if n else part, out)
    return out


def spread_out(value, sparse, lower):
    lane = lane_ids((DENSE, LANES)) & 7
    for n in range(4):
        part = pltpu.roll(value, LANES - 2 * n, 1) if n else value
        part = jnp.where(lane < 2, part, 0.0)
        sparse[pl.ds(n, DENSE, stride=4), :] = jnp.where(
            lower, part, pltpu.roll(part, LANES - 2, 1)
        )
    return sparse[...]


def pack(src, ids, table, observed, tensor, bins, window):
    face = jax.ShapeDtypeStruct((FIELDS, 8, LANES), F32)
    ends = jax.ShapeDtypeStruct((DENSE + 8, LANES), F32)
    given = (src, ids, table, observed, tensor, bins, window)
    return pl.pallas_call(
        pack_kernel,
        out_shape=(
            jax.ShapeDtypeStruct(src.shape, F32),
            face,
            face,
            ends,
            ends,
            jax.ShapeDtypeStruct((8, LANES), F32),
            jax.ShapeDtypeStruct((3 * PLANES, LANES), F32),
        ),
        in_specs=[hbm()] * 7,
        out_specs=(vmem(),) * 7,
        scratch_shapes=[pltpu.VMEM(ids.shape, ids.dtype), pltpu.SMEM(table.shape, table.dtype)]
        + [pltpu.VMEM(x.shape, x.dtype) for x in given[3:]]
        + [pltpu.VMEM((FIELDS, LANES), F32), pltpu.SemaphoreType.DMA((7,))],
        compiler_params=pltpu.CompilerParams(vmem_limit_bytes=VMEM_LIMIT),
        name="pack",
    )(*(in_hbm(x) for x in given))


def strike_kernel(src, part, from_core, x_lo, x_hi, to_cross):
    to_cross[: DENSE + 8, :] = part[...]
    to_cross[DENSE + 8 :, :] = from_core[DENSE:, :]
    first, second = src[:, 0:8, :], src[:, 8:16, :]
    row = lax.broadcasted_iota(jnp.int32, (FIELDS, 8, LANES), 1)
    x_lo[...] = jnp.where(row < 4, 0.0, 8.0 * pltpu.roll(first, 4, 1)) - first
    x_hi[...] = second - jnp.where(row < 4, 8.0 * pltpu.roll(second, 4, 1), 0.0)


def strike_faces(src, part, from_core):
    face = jax.ShapeDtypeStruct((FIELDS, 8, LANES), F32)
    return pl.pallas_call(
        strike_kernel,
        out_shape=(face, face, jax.ShapeDtypeStruct((DENSE + 16, LANES), F32)),
        in_specs=[vmem()] * 3,
        out_specs=(vmem(),) * 3,
        compiler_params=pltpu.CompilerParams(vmem_limit_bytes=VMEM_LIMIT),
        name="strike_faces",
    )(src, part, from_core)


def ends_of(axes):
    at = lax.axis_index(axes)
    last = math.prod(SIZES[a] for a in axes) - 1
    return jnp.where(at > 0, 1.0, 0.0).astype(F32), jnp.where(at < last, 1.0, 0.0).astype(F32)


def tile(ref, at):
    return ref[pl.ds(pl.multiple_of(at * PLANES, PLANES), PLANES), :]


def set_tile(ref, at, value):
    ref[pl.ds(pl.multiple_of(at * PLANES, PLANES), PLANES), :] = value


def within_kernel(
    scales, src, from_core, receiver_in, strain, receiver, grads, slots, sparse, sems
):
    def fetch(b):
        return pltpu.make_async_copy(receiver_in.at[:, b], slots.at[b], sems.at[b])

    for b in range(BINS):
        fetch(b).start()
    lane = lane_ids((FIELDS, LANES))
    halo = spread_out(from_core[:DENSE, :], sparse, lax.axis_index("core") == 1)

    def at(x, y):
        if min(x, y) < 0 or max(x, y) > 3:
            return 0.0
        return src[pl.ds(x * 4 + y, FIELDS, stride=PLANES), :]

    def put(p, plane, value):
        grads[pl.ds(p * FIELDS * PLANES + plane, FIELDS, stride=PLANES), :] = value

    for x in range(4):
        for y in range(4):
            plane = x * 4 + y
            put(0, plane, 8.0 * (at(x + 1, y) - at(x - 1, y)) - (at(x + 2, y) - at(x - 2, y)))
            put(1, plane, 8.0 * (at(x, y + 1) - at(x, y - 1)) - (at(x, y + 2) - at(x, y - 2)))
            mid = at(x, y)
            later = jnp.where(lane < LANES - 1, pltpu.roll(mid, LANES - 1, 1), 0.0)
            sooner = jnp.where(lane > 0, pltpu.roll(mid, 1, 1), 0.0)
            later_two = jnp.where(lane < LANES - 2, pltpu.roll(mid, LANES - 2, 1), 0.0)
            sooner_two = jnp.where(lane > 1, pltpu.roll(mid, 2, 1), 0.0)
            value = 8.0 * (later - sooner) - (later_two - sooner_two)
            put(2, plane, value + ends_at(halo, plane, lane))

    def body(b, carry):
        def grad(p, q, k):
            return tile(scales, p) * tile(grads, p * FIELDS + b * 6 + q * 2 + k)

        for k in range(2):
            for j, value in enumerate(
                (
                    grad(0, 0, k),
                    grad(1, 1, k),
                    grad(2, 2, k),
                    grad(1, 2, k) + grad(2, 1, k),
                    grad(0, 2, k) + grad(2, 0, k),
                    grad(0, 1, k) + grad(1, 0, k),
                )
            ):
                set_tile(strain, b * 12 + j * 2 + k, value)
        fetch(b).wait()
        for r in range(TENSORS):
            receiver[r, b] = slots[b, r].astype(F32)
        return carry

    lax.fori_loop(0, BINS, body, 0)


def ends_at(halo, plane, lane):
    turned = pltpu.roll(halo, LANES - 8 * plane, 1) if plane else halo
    return jnp.where((lane < 2) | (lane >= LANES - 2), turned, 0.0)


def within(scales, src, from_core, receiver):
    return pl.pallas_call(
        within_kernel,
        out_shape=(
            jax.ShapeDtypeStruct((BINS * 12 * PLANES, LANES), F32),
            jax.ShapeDtypeStruct(receiver.shape, F32),
        ),
        in_specs=[vmem(), vmem(), vmem(), hbm()],
        out_specs=(vmem(), vmem()),
        scratch_shapes=[
            pltpu.VMEM((3 * FIELDS * PLANES, LANES), F32),
            pltpu.VMEM((BINS, TENSORS, 12, PLANES, LANES), BF16),
            pltpu.VMEM((FIELDS, LANES), F32),
            pltpu.SemaphoreType.DMA((BINS,)),
        ],
        compiler_params=pltpu.CompilerParams(vmem_limit_bytes=VMEM_LIMIT),
        cost_estimate=pl.CostEstimate(
            flops=4_000_000, bytes_accessed=14_000_000, transcendentals=0
        ),
        name="within",
    )(scales, src, from_core, in_hbm(receiver))


def gram_kernel(
    scales, within, receiver, xb, xa, from_side, from_pair, own, from_core, from_cross,
    keep, send, cells, stats, ends, sparse
):
    lane = lane_ids((FIELDS, LANES))
    crossing = jnp.where(lax.axis_index("xhi") != lax.axis_index("core"), 1.0, 0.0).astype(F32)
    lower = lax.axis_index("core") == 0
    halo = spread_out(from_cross[:DENSE, :] * crossing, sparse, lower)
    for plane in range(PLANES):
        ends[pl.ds(plane, FIELDS, stride=PLANES), :] = ends_at(halo, plane, lane)
    x_before, x_after = ends_of(GX)
    y_before, y_after = ends_of(GY)
    low_y = (lax.broadcasted_iota(jnp.int32, (8, LANES), 0) & 3) < 2
    inside = jnp.where(low_y, y_before, y_after)
    of_pair = low_y == (lax.axis_index("xlo") == 1)
    scale_x = (scales[0:8, :] * x_before, scales[8:16, :] * x_after)
    scale_y = (scales[16:24, :] * inside, scales[24:32, :] * inside)
    scale_z = tile(scales, 2)

    def body(b, carry):
        def from_x(field):
            return jnp.concatenate([scale_x[0] * xb[field], scale_x[1] * xa[field]], axis=0)

        def from_y(field):
            side, pair = from_side[field], from_pair[field]
            first = jnp.where(of_pair, pair, side)
            second = pltpu.roll(jnp.where(of_pair, side, pair), 2, 0)
            return jnp.concatenate([scale_y[0] * first, scale_y[1] * second], axis=0)

        def from_z(field):
            return scale_z * tile(ends, field)

        strain = []
        for k in range(2):
            inner = [tile(within, b * 12 + j * 2 + k) for j in range(6)]
            ux, uy, uz = [b * 6 + q * 2 + k for q in range(3)]
            strain.append(
                (
                    inner[0] + from_x(ux),
                    inner[1] + from_y(uy),
                    inner[2] + from_z(uz),
                    inner[3] + (from_y(uz) + from_z(uy)),
                    inner[4] + (from_x(uz) + from_z(ux)),
                    inner[5] + (from_x(uy) + from_y(ux)),
                )
            )
        real, imag = strain
        for r in range(TENSORS):
            re = im = None
            for j in range(6):
                rec_re, rec_im = receiver[r, b, 2 * j], receiver[r, b, 2 * j + 1]
                add_re = rec_re * real[j] - rec_im * imag[j]
                add_im = rec_re * imag[j] + rec_im * real[j]
                re, im = (re + add_re, im + add_im) if j else (add_re, add_im)
            set_tile(cells, r * 32 + b * 2, re)
            set_tile(cells, r * 32 + b * 2 + 1, im)
        return carry

    lax.fori_loop(0, BINS, body, 0)

    total = jnp.zeros((ROWS, ROWS), F32)
    for plane in range(0, PLANES, 4):
        both = jnp.concatenate(
            [cells[pl.ds(plane + i, ROWS, stride=PLANES), :] for i in range(4)], axis=1
        )
        high = both.astype(BF16)
        low = (both - high.astype(F32)).astype(BF16)
        left = jnp.concatenate([high, high], axis=1)
        right = jnp.concatenate([high * BF16(0.5), low], axis=1)
        total = total + lax.dot_general(
            left, right, (((1,), (1,)), ((), ())), preferred_element_type=F32
        )

    def block(i, j):
        return total[i * LANES : (i + 1) * LANES, j * LANES : (j + 1) * LANES]

    full = [block(i, j) + block(j, i).T for i, j in BLOCKS]
    upper = lax.axis_index("core") == 1
    for n in range(3):
        part = slice(n * LANES, (n + 1) * LANES)
        keep[part, :] = jnp.where(upper, full[n + 3], full[n])
        send[part, :] = jnp.where(upper, full[n], full[n + 3])

    stats[...] = merge_sums(
        merge_sums(sums_of(own[...]), sums_of(from_core[DENSE:, :])),
        merge_sums(
            sums_of(from_cross[DENSE : DENSE + 8, :]), sums_of(from_cross[DENSE + 8 :, :])
        ),
    )


def gram(scales, within, receiver, halos, sums):
    half = jax.ShapeDtypeStruct((3 * LANES, LANES), F32)
    return pl.pallas_call(
        gram_kernel,
        out_shape=(
            half,
            half,
            jax.ShapeDtypeStruct((ROWS * PLANES, LANES), F32),
            jax.ShapeDtypeStruct((8, ROWS), F32),
        ),
        in_specs=[vmem()] * 10,
        out_specs=(vmem(),) * 4,
        scratch_shapes=[
            pltpu.VMEM((FIELDS * PLANES, LANES), F32),
            pltpu.VMEM((FIELDS, LANES), F32),
        ],
        compiler_params=pltpu.CompilerParams(vmem_limit_bytes=VMEM_LIMIT),
        cost_estimate=pl.CostEstimate(
            flops=1_200_000_000, bytes_accessed=8_000_000, transcendentals=0
        ),
        name="gram",
    )(scales, within, receiver, *halos, *sums)


def chain_kernel(
    mine, other, stats, cells, observed_in, tensor_in, bins_in, window_in, update, direction, data,
    full, coef, observed, tensor_ref, bins_ref, window, sems
):
    copies = [
        pltpu.make_async_copy(here, there, sems.at[n])
        for n, (here, there) in enumerate(
            (
                (observed_in, observed),
                (tensor_in, tensor_ref),
                (bins_in, bins_ref),
                (window_in, window),
            )
        )
    ]
    for copy in copies:
        copy.start()
    upper = lax.axis_index("core") == 1
    for n, (i, j) in enumerate(BLOCKS):
        part = slice(n % 3 * LANES, (n % 3 + 1) * LANES)
        near, far = mine[part, :], other[part, :]
        block = jnp.where(upper, far, near) if n < 3 else jnp.where(upper, near, far)
        full[i * LANES : (i + 1) * LANES, j * LANES : (j + 1) * LANES] = block
        if i != j:
            full[j * LANES : (j + 1) * LANES, i * LANES : (i + 1) * LANES] = block.T
    eye = lax.broadcasted_iota(jnp.int32, (LANES, LANES), 0) == lane_ids((LANES, LANES))

    def column(row):
        return jnp.concatenate(
            [
                jnp.sum(
                    jnp.where(eye, row[:, j * LANES : (j + 1) * LANES], 0.0), axis=1, keepdims=True
                )
                for j in range(3)
            ],
            axis=0,
        )

    def product(row):
        return jnp.sum(full[...] * column(row), axis=0, keepdims=True)

    def total(row):
        return jnp.sum(row, axis=1, keepdims=True)

    def norm_of(square):
        return jnp.sqrt(square + EPSILON)

    sums, count, rest = stats[0:1, :], stats[1:2, :], stats[2:3, 0:1]
    mean = sums / jnp.maximum(count, 1.0)

    def data_norm(scale, row):
        inside = scale * mean + row
        return norm_of(scale * scale * rest + total(count * inside * inside))

    one = jnp.ones((1, 1), F32)
    row = jnp.zeros((1, ROWS), F32)
    beta = data_norm(one, row)
    beta_first = beta
    scale = one / beta
    raw = scale * sums
    image = product(raw)
    alpha = norm_of(total(raw * image))
    alpha_first = alpha
    model = raw / alpha
    search = model
    answer = jnp.zeros((1, ROWS), F32)
    phi_bar, rho_bar = beta, alpha
    for _ in range(ITERS):
        model_image = image / alpha
        scale, row = -alpha * scale, model_image - alpha * row
        back = scale * sums + count * row
        back_image = product(back)
        beta = data_norm(scale, row)
        inverse = one / beta
        scale, row = scale * inverse, row * inverse
        raw = back * inverse - beta * model
        image = back_image * inverse - beta * model_image
        alpha = norm_of(total(raw * image))
        model = raw / alpha
        rho = jnp.sqrt(rho_bar * rho_bar + beta * beta)
        cosine, sine = rho_bar / rho, beta / rho
        theta = sine * alpha
        rho_bar = -cosine * alpha
        phi = cosine * phi_bar
        phi_bar = sine * phi_bar
        answer = answer + phi / rho * search
        search = model - theta / rho * search
    cell_scale = math.sqrt(PLANES * LANES * math.prod(SIZES.values()))
    coef[0] = jnp.broadcast_to(
        column(answer * (alpha_first * cell_scale / beta_first)), (ROWS, LANES)
    )
    coef[1] = jnp.broadcast_to(column(model * cell_scale), (ROWS, LANES))

    def body(n, totals):
        one, two = tile(cells, 2 * n), tile(cells, 2 * n + 1)
        return (
            totals[0] + coef[0, pl.ds(2 * n, 1), :] * one,
            totals[1] + coef[1, pl.ds(2 * n, 1), :] * one,
            totals[2] + coef[0, pl.ds(2 * n + 1, 1), :] * two,
            totals[3] + coef[1, pl.ds(2 * n + 1, 1), :] * two,
        )

    start = (jnp.zeros((PLANES, LANES), F32),) * 4
    totals = lax.fori_loop(0, ROWS // 2, body, start, unroll=16)
    first, second = totals[0] + totals[2], totals[1] + totals[3]
    update[...] = first
    direction[...] = second

    for copy in copies:
        copy.wait()
    mask = window[...].astype(F32)
    size = math.sqrt(math.prod(observed.shape) * SIZES["xhi"] * SIZES["core"])
    near = pick(column(row * size), bins_ref[...], tensor_ref[...])
    for k in range(2):
        data[k] = (observed[k] * (scale * size) + near[k]) * mask


def chain(mine, other, stats, cells, observed, tensor, bins, window):
    field = jax.ShapeDtypeStruct((PLANES, LANES), F32)
    given = (observed, tensor, bins, window)
    return pl.pallas_call(
        chain_kernel,
        out_shape=(field, field, jax.ShapeDtypeStruct(observed.shape, F32)),
        in_specs=[vmem()] * 4 + [pl.BlockSpec(memory_space=pl.ANY)] * 4,
        out_specs=(vmem(),) * 3,
        scratch_shapes=[pltpu.VMEM((ROWS, ROWS), F32), pltpu.VMEM((2, ROWS, LANES), F32)]
        + [pltpu.VMEM(x.shape, x.dtype) for x in given]
        + [pltpu.SemaphoreType.DMA((4,))],
        compiler_params=pltpu.CompilerParams(vmem_limit_bytes=VMEM_LIMIT),
        name="chain",
    )(mine, other, stats, cells, *given)


def shift(value, axes, step):
    count = math.prod(SIZES[a] for a in axes)
    return lax.ppermute(value, axes, [(i, (i + step) % count) for i in range(count)])


def swap(value, axis):
    return lax.ppermute(value, axis, [(0, 1), (1, 0)])


def exchange(value, axes):
    return lax.all_to_all(value, axes, 0, 0, tiled=True)


def scatter_sum(value, axes):
    count = math.prod(SIZES[a] for a in axes)
    return jnp.sum(exchange(value.reshape(count, -1, LANES), axes), axis=0)


def whole_sum(value, axes):
    count = math.prod(SIZES[a] for a in axes)
    return jnp.sum(exchange(jnp.broadcast_to(value, (count,) + value.shape), axes), axis=0)


def gather(value, axes):
    count = math.prod(SIZES[a] for a in axes)
    return exchange(jnp.broadcast_to(value, (count,) + value.shape), axes).reshape(-1, LANES)


def per_device(
    source_field,
    receiver_tensor,
    metric_ids,
    metric_table,
    observed,
    receiver_index,
    bin_ids,
    window,
):
    src = source_field.reshape(FIELDS, PLANES, LANES)
    receiver = receiver_tensor.reshape(TENSORS, BINS, 12, PLANES, LANES)
    ids = metric_ids.reshape(PLANES, LANES)
    table = metric_table.T
    values = observed.transpose(0, 2, 1)
    tensor = receiver_index.reshape(1, -1)
    bins, marks = bin_ids.T, window.T
    src, to_side, to_pair, to_core, to_cross, stats, scales = pack(
        src, ids, table, values, tensor, bins, marks
    )
    count = math.prod(SIZES[a] for a in GY)
    ring = [(i, (i + 1 if i % 2 else i - 1) % count) for i in range(count)]
    from_side, from_pair = lax.ppermute(to_side, GY, ring), swap(to_pair, "xlo")
    from_core = swap(to_core, "core")
    x_lo, x_hi, to_cross = strike_faces(src, to_cross, from_core)
    xb, xa = shift(x_hi, GX, 1), shift(x_lo, GX, -1)
    from_cross = lax.ppermute(to_cross, GZ, [(i, 3 - i) for i in range(4)])

    strain, receiver = within(scales, src.reshape(FIELDS * PLANES, LANES), from_core, receiver)
    sums = (stats, from_core, from_cross)
    keep, send, cells, stats = gram(scales, strain, receiver, (xb, xa, from_side, from_pair), sums)
    packed = keep + swap(send, "core")
    packed = scatter_sum(packed, PLANE)
    packed = whole_sum(packed, ("z",))
    packed = gather(packed, PLANE)
    other = swap(packed, "core")
    update, direction, data = chain(packed, other, stats, cells, values, tensor, bins, marks)
    return (
        update.reshape(metric_ids.shape),
        direction.reshape(metric_ids.shape),
        data.transpose(0, 2, 1),
    )


def solution(mesh):
    fine = Mesh(mesh.devices.reshape([SIZES[a] for a in AXES]), AXES)
    return jax.shard_map(
        per_device,
        mesh=fine,
        in_specs=(
            P(None, None, None, GX, GY, GZ),
            P(None, None, None, None, GX, GY, GZ),
            P(GX, GY, GZ),
            P(),
            P(None, GZ, None),
            P(GZ),
            P(GZ, None),
            P(GZ, None),
        ),
        out_specs=(P(GX, GY, GZ), P(GX, GY, GZ), P(None, GZ, None)),
        check_vma=False,
    )
```

```python
import functools
import math

import jax
import jax.numpy as jnp
from jax import lax
from jax.experimental import pallas as pl
from jax.experimental.pallas import tpu as pltpu
from jax.sharding import Mesh, PartitionSpec as P

ITERS = 2
EPSILON = 1e-06
F32 = jnp.float32
BF16 = jnp.bfloat16

AXES = ("y", "z", "xlo", "xhi", "core")
SIZES = {"y": 4, "z": 8, "xlo": 2, "xhi": 2, "core": 2}
GX = ("y",)
GY = ("z", "xlo")
GZ = ("xhi", "core")
PLANE = ("xlo", "xhi", "y")
VMEM_LIMIT = 16 * 1024 * 1024

BINS = 16
TENSORS = 12
FIELDS = 96
PLANES = 16
LANES = 128
DENSE = 24
ROWS = 384
BLOCKS = ((0, 0), (0, 1), (0, 2), (1, 1), (1, 2), (2, 2))


def vmem():
    return pl.BlockSpec(memory_space=pltpu.VMEM)


def in_hbm(value):
    return pltpu.with_memory_space_constraint(value, pltpu.HBM)


def hbm():
    return pl.BlockSpec(memory_space=pltpu.HBM)


def lane_ids(shape):
    return lax.broadcasted_iota(jnp.int32, shape, len(shape) - 1)


def spread(values, bins, tensor):
    parts = []
    for b in range(BINS):
        here = bins == b
        for k in range(2):
            if k == 0 or len(values) == 2:
                part = jnp.sum(jnp.where(here, values[k], 0.0), axis=0, keepdims=True)
            parts.append(part)
    table = jnp.concatenate(parts, axis=0)
    return jnp.concatenate(
        [
            jnp.sum(jnp.where(tensor == r, table, 0.0), axis=1, keepdims=True)
            for r in range(TENSORS)
        ],
        axis=0,
    )


def pick(column, bins, tensor):
    table = jnp.zeros((2 * BINS, bins.shape[1]), F32)
    for r in range(TENSORS):
        table = jnp.where(tensor == r, column[r * 32 : (r + 1) * 32, :], table)
    out = [jnp.zeros(bins.shape, F32), jnp.zeros(bins.shape, F32)]
    for b in range(BINS):
        here = bins == b
        for k in range(2):
            out[k] = jnp.where(here, table[2 * b + k : 2 * b + k + 1, :], out[k])
    return out


def data_sums(observed, tensor, bins, window):
    mask = window.astype(F32)
    rhs = [observed[k] * mask for k in range(2)]
    total = spread(rhs, bins, tensor)
    count = spread([mask], bins, tensor)
    mean = total / jnp.maximum(count, 1.0)
    near = pick(mean, bins, tensor)
    rest = [rhs[k] - near[k] * mask for k in range(2)]
    square = jnp.sum(rest[0] * rest[0] + rest[1] * rest[1], axis=(0, 1), keepdims=True)
    lane = lane_ids((ROWS, LANES))
    wide = jnp.where(lane == 0, total, jnp.where(lane == 1, count, square))
    part = [wide[j * LANES : (j + 1) * LANES, :].T[:8] for j in range(3)]
    rows = [part[j][k : k + 1] for k in range(2) for j in range(3)] + [part[0][2:3]] * 2
    return jnp.concatenate(rows, axis=0)


def sums_of(value):
    total = jnp.concatenate([value[j : j + 1, :] for j in range(3)], axis=1)
    count = jnp.concatenate([value[j : j + 1, :] for j in range(3, 6)], axis=1)
    return jnp.concatenate([total, count, jnp.concatenate([value[6:7, :]] * 3, axis=1)], axis=0)


def merge_sums(one, two):
    total, count = one[0:1] + two[0:1], one[1:2] + two[1:2]
    gap = one[0:1] / jnp.maximum(one[1:2], 1.0) - two[0:1] / jnp.maximum(two[1:2], 1.0)
    apart = jnp.sum(
        one[1:2] * two[1:2] / jnp.maximum(count, 1.0) * gap * gap, axis=1, keepdims=True
    )
    rest = one[2:3] + two[2:3] + apart
    return jnp.concatenate([total, count, rest, jnp.zeros((5, ROWS), F32)], axis=0)


def pack_kernel(
    src_in, ids_in, table_in, observed_in, tensor_in, bins_in, window_in,
    src, to_side, to_pair, to_core, to_cross, stats, scales,
    ids, table, observed, tensor, bins, window, sparse, sems,
):
    copies = [
        pltpu.make_async_copy(here, there, sems.at[n])
        for n, (here, there) in enumerate(
            (
                (src_in, src),
                (ids_in, ids),
                (table_in, table),
                (observed_in, observed),
                (tensor_in, tensor),
                (bins_in, bins),
                (window_in, window),
            )
        )
    ]
    for copy in copies[1:] + copies[:1]:
        copy.start()
    for copy in copies[1:]:
        copy.wait()
    for p in range(3):
        scale = jnp.zeros((PLANES, LANES), F32)
        for m in range(8):
            scale = jnp.where(ids[...] == m, table[p, m], scale)
        scales[p * PLANES : (p + 1) * PLANES, :] = scale * (1.0 / 12.0)
    sums = data_sums(observed, tensor[...], bins[...], window[...])
    stats[...] = sums
    to_core[DENSE:, :] = sums
    to_cross[DENSE:, :] = sums

    copies[0].wait()
    y = lax.broadcasted_iota(jnp.int32, (FIELDS, 8, LANES), 1) & 3
    first, second = src[:, 0:8, :], src[:, 8:16, :]
    low = [
        jnp.where(y == 1, 8.0 * pltpu.roll(half, 1, 1), 0.0) - half for half in (first, second)
    ]
    high = [
        half - jnp.where(y == 2, 8.0 * pltpu.roll(half, 7, 1), 0.0) for half in (first, second)
    ]
    lower = jnp.where(y < 2, low[1], pltpu.roll(low[0], 2, 1))
    higher = jnp.where(y < 2, pltpu.roll(high[0], 6, 1), pltpu.roll(high[1], 4, 1))
    odd = lax.axis_index("xlo") == 1
    to_side[...] = jnp.where(odd, higher, lower)
    to_pair[...] = jnp.where(odd, lower, higher)

    lane = lane_ids((FIELDS, LANES))
    ends = lane_ids((1, LANES))
    ends = jnp.where((ends < 2) | (ends >= LANES - 2), 1.0, 0.0).astype(F32)
    packed = jnp.zeros((FIELDS, LANES), F32)
    for plane in range(PLANES):
        value = src[:, plane, :] * ends
        packed = packed + (pltpu.roll(value, 8 * plane, 1) if plane else value)
    place = lane & 7
    low = jnp.where(place < 2, packed, 0.0)
    high = jnp.where(place >= 6, packed, 0.0)
    low = jnp.where(place == 1, 8.0 * pltpu.roll(low, 1, 1), 0.0) - low
    high = high - jnp.where(place == 6, 8.0 * pltpu.roll(high, LANES - 1, 1), 0.0)
    high = pltpu.roll(high, 2, 1)
    upper = lax.axis_index("core") == 1
    to_core[:DENSE, :] = dense(jnp.where(upper, low, high), sparse)
    to_cross[:DENSE, :] = dense(jnp.where(upper, high, low), sparse)


def dense(value, sparse):
    sparse[...] = value
    lane = lane_ids((DENSE, LANES)) & 7
    out = jnp.zeros((DENSE, LANES), F32)
    for n in range(4):
        part = sparse[pl.ds(n, DENSE, stride=4), :]
        out = jnp.where(lane >> 1 == n, pltpu.roll(part, 2 * n, 1) if n else part, out)
    return out


def spread_out(value, sparse, lower):
    lane = lane_ids((DENSE, LANES)) & 7
    for n in range(4):
        part = pltpu.roll(value, LANES - 2 * n, 1) if n else value
        part = jnp.where(lane < 2, part, 0.0)
        sparse[pl.ds(n, DENSE, stride=4), :] = jnp.where(
            lower, part, pltpu.roll(part, LANES - 2, 1)
        )
    return sparse[...]


def pack(src, ids, table, observed, tensor, bins, window):
    face = jax.ShapeDtypeStruct((FIELDS, 8, LANES), F32)
    ends = jax.ShapeDtypeStruct((DENSE + 8, LANES), F32)
    given = (src, ids, table, observed, tensor, bins, window)
    return pl.pallas_call(
        pack_kernel,
        out_shape=(
            jax.ShapeDtypeStruct(src.shape, F32),
            face,
            face,
            ends,
            ends,
            jax.ShapeDtypeStruct((8, LANES), F32),
            jax.ShapeDtypeStruct((3 * PLANES, LANES), F32),
        ),
        in_specs=[hbm()] * 7,
        out_specs=(vmem(),) * 7,
        scratch_shapes=[pltpu.VMEM(ids.shape, ids.dtype), pltpu.SMEM(table.shape, table.dtype)]
        + [pltpu.VMEM(x.shape, x.dtype) for x in given[3:]]
        + [pltpu.VMEM((FIELDS, LANES), F32), pltpu.SemaphoreType.DMA((7,))],
        compiler_params=pltpu.CompilerParams(vmem_limit_bytes=VMEM_LIMIT),
        name="pack",
    )(*(in_hbm(x) for x in given))


def strike_kernel(src, part, from_core, x_lo, x_hi, to_cross):
    to_cross[: DENSE + 8, :] = part[...]
    to_cross[DENSE + 8 :, :] = from_core[DENSE:, :]
    first, second = src[:, 0:8, :], src[:, 8:16, :]
    row = lax.broadcasted_iota(jnp.int32, (FIELDS, 8, LANES), 1)
    x_lo[...] = jnp.where(row < 4, 0.0, 8.0 * pltpu.roll(first, 4, 1)) - first
    x_hi[...] = second - jnp.where(row < 4, 8.0 * pltpu.roll(second, 4, 1), 0.0)


def strike_faces(src, part, from_core):
    face = jax.ShapeDtypeStruct((FIELDS, 8, LANES), F32)
    return pl.pallas_call(
        strike_kernel,
        out_shape=(face, face, jax.ShapeDtypeStruct((DENSE + 16, LANES), F32)),
        in_specs=[vmem()] * 3,
        out_specs=(vmem(),) * 3,
        compiler_params=pltpu.CompilerParams(vmem_limit_bytes=VMEM_LIMIT),
        name="strike_faces",
    )(src, part, from_core)


def ends_of(axes):
    at = lax.axis_index(axes)
    last = math.prod(SIZES[a] for a in axes) - 1
    return jnp.where(at > 0, 1.0, 0.0).astype(F32), jnp.where(at < last, 1.0, 0.0).astype(F32)


def tile(ref, at):
    return ref[pl.ds(pl.multiple_of(at * PLANES, PLANES), PLANES), :]


def set_tile(ref, at, value):
    ref[pl.ds(pl.multiple_of(at * PLANES, PLANES), PLANES), :] = value


def within_kernel(
    scales, src, from_core, receiver_in, strain, receiver, grads, slots, sparse, sems
):
    def fetch(b):
        return pltpu.make_async_copy(receiver_in.at[:, b], slots.at[b], sems.at[b])

    for b in range(BINS):
        fetch(b).start()
    lane = lane_ids((FIELDS, LANES))
    halo = spread_out(from_core[:DENSE, :], sparse, lax.axis_index("core") == 1)

    def at(x, y):
        if min(x, y) < 0 or max(x, y) > 3:
            return 0.0
        return src[pl.ds(x * 4 + y, FIELDS, stride=PLANES), :]

    def put(p, plane, value):
        grads[pl.ds(p * FIELDS * PLANES + plane, FIELDS, stride=PLANES), :] = value

    for x in range(4):
        for y in range(4):
            plane = x * 4 + y
            put(0, plane, 8.0 * (at(x + 1, y) - at(x - 1, y)) - (at(x + 2, y) - at(x - 2, y)))
            put(1, plane, 8.0 * (at(x, y + 1) - at(x, y - 1)) - (at(x, y + 2) - at(x, y - 2)))
            mid = at(x, y)
            later = jnp.where(lane < LANES - 1, pltpu.roll(mid, LANES - 1, 1), 0.0)
            sooner = jnp.where(lane > 0, pltpu.roll(mid, 1, 1), 0.0)
            later_two = jnp.where(lane < LANES - 2, pltpu.roll(mid, LANES - 2, 1), 0.0)
            sooner_two = jnp.where(lane > 1, pltpu.roll(mid, 2, 1), 0.0)
            value = 8.0 * (later - sooner) - (later_two - sooner_two)
            put(2, plane, value + ends_at(halo, plane, lane))

    def body(b, carry):
        def grad(p, q, k):
            return tile(scales, p) * tile(grads, p * FIELDS + b * 6 + q * 2 + k)

        for k in range(2):
            for j, value in enumerate(
                (
                    grad(0, 0, k),
                    grad(1, 1, k),
                    grad(2, 2, k),
                    grad(1, 2, k) + grad(2, 1, k),
                    grad(0, 2, k) + grad(2, 0, k),
                    grad(0, 1, k) + grad(1, 0, k),
                )
            ):
                set_tile(strain, b * 12 + j * 2 + k, value)
        fetch(b).wait()
        for r in range(TENSORS):
            receiver[r, b] = slots[b, r].astype(F32)
        return carry

    lax.fori_loop(0, BINS, body, 0)


def ends_at(halo, plane, lane):
    turned = pltpu.roll(halo, LANES - 8 * plane, 1) if plane else halo
    return jnp.where((lane < 2) | (lane >= LANES - 2), turned, 0.0)


def within(scales, src, from_core, receiver):
    return pl.pallas_call(
        within_kernel,
        out_shape=(
            jax.ShapeDtypeStruct((BINS * 12 * PLANES, LANES), F32),
            jax.ShapeDtypeStruct(receiver.shape, F32),
        ),
        in_specs=[vmem(), vmem(), vmem(), hbm()],
        out_specs=(vmem(), vmem()),
        scratch_shapes=[
            pltpu.VMEM((3 * FIELDS * PLANES, LANES), F32),
            pltpu.VMEM((BINS, TENSORS, 12, PLANES, LANES), BF16),
            pltpu.VMEM((FIELDS, LANES), F32),
            pltpu.SemaphoreType.DMA((BINS,)),
        ],
        compiler_params=pltpu.CompilerParams(vmem_limit_bytes=VMEM_LIMIT),
        cost_estimate=pl.CostEstimate(
            flops=4_000_000, bytes_accessed=14_000_000, transcendentals=0
        ),
        name="within",
    )(scales, src, from_core, in_hbm(receiver))


def gram_kernel(
    scales, within, receiver, xb, xa, from_side, from_pair, own, from_core, from_cross,
    keep, send, cells, stats, ends, sparse
):
    lane = lane_ids((FIELDS, LANES))
    crossing = jnp.where(lax.axis_index("xhi") != lax.axis_index("core"), 1.0, 0.0).astype(F32)
    lower = lax.axis_index("core") == 0
    halo = spread_out(from_cross[:DENSE, :] * crossing, sparse, lower)
    for plane in range(PLANES):
        ends[pl.ds(plane, FIELDS, stride=PLANES), :] = ends_at(halo, plane, lane)
    x_before, x_after = ends_of(GX)
    y_before, y_after = ends_of(GY)
    low_y = (lax.broadcasted_iota(jnp.int32, (8, LANES), 0) & 3) < 2
    inside = jnp.where(low_y, y_before, y_after)
    of_pair = low_y == (lax.axis_index("xlo") == 1)
    scale_x = (scales[0:8, :] * x_before, scales[8:16, :] * x_after)
    scale_y = (scales[16:24, :] * inside, scales[24:32, :] * inside)
    scale_z = tile(scales, 2)

    def body(b, carry):
        def from_x(field):
            return jnp.concatenate([scale_x[0] * xb[field], scale_x[1] * xa[field]], axis=0)

        def from_y(field):
            side, pair = from_side[field], from_pair[field]
            first = jnp.where(of_pair, pair, side)
            second = pltpu.roll(jnp.where(of_pair, side, pair), 2, 0)
            return jnp.concatenate([scale_y[0] * first, scale_y[1] * second], axis=0)

        def from_z(field):
            return scale_z * tile(ends, field)

        strain = []
        for k in range(2):
            inner = [tile(within, b * 12 + j * 2 + k) for j in range(6)]
            ux, uy, uz = [b * 6 + q * 2 + k for q in range(3)]
            strain.append(
                (
                    inner[0] + from_x(ux),
                    inner[1] + from_y(uy),
                    inner[2] + from_z(uz),
                    inner[3] + (from_y(uz) + from_z(uy)),
                    inner[4] + (from_x(uz) + from_z(ux)),
                    inner[5] + (from_x(uy) + from_y(ux)),
                )
            )
        real, imag = strain
        for r in range(TENSORS):
            re = im = None
            for j in range(6):
                rec_re, rec_im = receiver[r, b, 2 * j], receiver[r, b, 2 * j + 1]
                add_re = rec_re * real[j] - rec_im * imag[j]
                add_im = rec_re * imag[j] + rec_im * real[j]
                re, im = (re + add_re, im + add_im) if j else (add_re, add_im)
            set_tile(cells, r * 32 + b * 2, re)
            set_tile(cells, r * 32 + b * 2 + 1, im)
        return carry

    lax.fori_loop(0, BINS, body, 0)

    total = jnp.zeros((ROWS, ROWS), F32)
    for plane in range(0, PLANES, 4):
        both = jnp.concatenate(
            [cells[pl.ds(plane + i, ROWS, stride=PLANES), :] for i in range(4)], axis=1
        )
        high = both.astype(BF16)
        low = (both - high.astype(F32)).astype(BF16)
        left = jnp.concatenate([high, high], axis=1)
        right = jnp.concatenate([high * BF16(0.5), low], axis=1)
        total = total + lax.dot_general(
            left, right, (((1,), (1,)), ((), ())), preferred_element_type=F32
        )

    def block(i, j):
        return total[i * LANES : (i + 1) * LANES, j * LANES : (j + 1) * LANES]

    full = [block(i, j) + block(j, i).T for i, j in BLOCKS]
    upper = lax.axis_index("core") == 1
    for n in range(3):
        part = slice(n * LANES, (n + 1) * LANES)
        keep[part, :] = jnp.where(upper, full[n + 3], full[n])
        send[part, :] = jnp.where(upper, full[n], full[n + 3])

    stats[...] = merge_sums(
        merge_sums(sums_of(own[...]), sums_of(from_core[DENSE:, :])),
        merge_sums(
            sums_of(from_cross[DENSE : DENSE + 8, :]), sums_of(from_cross[DENSE + 8 :, :])
        ),
    )


def gram(scales, within, receiver, halos, sums):
    half = jax.ShapeDtypeStruct((3 * LANES, LANES), F32)
    return pl.pallas_call(
        gram_kernel,
        out_shape=(
            half,
            half,
            jax.ShapeDtypeStruct((ROWS * PLANES, LANES), F32),
            jax.ShapeDtypeStruct((8, ROWS), F32),
        ),
        in_specs=[vmem()] * 10,
        out_specs=(vmem(),) * 4,
        scratch_shapes=[
            pltpu.VMEM((FIELDS * PLANES, LANES), F32),
            pltpu.VMEM((FIELDS, LANES), F32),
        ],
        compiler_params=pltpu.CompilerParams(vmem_limit_bytes=VMEM_LIMIT),
        cost_estimate=pl.CostEstimate(
            flops=1_200_000_000, bytes_accessed=8_000_000, transcendentals=0
        ),
        name="gram",
    )(scales, within, receiver, *halos, *sums)


def chain_kernel(
    mine, other, stats, cells, observed_in, tensor_in, bins_in, window_in, update, direction, data,
    full, coef, observed, tensor_ref, bins_ref, window, sems
):
    copies = [
        pltpu.make_async_copy(here, there, sems.at[n])
        for n, (here, there) in enumerate(
            (
                (observed_in, observed),
                (tensor_in, tensor_ref),
                (bins_in, bins_ref),
                (window_in, window),
            )
        )
    ]
    for copy in copies:
        copy.start()
    upper = lax.axis_index("core") == 1
    for n, (i, j) in enumerate(BLOCKS):
        part = slice(n % 3 * LANES, (n % 3 + 1) * LANES)
        near, far = mine[part, :], other[part, :]
        block = jnp.where(upper, far, near) if n < 3 else jnp.where(upper, near, far)
        full[i * LANES : (i + 1) * LANES, j * LANES : (j + 1) * LANES] = block
        if i != j:
            full[j * LANES : (j + 1) * LANES, i * LANES : (i + 1) * LANES] = block.T
    eye = lax.broadcasted_iota(jnp.int32, (LANES, LANES), 0) == lane_ids((LANES, LANES))

    def column(row):
        return jnp.concatenate(
            [
                jnp.sum(
                    jnp.where(eye, row[:, j * LANES : (j + 1) * LANES], 0.0), axis=1, keepdims=True
                )
                for j in range(3)
            ],
            axis=0,
        )

    def product(row):
        return jnp.sum(full[...] * column(row), axis=0, keepdims=True)

    def total(row):
        return jnp.sum(row, axis=1, keepdims=True)

    def norm_of(square):
        return jnp.sqrt(square + EPSILON)

    sums, count, rest = stats[0:1, :], stats[1:2, :], stats[2:3, 0:1]
    mean = sums / jnp.maximum(count, 1.0)

    def data_norm(scale, row):
        inside = scale * mean + row
        return norm_of(scale * scale * rest + total(count * inside * inside))

    one = jnp.ones((1, 1), F32)
    row = jnp.zeros((1, ROWS), F32)
    beta = data_norm(one, row)
    beta_first = beta
    scale = one / beta
    raw = scale * sums
    image = product(raw)
    alpha = norm_of(total(raw * image))
    alpha_first = alpha
    model = raw / alpha
    search = model
    answer = jnp.zeros((1, ROWS), F32)
    phi_bar, rho_bar = beta, alpha
    for _ in range(ITERS):
        model_image = image / alpha
        scale, row = -alpha * scale, model_image - alpha * row
        back = scale * sums + count * row
        back_image = product(back)
        beta = data_norm(scale, row)
        inverse = one / beta
        scale, row = scale * inverse, row * inverse
        raw = back * inverse - beta * model
        image = back_image * inverse - beta * model_image
        alpha = norm_of(total(raw * image))
        model = raw / alpha
        rho = jnp.sqrt(rho_bar * rho_bar + beta * beta)
        cosine, sine = rho_bar / rho, beta / rho
        theta = sine * alpha
        rho_bar = -cosine * alpha
        phi = cosine * phi_bar
        phi_bar = sine * phi_bar
        answer = answer + phi / rho * search
        search = model - theta / rho * search
    cell_scale = math.sqrt(PLANES * LANES * math.prod(SIZES.values()))
    coef[0] = jnp.broadcast_to(
        column(answer * (alpha_first * cell_scale / beta_first)), (ROWS, LANES)
    )
    coef[1] = jnp.broadcast_to(column(model * cell_scale), (ROWS, LANES))

    def body(n, totals):
        one, two = tile(cells, 2 * n), tile(cells, 2 * n + 1)
        return (
            totals[0] + coef[0, pl.ds(2 * n, 1), :] * one,
            totals[1] + coef[1, pl.ds(2 * n, 1), :] * one,
            totals[2] + coef[0, pl.ds(2 * n + 1, 1), :] * two,
            totals[3] + coef[1, pl.ds(2 * n + 1, 1), :] * two,
        )

    start = (jnp.zeros((PLANES, LANES), F32),) * 4
    totals = lax.fori_loop(0, ROWS // 2, body, start, unroll=16)
    first, second = totals[0] + totals[2], totals[1] + totals[3]
    update[...] = first
    direction[...] = second

    for copy in copies:
        copy.wait()
    mask = window[...].astype(F32)
    size = math.sqrt(math.prod(observed.shape) * SIZES["xhi"] * SIZES["core"])
    near = pick(column(row * size), bins_ref[...], tensor_ref[...])
    for k in range(2):
        data[k] = (observed[k] * (scale * size) + near[k]) * mask


def chain(mine, other, stats, cells, observed, tensor, bins, window):
    field = jax.ShapeDtypeStruct((PLANES, LANES), F32)
    given = (observed, tensor, bins, window)
    return pl.pallas_call(
        chain_kernel,
        out_shape=(field, field, jax.ShapeDtypeStruct(observed.shape, F32)),
        in_specs=[vmem()] * 4 + [pl.BlockSpec(memory_space=pl.ANY)] * 4,
        out_specs=(vmem(),) * 3,
        scratch_shapes=[pltpu.VMEM((ROWS, ROWS), F32), pltpu.VMEM((2, ROWS, LANES), F32)]
        + [pltpu.VMEM(x.shape, x.dtype) for x in given]
        + [pltpu.SemaphoreType.DMA((4,))],
        compiler_params=pltpu.CompilerParams(vmem_limit_bytes=VMEM_LIMIT),
        name="chain",
    )(mine, other, stats, cells, *given)


def shift(value, axes, step):
    count = math.prod(SIZES[a] for a in axes)
    return lax.ppermute(value, axes, [(i, (i + step) % count) for i in range(count)])


def swap(value, axis):
    return lax.ppermute(value, axis, [(0, 1), (1, 0)])


def exchange(value, axes):
    return lax.all_to_all(value, axes, 0, 0, tiled=True)


def scatter_sum(value, axes):
    count = math.prod(SIZES[a] for a in axes)
    return jnp.sum(exchange(value.reshape(count, -1, LANES), axes), axis=0)


def whole_sum(value, axes):
    count = math.prod(SIZES[a] for a in axes)
    return jnp.sum(exchange(jnp.broadcast_to(value, (count,) + value.shape), axes), axis=0)


def gather(value, axes):
    count = math.prod(SIZES[a] for a in axes)
    return exchange(jnp.broadcast_to(value, (count,) + value.shape), axes).reshape(-1, LANES)


def per_device(
    source_field,
    receiver_tensor,
    metric_ids,
    metric_table,
    observed,
    receiver_index,
    bin_ids,
    window,
):
    src = source_field.reshape(FIELDS, PLANES, LANES)
    receiver = receiver_tensor.reshape(TENSORS, BINS, 12, PLANES, LANES)
    ids = metric_ids.reshape(PLANES, LANES)
    table = metric_table.T
    values = observed.transpose(0, 2, 1)
    tensor = receiver_index.reshape(1, -1)
    bins, marks = bin_ids.T, window.T
    src, to_side, to_pair, to_core, to_cross, stats, scales = pack(
        src, ids, table, values, tensor, bins, marks
    )
    count = math.prod(SIZES[a] for a in GY)
    ring = [(i, (i + 1 if i % 2 else i - 1) % count) for i in range(count)]
    from_side, from_pair = lax.ppermute(to_side, GY, ring), swap(to_pair, "xlo")
    from_core = swap(to_core, "core")
    x_lo, x_hi, to_cross = strike_faces(src, to_cross, from_core)
    xb, xa = shift(x_hi, GX, 1), shift(x_lo, GX, -1)
    from_cross = lax.ppermute(to_cross, GZ, [(i, 3 - i) for i in range(4)])

    strain, receiver = within(scales, src.reshape(FIELDS * PLANES, LANES), from_core, receiver)
    sums = (stats, from_core, from_cross)
    keep, send, cells, stats = gram(scales, strain, receiver, (xb, xa, from_side, from_pair), sums)
    packed = keep + swap(send, "core")
    packed = scatter_sum(packed, PLANE)
    packed = whole_sum(packed, ("z",))
    packed = gather(packed, PLANE)
    other = swap(packed, "core")
    update, direction, data = chain(packed, other, stats, cells, values, tensor, bins, marks)
    return (
        update.reshape(metric_ids.shape),
        direction.reshape(metric_ids.shape),
        data.transpose(0, 2, 1),
    )


def solution(mesh):
    fine = Mesh(mesh.devices.reshape([SIZES[a] for a in AXES]), AXES)
    return jax.shard_map(
        per_device,
        mesh=fine,
        in_specs=(
            P(None, None, None, GX, GY, GZ),
            P(None, None, None, None, GX, GY, GZ),
            P(GX, GY, GZ),
            P(),
            P(None, GZ, None),
            P(GZ),
            P(GZ, None),
            P(GZ, None),
        ),
        out_specs=(P(GX, GY, GZ), P(GX, GY, GZ), P(None, GZ, None)),
        check_vma=False,
    )
```
